256 devices in a mesh: lon: 16 (over x_hi, z), lat: 16 (over x_lo, y, core).
Axes of the slice: x: 4 (x_hi: 2, x_lo: 2; x = x_hi * 2 + x_lo), y: 4, z: 8, core: 2. Of those that a mesh axis runs over, the one named last changes fastest.
Arguments:
- pressure: float32 [4, 3840, 4096], P(None, 'lat', 'lon'), may hold values from -6 to 6
- wind_east: float32 [4, 3840, 4096], P(None, 'lat', 'lon'), may hold values from -6 to 6
- wind_north: float32 [4, 3840, 4096], P(None, 'lat', 'lon'), may hold values from -6 to 6
- forcing: float32 [4, 3840, 4096], P(None, 'lat', 'lon'), may hold values from -6 to 6
- coef_lon: float32 [4, 3840, 4096], P(None, 'lat', 'lon'), may hold values from 0.2 to 2
- coef_lat: float32 [4, 3840, 4096], P(None, 'lat', 'lon'), may hold values from 0.2 to 2
- coef_vert: float32 [4, 3840, 4096], P(None, 'lat', 'lon'), may hold values from 0.2 to 2
- diag_coef: float32 [4, 3840, 4096], P(None, 'lat', 'lon'), may hold values from 0.5 to 2
Outputs:
- new_pressure: float32 [4, 3840, 4096], P(None, 'lat', 'lon')
- residual: float32 [4, 3840, 4096], P(None, 'lat', 'lon')
The draws below stay inside these ranges and needn't reach their ends.
All inputs are finite; a program needn't handle non-finite values.
Results may differ from the reference program's by a relative error of at most 0.00002.
Values sent between devices are 32-bit elements; how exact they have to be, the bound alone decides.
No kernel may reach another device: no remote copies, remote signals or barrier semaphores. Data moves between devices by JAX's collectives and lax.ppermute only.
A program may use at most 128 MiB of HBM per device.

```python
import math
import jax
import jax.numpy as jnp

LEV = 4
NLAT = 3840
NLON = 4096


def block_scale(key, dims, split, least, largest):
    factor_of = 1.0
    for axis_at, blocks in split:
        steps = jax.random.uniform(jax.random.fold_in(jax.random.fold_in(key, 6), axis_at), (blocks,), jnp.float32, least / len(split), largest / len(split))
        factor_of = factor_of * jnp.repeat(jnp.exp(steps), dims[axis_at] // blocks).reshape((-1,) + (1,) * (len(dims) - 1 - axis_at))
    return factor_of


def bell_draw(stream_key, shape, scale, limit, shards=(), kind=jnp.bfloat16):
    entries = scale * jax.random.normal(stream_key, shape, jnp.float32)
    if shards:
        entries = entries * block_scale(stream_key, shape, shards, -0.22, 0.18)
    return jnp.clip(entries, -limit, limit).astype(kind)


def setup_inputs(seed: int = 0) -> dict:
    key_list = jax.random.split(jax.random.key(seed), 9)
    pressure = bell_draw(key_list[0], (LEV, NLAT, NLON), 1.0, 6.0, ((1, 16), (2, 16)), jnp.float32)
    wind_east = bell_draw(key_list[1], (LEV, NLAT, NLON), 1.0, 6.0, ((1, 16), (2, 16)), jnp.float32)
    wind_north = bell_draw(key_list[2], (LEV, NLAT, NLON), 1.0, 6.0, ((1, 16), (2, 16)), jnp.float32)
    forcing = bell_draw(key_list[3], (LEV, NLAT, NLON), 1.0, 6.0, ((1, 16), (2, 16)), jnp.float32)
    coef_lon = jnp.clip(jnp.exp(math.log(2.0) - 2.3025851 * jax.random.uniform(key_list[4], (LEV, NLAT, NLON), jnp.float32) ** block_scale(key_list[4], (LEV, NLAT, NLON), ((1, 16), (2, 16)), -0.2, 0.2)), 0.2, 2.0)
    coef_lat = jnp.clip(jnp.exp(math.log(2.0) - 2.3025851 * jax.random.uniform(key_list[5], (LEV, NLAT, NLON), jnp.float32) ** block_scale(key_list[5], (LEV, NLAT, NLON), ((1, 16), (2, 16)), -0.2, 0.2)), 0.2, 2.0)
    coef_vert = jnp.clip(jnp.exp(math.log(2.0) - 2.3025851 * jax.random.uniform(key_list[6], (LEV, NLAT, NLON), jnp.float32) ** block_scale(key_list[6], (LEV, NLAT, NLON), ((1, 16), (2, 16)), -0.2, 0.2)), 0.2, 2.0)
    diag_coef = jnp.clip(jnp.exp(math.log(2.0) - 1.3862944 * jax.random.uniform(key_list[7], (LEV, NLAT, NLON), jnp.float32) ** block_scale(key_list[7], (LEV, NLAT, NLON), ((1, 16), (2, 16)), -0.2, 0.2)), 0.5, 2.0)
    return {"pressure": pressure, "wind_east": wind_east, "wind_north": wind_north, "forcing": forcing, "coef_lon": coef_lon, "coef_lat": coef_lat, "coef_vert": coef_vert, "diag_coef": diag_coef}


def face_cosines(start_row, face_count, lat_total):
    positions = (start_row + jnp.arange(face_count, dtype=jnp.int32)).astype(jnp.float32)
    return jnp.cos(positions * (math.pi / lat_total) - math.pi / 2)


def divergence(east_ext, north_ext, face_cos):
    cos_low = face_cos[:-1][None, :, None]
    cos_high = face_cos[1:][None, :, None]
    middle = north_ext[:, 1:-1, 1:-1]
    zonal = 0.5 * (east_ext[:, 1:-1, 2:] - east_ext[:, 1:-1, :-2])
    merid = 0.5 * (cos_high * (middle + north_ext[:, 2:, 1:-1]) - cos_low * (north_ext[:, :-2, 1:-1] + middle))
    return zonal + merid


def helmholtz(field_ext, lon_ext, lat_ext, vert_coef, diag_coef, face_cos):
    centre = field_ext[:, 1:-1, 1:-1]
    lon_mid = lon_ext[:, 1:-1, 1:-1]
    west_weight = 0.5 * (lon_mid + lon_ext[:, 1:-1, :-2])
    east_weight = 0.5 * (lon_mid + lon_ext[:, 1:-1, 2:])
    metric = 0.5 * (1.0 + jnp.abs(face_cos))
    lat_mid = lat_ext[:, 1:-1, 1:-1]
    south_weight = metric[:-1][None, :, None] * (0.5 * (lat_mid + lat_ext[:, :-2, 1:-1]))
    north_weight = metric[1:][None, :, None] * (0.5 * (lat_mid + lat_ext[:, 2:, 1:-1]))
    zero_level = jnp.zeros_like(centre[:1])
    upper_weight = jnp.concatenate((vert_coef[1:], jnp.zeros_like(vert_coef[:1])), 0)
    below = jnp.concatenate((zero_level, centre[:-1]), 0)
    above = jnp.concatenate((centre[1:], zero_level), 0)
    diag_total = diag_coef + west_weight + east_weight + south_weight + north_weight + vert_coef + upper_weight
    coupled = (west_weight * field_ext[:, 1:-1, :-2] + east_weight * field_ext[:, 1:-1, 2:]
               + south_weight * field_ext[:, :-2, 1:-1] + north_weight * field_ext[:, 2:, 1:-1]
               + vert_coef * below + upper_weight * above)
    return diag_total * centre - coupled, diag_total


def extend_field(field, rim_width):
    south_rim = jnp.roll(jnp.flip(field[:, :rim_width], 1), NLON // 2, 2)
    north_rim = jnp.roll(jnp.flip(field[:, -rim_width:], 1), NLON // 2, 2)
    tall = jnp.concatenate((south_rim, field, north_rim), 1)
    return jnp.concatenate((tall[:, :, -rim_width:], tall, tall[:, :, :rim_width]), 2)


def reference(pressure, wind_east, wind_north, forcing, coef_lon, coef_lat, coef_vert, diag_coef):
    face_cos = face_cosines(0, NLAT + 1, NLAT)
    lon_ext = extend_field(coef_lon, 1)
    lat_ext = extend_field(coef_lat, 1)
    rhs_field = forcing - divergence(extend_field(wind_east, 1), extend_field(wind_north, 1), face_cos)
    applied, diag_total = helmholtz(extend_field(pressure, 1), lon_ext, lat_ext, coef_vert, diag_coef, face_cos)
    new_pressure = pressure + (rhs_field - applied) / diag_total
    applied_new, unused = helmholtz(extend_field(new_pressure, 1), lon_ext, lat_ext, coef_vert, diag_coef, face_cos)
    return new_pressure, rhs_field - applied_new
```

```python
import math

import jax
import jax.numpy as jnp
from jax import lax
from jax.experimental import pallas as pl
from jax.experimental.pallas import tpu as pltpu
from jax.sharding import PartitionSpec as P

F32 = jnp.float32
AXES = ("lon", "lat")
LANES = 128
ROW_FIELDS = 7
COL_FIELDS = 5


def swap_pairs(lon_count, lat_count):
    def flat(lon, lat):
        return (lon % lon_count) * lat_count + lat

    rows_near, rows_far, cols_near, cols_far = [], [], [], []
    for lon in range(lon_count):
        for lat in range(lat_count):
            me = flat(lon, lat)
            rows_near.append((me, flat(lon, lat ^ 1)))
            if lat in (0, lat_count - 1):
                rows_far.append((me, flat(lon + lon_count // 2, lat)))
            else:
                rows_far.append((me, flat(lon, lat + 1 if lat % 2 else lat - 1)))
            cols_near.append((me, flat(lon ^ 1, lat)))
            cols_far.append((me, flat(lon + 1 if lon % 2 else lon - 1, lat)))
    return rows_near, rows_far, cols_near, cols_far


def face_cos(first, shape, axis, lat_total):
    position = (first + lax.broadcasted_iota(jnp.int32, shape, axis)).astype(F32)
    return jnp.cos(position * (math.pi / lat_total) - math.pi / 2)


def metric(cosine):
    return 0.5 * (1.0 + jnp.abs(cosine))


def up_level(x):
    return jnp.concatenate((x[1:], jnp.zeros_like(x[:1])), 0)


def down_level(x):
    return jnp.concatenate((jnp.zeros_like(x[:1]), x[:-1]), 0)


def one_cos(row, lat_total):
    return face_cos(row, (1, 2 * LANES), 0, lat_total)


def rows_kernel(lat_total, rows, *refs):
    low, high, (near_ref, far_ref) = refs[:8], refs[8:16], refs[16:]
    lat = lax.axis_index("lat")
    width = near_ref.shape[-1]
    lane = lax.broadcasted_iota(jnp.int32, (4, width), 1)

    def message(fields, edge, inner, face, sign):
        p, we, wn, forcing, clon, clat, cvert, diag = [f[:, edge, :] for f in fields]
        p_in, wn_in, clat_in = [fields[i][:, inner, :] for i in (0, 2, 5)]
        cosine = one_cos(face, lat_total)
        east = lane < width - 1
        w_east = jnp.where(east, 0.5 * (clon + pltpu.roll(clon, width - 1, 1)), 0.0)
        h_east = jnp.where(
            east,
            w_east * (pltpu.roll(p, width - 1, 1) - p) - 0.5 * (we + pltpu.roll(we, width - 1, 1)),
            0.0,
        )
        w_in = metric(cosine) * (0.5 * (clat + clat_in))
        h_in = w_in * (p_in - p) - sign * (0.5 * cosine * (wn + wn_in))
        w_up = up_level(cvert)
        h_up = w_up * (up_level(p) - p)
        below = cvert * (p - down_level(p))
        total = diag + w_east + pltpu.roll(w_east, 1, 1) + w_in + cvert + w_up
        number = forcing - diag * p + h_east - pltpu.roll(h_east, 1, 1) + h_in + h_up - below
        return jnp.concatenate((p, wn, clat, total, number, clon, we), 0)

    start = lat * rows
    south = message(low, 0, 1, start + 1, 1.0)
    north = message(high, 7, 6, start + rows - 1, -1.0)
    even = lat % 2 == 0
    near_ref[...] = jnp.where(even, north, south)
    far_ref[...] = jnp.where(even, south, north)


def rows_call(lat_total, fields):
    lev, rows, width = fields[0].shape
    low = pl.BlockSpec((lev, 8, width), lambda i: (0, 0, 0))
    high = pl.BlockSpec((lev, 8, width), lambda i: (0, rows // 8 - 1, 0))
    shape = jax.ShapeDtypeStruct((ROW_FIELDS * lev, width), F32)
    out = pl.BlockSpec((ROW_FIELDS * lev, width), lambda i: (0, 0))
    return pl.pallas_call(
        lambda *refs: rows_kernel(lat_total, rows, *refs),
        grid=(1,),
        in_specs=[low] * 8 + [high] * 8,
        out_specs=[out, out],
        out_shape=[shape, shape],
        name="row_messages",
    )(*fields, *fields)


CHUNKS = 5


def partial_kernel(lat_total, rows, *refs):
    hbm, (total_ref, number_ref, cols_ref) = refs[:8], refs[8:11]
    bufs, pack, sems = refs[11:19], refs[19], refs[20]
    lat = lax.axis_index("lat")
    start = lat * rows
    per = rows // CHUNKS

    def copy(chunk, field, tile):
        return pltpu.make_async_copy(
            hbm[field].at[:, pl.ds(chunk * per, per), pl.ds(tile * LANES, LANES)],
            bufs[field].at[tile, :, pl.ds(chunk * per, per), :],
            sems.at[chunk, field, tile],
        )

    for chunk in range(CHUNKS):
        for field in range(8):
            for tile in range(2):
                copy(chunk, field, tile).start()

    def wait(chunk):
        for field in range(8):
            for tile in range(2):
                copy(chunk, field, tile).wait()

    shape = (8, LANES)
    lane = lax.broadcasted_iota(jnp.int32, shape, 1)
    sub = lax.broadcasted_iota(jnp.int32, shape, 0)
    zero = jnp.zeros(shape, F32)
    pack[pl.ds(rows, 256 - rows), :] = jnp.zeros((256 - rows, LANES), F32)

    def east(t):
        a, b = pltpu.roll(t[0], LANES - 1, 1), pltpu.roll(t[1], LANES - 1, 1)
        return jnp.where(lane == LANES - 1, b, a), b

    def west(t):
        a, b = pltpu.roll(t[0], 1, 1), pltpu.roll(t[1], 1, 1)
        return jnp.where(lane == 0, b, a), jnp.where(lane == 0, a, b)

    def south(x, carried):
        rolled = pltpu.roll(x, 1, 0)
        return jnp.where(sub == 0, carried, rolled), rolled

    def step(r, carry):
        row = pl.multiple_of(r * 8, 8)
        cosine = face_cos(start + row + 1, shape, 0, lat_total)
        half_metric = 0.5 * metric(cosine)
        half_cos = 0.5 * cosine
        last = (row + sub) == rows - 1
        acc = zero
        p_here = [[bufs[0][t, k, pl.ds(row, 8), :] for t in range(2)] for k in range(4)]
        h_below = None
        new_carry = []
        for k in range(4):
            here = lambda f: [bufs[f][t, k, pl.ds(row, 8), :] for t in range(2)]
            above = lambda f: [bufs[f][t, k, pl.ds(row + 1, 8), :] for t in range(2)]
            p, we, wn, forcing, clon, clat, cvert, diag = (
                p_here[k], here(1), here(2), here(3), here(4), here(5), here(6), here(7),
            )
            p_up, wn_up, clat_up = above(0), above(2), above(5)
            p_e, we_e, clon_e = east(p), east(we), east(clon)
            w_e, h_e = [], []
            for t in range(2):
                w = 0.5 * (clon[t] + clon_e[t])
                h = w * (p_e[t] - p[t]) - 0.5 * (we[t] + we_e[t])
                if t == 1:
                    w, h = jnp.where(lane < LANES - 1, w, 0.0), jnp.where(lane < LANES - 1, h, 0.0)
                w_e.append(w)
                h_e.append(h)
            w_w, h_w = west(w_e), west(h_e)
            if k < 3:
                cvert_up = [bufs[6][t, k + 1, pl.ds(row, 8), :] for t in range(2)]
                h_above = [cvert_up[t] * (p_here[k + 1][t] - p[t]) for t in range(2)]
            total, number = [], []
            for t in range(2):
                w_n = jnp.where(last, 0.0, half_metric * (clat[t] + clat_up[t]))
                h_n = w_n * (p_up[t] - p[t]) - half_cos * (wn[t] + wn_up[t])
                h_n = jnp.where(last, 0.0, h_n)
                slot = (k * 2 + t) * 2
                w_s, w_c = south(w_n, carry[slot])
                h_s, h_c = south(h_n, carry[slot + 1])
                new_carry += [w_c, h_c]
                tt = diag[t] + w_e[t] + w_w[t] + w_n + w_s + cvert[t]
                nn = forcing[t] - diag[t] * p[t] + (h_e[t] - h_w[t]) + (h_n - h_s)
                nn = nn - (cvert[t] * p[t] if k == 0 else h_below[t])
                if k < 3:
                    tt = tt + cvert_up[t]
                    nn = nn + h_above[t]
                total_ref[t, k, pl.ds(row, 8), :] = tt
                number_ref[t, k, pl.ds(row, 8), :] = nn
                total.append(tt)
                number.append(nn)
            for side in range(2):
                for i, f in enumerate((p, we, clon, total, number)):
                    j = (side * COL_FIELDS + i) * 4 + k
                    source = 0 if side == 0 else LANES - 1
                    acc = jnp.where(lane == j, pltpu.roll(f[side], (j - source) % LANES, 1), acc)
            if k < 3:
                h_below = h_above
        pack[pl.ds(row, 8), :] = acc
        return tuple(new_carry)

    carry = tuple([zero] * 16)
    wait(0)
    for chunk in range(CHUNKS):
        if chunk + 1 < CHUNKS:
            wait(chunk + 1)
        carry = lax.fori_loop(chunk * per // 8, (chunk + 1) * per // 8, step, carry)
    cols_ref[...] = pack[...].T[: 2 * COL_FIELDS * 4]


def partial_call(lat_total, fields):
    lev, rows, width = fields[0].shape
    tiles = width // LANES
    plane = jax.ShapeDtypeStruct((tiles, lev, rows, LANES), F32)
    cols = jax.ShapeDtypeStruct((2 * COL_FIELDS * lev, 256), F32)
    vmem = pl.BlockSpec(memory_space=pltpu.VMEM)
    return pl.pallas_call(
        lambda *refs: partial_kernel(lat_total, rows, *refs),
        in_specs=[pl.BlockSpec(memory_space=pl.ANY)] * 8,
        out_specs=[vmem, vmem, vmem],
        out_shape=[plane, plane, cols],
        scratch_shapes=[pltpu.VMEM((tiles, lev, rows + 8, LANES), F32)] * 8
        + [pltpu.VMEM((256, LANES), F32), pltpu.SemaphoreType.DMA((CHUNKS, 8, tiles))],
        compiler_params=pltpu.CompilerParams(vmem_limit_bytes=40 * 2**20),
        cost_estimate=pl.CostEstimate(flops=20_000_000, bytes_accessed=10_000_000, transcendentals=0),
        name="partial_sums",
    )(*fields)


def edge_rows(own, halo, cosine, low):
    w = metric(cosine) * (0.5 * (own[8:12] + halo[8:12]))
    g = 0.5 * cosine * (own[4:8] + halo[4:8])
    f = w * (own[0:4] - halo[0:4]) if low else w * (halo[0:4] - own[0:4])
    return w, f, g


def pick(even, near, far):
    return jnp.where(even, far, near), jnp.where(even, near, far)


def columns_kernel(lat_total, rows, cols, near, far, near_in, far_in, near_ref, far_ref):
    lat, lon = lax.axis_index("lat"), lax.axis_index("lon")
    even = lat % 2 == 0
    own_s, own_n = pick(even, near[...], far[...])
    halo_s, halo_n = pick(even, near_in[...], far_in[...])
    w_s, f_s, g_s = edge_rows(own_s, halo_s, one_cos(lat * rows, lat_total), True)
    w_n, f_n, g_n = edge_rows(own_n, halo_n, one_cos((lat + 1) * rows, lat_total), False)
    h_s, h_n = f_s - g_s, f_n - g_n
    width = w_s.shape[-1]
    lane = lax.broadcasted_iota(jnp.int32, (4, width), 1)

    def side(at):
        source = 0 if at == 0 else width - 1
        base = at * COL_FIELDS * 4
        p, we, clon, total, number = [cols[pl.ds(base + i * 4, 4), :] for i in range(COL_FIELDS)]

        def put(x, value, target):
            return jnp.where(lane == target, pltpu.roll(value, (target - source) % width, 1), x)

        no = jnp.zeros_like(p)
        total = total + put(put(no, w_s, 0), w_n, rows - 1)
        number = number + put(put(no, -h_s, 0), h_n, rows - 1)
        p = put(put(p, halo_s[0:4], rows), halo_n[0:4], rows + 1)
        clon = put(put(clon, halo_s[20:24], rows), halo_n[20:24], rows + 1)
        we = put(put(we, halo_s[24:28], rows), halo_n[24:28], rows + 1)
        return jnp.concatenate((p, we, clon, total, number), 0)

    west, east = side(0), side(1)
    lon_even = lon % 2 == 0
    near_ref[...] = jnp.where(lon_even, east, west)
    far_ref[...] = jnp.where(lon_even, west, east)


def columns_call(lat_total, rows, cols, near, far, near_in, far_in):
    shape = jax.ShapeDtypeStruct((cols.shape[0] // 2, cols.shape[1]), F32)
    vmem = pl.BlockSpec(memory_space=pltpu.VMEM)
    return pl.pallas_call(
        lambda *refs: columns_kernel(lat_total, rows, *refs),
        in_specs=[vmem] * 5,
        out_specs=[vmem, vmem],
        out_shape=[shape, shape],
        name="column_messages",
    )(cols, near, far, near_in, far_in)


def final_kernel(lat_total, rows, *refs):
    (p_hbm, clon_hbm, clat_hbm, cvert_hbm, total_ref, number_ref) = refs[:6]
    rn, rf, rn_in, rf_in, cn, cf, cn_in, cf_in = refs[6:14]
    new_ref, res_ref = refs[14:16]
    pb, lonb, latb, vertb, delta, colv, sems = refs[16:]
    bufs = (pb, lonb, latb, vertb)
    hbm = (p_hbm, clon_hbm, clat_hbm, cvert_hbm)
    lat, lon = lax.axis_index("lat"), lax.axis_index("lon")

    def copy(field, tile):
        return pltpu.make_async_copy(
            hbm[field].at[:, :, pl.ds(tile * LANES, LANES)],
            bufs[field].at[tile, :, pl.ds(0, rows), :],
            sems.at[field, tile],
        )

    for field in range(4):
        for tile in range(2):
            copy(field, tile).start()

    width = 2 * LANES
    wide = lax.broadcasted_iota(jnp.int32, (4, width), 1)
    even = lat % 2 == 0
    own_s, own_n = pick(even, rn[...], rf[...])
    halo_s, halo_n = pick(even, rn_in[...], rf_in[...])
    w_s, f_s, g_s = edge_rows(own_s, halo_s, one_cos(lat * rows, lat_total), True)
    w_n, f_n, g_n = edge_rows(own_n, halo_n, one_cos((lat + 1) * rows, lat_total), False)
    lon_even = lon % 2 == 0
    own_w, own_e = pick(lon_even, cn[...], cf[...])
    halo_w, halo_e = pick(lon_even, cn_in[...], cf_in[...])

    def edge_cols(own, halo, sign):
        w = 0.5 * (own[8:12] + halo[8:12])
        h = sign * w * (own[0:4] - halo[0:4]) - 0.5 * (own[4:8] + halo[4:8])
        d_own = (own[16:20] - sign * h) / (own[12:16] + w)
        d_halo = (halo[16:20] + sign * h) / (halo[12:16] + w)
        inside = wide < rows
        return w, h, jnp.where(inside, d_own, 0.0), jnp.where(inside, w * d_halo, 0.0)

    w_w, h_w, d_w, r_w = edge_cols(own_w, halo_w, 1.0)
    w_e, h_e, d_e, r_e = edge_cols(own_e, halo_e, -1.0)

    def put(x, value, source, target):
        return jnp.where(wide == target, pltpu.roll(value, (target - source) % width, 1), x)

    no = jnp.zeros((4, width), F32)

    def halo_delta(halo, w, f, g, source, low, pole):
        add_w = put(put(no, w_w, source, 0), w_e, source, width - 1)
        add_h = put(put(no, -h_w, source, 0), h_e, source, width - 1)
        turned = jnp.where(pole, -g, g)
        flux = f - turned if low else turned - f
        return (halo[16:20] + add_h + flux) / (halo[12:16] + add_w + w)

    lat_last = lax.axis_size("lat") - 1
    d_s = halo_delta(halo_s, w_s, f_s, g_s, rows, True, lat == 0)
    d_n = halo_delta(halo_n, w_n, f_n, g_n, rows + 1, False, lat == lat_last)
    r_s, r_n = w_s * d_s, w_n * d_n
    row_s = (own_s[16:20] - (f_s - g_s)) / (own_s[12:16] + w_s)
    row_n = (own_n[16:20] + (f_n - g_n)) / (own_n[12:16] + w_n)
    row_s = put(put(row_s, d_w, 0, 0), d_e, 0, width - 1)
    row_n = put(put(row_n, d_w, rows - 1, 0), d_e, rows - 1, width - 1)
    stack = jnp.concatenate((d_w, d_e, r_w, r_e, jnp.zeros((LANES - 16, width), F32)), 0)
    colv[...] = stack.T

    for field in range(4):
        for tile in range(2):
            copy(field, tile).wait()

    shape = (8, LANES)
    lane = lax.broadcasted_iota(jnp.int32, shape, 1)
    sub = lax.broadcasted_iota(jnp.int32, shape, 0)
    zero = jnp.zeros(shape, F32)
    edge = (0, LANES - 1)

    def first(r, carry):
        row = pl.multiple_of(r * 8, 8)
        packed = colv[pl.ds(row, 8), :]
        for k in range(4):
            for t in range(2):
                d = number_ref[t, k, pl.ds(row, 8), :] / total_ref[t, k, pl.ds(row, 8), :]
                column = pltpu.roll(packed, (edge[t] - (t * 4 + k)) % LANES, 1)
                d = jnp.where(lane == edge[t], column, d)
                delta[t, k, pl.ds(row + 8, 8), :] = d
                new_ref[k, pl.ds(row, 8), pl.ds(t * LANES, LANES)] = pb[t, k, pl.ds(row, 8), :] + d
        return carry

    lax.fori_loop(0, rows // 8, first, 0)
    for k in range(4):
        for t in range(2):
            cut = slice(t * LANES, (t + 1) * LANES)
            delta[t, k, 7:8, :] = jnp.zeros((1, LANES), F32)
            delta[t, k, rows + 8 : rows + 9, :] = jnp.zeros((1, LANES), F32)
            for at, value in ((0, row_s), (rows - 1, row_n)):
                delta[t, k, at + 8 : at + 9, :] = value[k : k + 1, cut]
                new_ref[k, at : at + 1, cut] = pb[t, k, at : at + 1, :] + value[k : k + 1, cut]

    start = lat * rows

    def second(r, carry):
        row = pl.multiple_of(r * 8, 8)
        packed = colv[pl.ds(row, 8), :]
        cosine = face_cos(start + row + 1, shape, 0, lat_total)
        half_metric = 0.5 * metric(cosine)
        last = (row + sub) == rows - 1
        new_carry = []
        d_here = [[delta[t, k, pl.ds(row + 8, 8), :] for t in range(2)] for k in range(4)]
        for k in range(4):
            d = d_here[k]
            clon = [lonb[t, k, pl.ds(row, 8), :] for t in range(2)]
            c0, c1 = [pltpu.roll(c, LANES - 1, 1) for c in clon]
            e0, e1 = [pltpu.roll(x, LANES - 1, 1) for x in d]
            w0 = 0.5 * (clon[0] + jnp.where(lane == LANES - 1, c1, c0))
            w1 = jnp.where(lane < LANES - 1, 0.5 * (clon[1] + c1), 0.0)
            east = w0 * jnp.where(lane == LANES - 1, e1, e0), w1 * e1
            v0, v1 = pltpu.roll(w0 * d[0], 1, 1), pltpu.roll(w1 * d[1], 1, 1)
            west = jnp.where(lane == 0, v1, v0), jnp.where(lane == 0, v0, v1)
            for t in range(2):
                clat = latb[t, k, pl.ds(row, 8), :]
                clat_up = latb[t, k, pl.ds(row + 1, 8), :]
                w_north = jnp.where(last, 0.0, half_metric * (clat + clat_up))
                sent = pltpu.roll(w_north * d[t], 1, 0)
                from_south = jnp.where(sub == 0, carry[k * 2 + t], sent)
                new_carry.append(sent)
                out = east[t] + west[t] + w_north * delta[t, k, pl.ds(row + 9, 8), :] + from_south
                if k > 0:
                    out = out + vertb[t, k, pl.ds(row, 8), :] * d_here[k - 1][t]
                if k < 3:
                    out = out + vertb[t, k + 1, pl.ds(row, 8), :] * d_here[k + 1][t]
                column = pltpu.roll(packed, (edge[t] - (8 + t * 4 + k)) % LANES, 1)
                out = out + jnp.where(lane == edge[t], column, 0.0)
                res_ref[k, pl.ds(row, 8), pl.ds(t * LANES, LANES)] = out
        return tuple(new_carry)

    lax.fori_loop(0, rows // 8, second, tuple([zero] * 8))
    for k in range(4):
        for t in range(2):
            cut = slice(t * LANES, (t + 1) * LANES)
            for at, value in ((0, r_s), (rows - 1, r_n)):
                res_ref[k, at : at + 1, cut] = res_ref[k, at : at + 1, cut] + value[k : k + 1, cut]


def final_call(lat_total, fields, planes, messages):
    lev, rows, width = fields[0].shape
    tiles = width // LANES
    vmem = pl.BlockSpec(memory_space=pltpu.VMEM)
    shape = jax.ShapeDtypeStruct(fields[0].shape, F32)
    buf = pltpu.VMEM((tiles, lev, rows + 8, LANES), F32)
    return pl.pallas_call(
        lambda *refs: final_kernel(lat_total, rows, *refs),
        in_specs=[pl.BlockSpec(memory_space=pl.ANY)] * 4 + [vmem] * 10,
        out_specs=[vmem, vmem],
        out_shape=[shape, shape],
        scratch_shapes=[buf] * 4
        + [
            pltpu.VMEM((tiles, lev, rows + 24, LANES), F32),
            pltpu.VMEM((256, LANES), F32),
            pltpu.SemaphoreType.DMA((4, tiles)),
        ],
        compiler_params=pltpu.CompilerParams(vmem_limit_bytes=40 * 2**20),
        name="corrected",
    )(*fields, *planes, *messages)


def per_device(pressure, wind_east, wind_north, forcing, coef_lon, coef_lat, coef_vert, diag_coef):
    fields = (pressure, wind_east, wind_north, forcing, coef_lon, coef_lat, coef_vert, diag_coef)
    rows = pressure.shape[1]
    lat_total = rows * lax.axis_size("lat")
    rows_near, rows_far, cols_near, cols_far = swap_pairs(
        lax.axis_size("lon"), lax.axis_size("lat")
    )
    near, far = rows_call(lat_total, fields)
    far_in = lax.ppermute(far, AXES, rows_far)
    near_in = lax.ppermute(near, AXES, rows_near)
    total, number, cols = partial_call(lat_total, fields)
    col_near, col_far = columns_call(lat_total, rows, cols, near, far, near_in, far_in)
    col_far_in = lax.ppermute(col_far, AXES, cols_far)
    col_near_in = lax.ppermute(col_near, AXES, cols_near)
    return final_call(
        lat_total,
        (pressure, coef_lon, coef_lat, coef_vert),
        (total, number),
        (near, far, near_in, far_in, col_near, col_far, col_near_in, col_far_in),
    )


def solution(mesh):
    spec = P(None, "lat", "lon")
    return jax.shard_map(
        per_device, mesh=mesh, in_specs=(spec,) * 8, out_specs=(spec, spec), check_vma=False
    )
```

```python
import math

import jax
import jax.numpy as jnp
from jax import lax
from jax.experimental import pallas as pl
from jax.experimental.pallas import tpu as pltpu
from jax.sharding import PartitionSpec as P

F32 = jnp.float32
AXES = ("lon", "lat")
LANES = 128
VMEM_LIMIT = 24 * 2**20
ROW_FIELDS = 7
COL_FIELDS = 5


def swap_pairs(lon_count, lat_count):
    def flat(lon, lat):
        return (lon % lon_count) * lat_count + lat

    rows_near, rows_far, cols_near, cols_far = [], [], [], []
    for lon in range(lon_count):
        for lat in range(lat_count):
            me = flat(lon, lat)
            rows_near.append((me, flat(lon, lat ^ 1)))
            if lat in (0, lat_count - 1):
                rows_far.append((me, flat(lon + lon_count // 2, lat)))
            else:
                rows_far.append((me, flat(lon, lat + 1 if lat % 2 else lat - 1)))
            cols_near.append((me, flat(lon ^ 1, lat)))
            cols_far.append((me, flat(lon + 1 if lon % 2 else lon - 1, lat)))
    return rows_near, rows_far, cols_near, cols_far


def face_cos(first, shape, axis, lat_total):
    position = (first + lax.broadcasted_iota(jnp.int32, shape, axis)).astype(F32)
    angle = position * (math.pi / lat_total) - math.pi / 2
    square = angle * angle
    cosine = jnp.full(shape, 1.0 / math.factorial(16), F32)
    for power in range(14, -1, -2):
        cosine = (-1.0) ** (power // 2) / math.factorial(power) + square * cosine
    return cosine


def metric(cosine):
    return 0.5 * (1.0 + jnp.abs(cosine))


def up_level(x):
    return jnp.concatenate((x[1:], jnp.zeros_like(x[:1])), 0)


def down_level(x):
    return jnp.concatenate((jnp.zeros_like(x[:1]), x[:-1]), 0)


def one_cos(row, lat_total):
    return face_cos(row, (1, 2 * LANES), 0, lat_total)


def rows_kernel(lat_total, rows, *refs):
    low, high, (near_ref, far_ref) = refs[:8], refs[8:16], refs[16:]
    lat = lax.axis_index("lat")
    width = near_ref.shape[-1]
    lane = lax.broadcasted_iota(jnp.int32, (4, width), 1)

    def message(fields, edge, inner, face, sign):
        p, we, wn, forcing, clon, clat, cvert, diag = [f[:, edge, :] for f in fields]
        p_in, wn_in, clat_in = [fields[i][:, inner, :] for i in (0, 2, 5)]
        cosine = one_cos(face, lat_total)
        east = lane < width - 1
        w_east = jnp.where(east, 0.5 * (clon + pltpu.roll(clon, width - 1, 1)), 0.0)
        h_east = jnp.where(
            east,
            w_east * (pltpu.roll(p, width - 1, 1) - p) - 0.5 * (we + pltpu.roll(we, width - 1, 1)),
            0.0,
        )
        w_in = metric(cosine) * (0.5 * (clat + clat_in))
        h_in = w_in * (p_in - p) - sign * (0.5 * cosine * (wn + wn_in))
        w_up = up_level(cvert)
        h_up = w_up * (up_level(p) - p)
        below = cvert * (p - down_level(p))
        total = diag + w_east + pltpu.roll(w_east, 1, 1) + w_in + cvert + w_up
        number = forcing - diag * p + h_east - pltpu.roll(h_east, 1, 1) + h_in + h_up - below
        return jnp.concatenate((p, wn, clat, total, number, clon, we), 0)

    start = lat * rows
    south = message(low, 0, 1, start + 1, 1.0)
    north = message(high, 7, 6, start + rows - 1, -1.0)
    even = lat % 2 == 0
    near_ref[...] = jnp.where(even, north, south)
    far_ref[...] = jnp.where(even, south, north)


def rows_call(lat_total, fields):
    lev, rows, width = fields[0].shape
    low = pl.BlockSpec((lev, 8, width), lambda i: (0, 0, 0))
    high = pl.BlockSpec((lev, 8, width), lambda i: (0, rows // 8 - 1, 0))
    shape = jax.ShapeDtypeStruct((ROW_FIELDS * lev, width), F32)
    pinned = [pltpu.with_memory_space_constraint(f, pltpu.HBM) for f in fields]
    out = pl.BlockSpec((ROW_FIELDS * lev, width), lambda i: (0, 0))
    return pl.pallas_call(
        lambda *refs: rows_kernel(lat_total, rows, *refs),
        grid=(1,),
        in_specs=[low] * 8 + [high] * 8,
        out_specs=[out, out],
        out_shape=[shape, shape],
        compiler_params=pltpu.CompilerParams(vmem_limit_bytes=4 * 2**20),
        name="row_messages",
    )(*pinned, *pinned)


CHUNKS = 5
PAD = 8
BLOCK = 48


def west_of(tiles, lane, edge):
    a, b = [pltpu.roll(x, 1, 1) for x in tiles]
    return jnp.where(lane == 0, edge, a), jnp.where(lane == 0, a, b)


def east_of(tiles, lane, edge):
    a, b = [pltpu.roll(x, LANES - 1, 1) for x in tiles]
    return jnp.where(lane == LANES - 1, b, a), jnp.where(lane == LANES - 1, edge, b)


def tile_copy(hbm, buf, sem, row, count, tile, pad=0):
    return pltpu.make_async_copy(
        hbm.at[:, pl.ds(row, count), pl.ds(tile * LANES, LANES)],
        buf.at[tile, :, pl.ds(pad + row, count), :],
        sem,
    )


def partial_kernel(lat_total, rows, *refs):
    hbm, (delta_hbm, cols_ref) = refs[:8], refs[8:10]
    bufs, delta, pack, cosines, sems, out_sems = refs[10:18], *refs[18:]
    start = lax.axis_index("lat") * rows
    per = rows // CHUNKS

    def copies(chunk):
        return [
            tile_copy(hbm[f], bufs[f], sems.at[chunk, f, t], chunk * per, per, t, PAD)
            for f in range(8)
            for t in range(2)
        ]

    def sends(chunk):
        cut = pl.ds(chunk * per, per)
        return [
            pltpu.make_async_copy(
                delta.at[t, :, cut, :], delta_hbm.at[t, :, cut, :], out_sems.at[chunk, t]
            )
            for t in range(2)
        ]

    def pads(inside, outside):
        for f, sign in ((0, 1.0), (2, -1.0), (5, -1.0)):
            for t in range(2):
                for k in range(4):
                    edge = bufs[f][t, k, inside : inside + 1, :]
                    bufs[f][t, k, outside : outside + 1, :] = sign * edge

    for chunk in range(CHUNKS):
        for c in copies(chunk):
            c.start()
    cosines[...] = face_cos(start, cosines.shape, 0, lat_total)
    pack[pl.ds(rows, 256 - rows), :] = jnp.zeros((256 - rows, LANES), F32)
    shape = (BLOCK, LANES)
    lane = lax.broadcasted_iota(jnp.int32, shape, 1)

    def step(r, carry):
        row = pl.multiple_of(r * BLOCK, BLOCK)
        c_s, c_n = cosines[pl.ds(row, BLOCK), :], cosines[pl.ds(row + 1, BLOCK), :]
        m_s, m_n = metric(c_s), metric(c_n)
        acc = [jnp.zeros(shape, F32) for _ in range(4)]
        for k in range(4):

            def get(f, shift=0, level=k):
                at = pl.ds(row + PAD + shift, BLOCK)
                return [bufs[f][t, level, at, :] for t in range(2)]

            p, we, clon = get(0), get(1), get(4)
            p_w, p_e = west_of(p, lane, p[0]), east_of(p, lane, p[1])
            we_w, we_e = west_of(we, lane, -we[0]), east_of(we, lane, -we[1])
            clon_w, clon_e = west_of(clon, lane, -clon[0]), east_of(clon, lane, -clon[1])
            wn, wn_s, wn_n = get(2), get(2, -1), get(2, 1)
            clat, clat_s, clat_n = get(5), get(5, -1), get(5, 1)
            p_s, p_n = get(0, -1), get(0, 1)
            forcing, below, diag = get(3), get(6), get(7)
            if k < 3:
                above, p_a = get(6, 0, k + 1), get(0, 0, k + 1)
            if k > 0:
                p_b = get(0, 0, k - 1)
            total, number = [], []
            for t in range(2):
                w_e, w_w = clon[t] + clon_e[t], clon[t] + clon_w[t]
                w_n, w_s = m_n * (clat[t] + clat_n[t]), m_s * (clat[t] + clat_s[t])
                flux = w_e * (p_e[t] - p[t]) + w_w * (p_w[t] - p[t]) - (we_e[t] - we_w[t])
                flux += w_n * (p_n[t] - p[t]) + w_s * (p_s[t] - p[t])
                flux += c_s * (wn[t] + wn_s[t]) - c_n * (wn[t] + wn_n[t])
                weight = (w_e + w_w) + (w_n + w_s)
                tt = diag[t] + below[t]
                nn = forcing[t] - diag[t] * p[t]
                nn += below[t] * (p_b[t] - p[t]) if k > 0 else -below[t] * p[t]
                if k < 3:
                    tt += above[t]
                    nn += above[t] * (p_a[t] - p[t])
                tt = tt + 0.5 * weight
                nn = nn + 0.5 * flux
                delta[t, k, pl.ds(row, BLOCK), :] = nn / tt
                total.append(tt)
                number.append(nn)
            for side in range(2):
                for i, f in enumerate((p, we, clon, total, number)):
                    j = (side * COL_FIELDS + i) * 4 + k
                    source = 0 if side == 0 else LANES - 1
                    moved = pltpu.roll(f[side], (j - source) % LANES, 1)
                    acc[k] = jnp.where(lane == j, moved, acc[k])
        pack[pl.ds(row, BLOCK), :] = (acc[0] + acc[1]) + (acc[2] + acc[3])
        return carry

    for c in copies(0):
        c.wait()
    pads(PAD, PAD - 1)
    for chunk in range(CHUNKS):
        if chunk + 1 < CHUNKS:
            for c in copies(chunk + 1):
                c.wait()
        if chunk == CHUNKS - 1:
            pads(PAD + rows - 1, PAD + rows)
        lax.fori_loop(chunk * per // BLOCK, (chunk + 1) * per // BLOCK, step, 0)
        for c in sends(chunk):
            c.start()
    cols_ref[...] = pack[...].T[: 2 * COL_FIELDS * 4]
    for chunk in range(CHUNKS):
        for c in sends(chunk):
            c.wait()


def partial_call(lat_total, fields):
    lev, rows, width = fields[0].shape
    tiles = width // LANES
    plane = jax.ShapeDtypeStruct((tiles, lev, rows, LANES), F32)
    cols = jax.ShapeDtypeStruct((2 * COL_FIELDS * lev, 256), F32)
    hbm, vmem = pl.BlockSpec(memory_space=pl.ANY), pl.BlockSpec(memory_space=pltpu.VMEM)
    return pl.pallas_call(
        lambda *refs: partial_kernel(lat_total, rows, *refs),
        in_specs=[hbm] * 8,
        out_specs=[hbm, vmem],
        out_shape=[plane, cols],
        scratch_shapes=[pltpu.VMEM((tiles, lev, rows + 2 * PAD, LANES), F32)] * 8
        + [
            pltpu.VMEM((tiles, lev, rows, LANES), F32),
            pltpu.VMEM((256, LANES), F32),
            pltpu.VMEM((rows + 8, LANES), F32),
            pltpu.SemaphoreType.DMA((CHUNKS, 8, tiles)),
            pltpu.SemaphoreType.DMA((CHUNKS, tiles)),
        ],
        compiler_params=pltpu.CompilerParams(vmem_limit_bytes=VMEM_LIMIT),
        cost_estimate=pl.CostEstimate(flops=20_000_000, bytes_accessed=10_000_000, transcendentals=0),
        name="partial_sums",
    )(*fields)


def edge_rows(own, halo, cosine, low):
    w = metric(cosine) * (0.5 * (own[8:12] + halo[8:12]))
    g = 0.5 * cosine * (own[4:8] + halo[4:8])
    f = w * (own[0:4] - halo[0:4]) if low else w * (halo[0:4] - own[0:4])
    return w, f, g


def pick(even, near, far):
    return jnp.where(even, far, near), jnp.where(even, near, far)


def columns_kernel(lat_total, rows, cols, near, far, near_in, far_in, near_ref, far_ref):
    lat, lon = lax.axis_index("lat"), lax.axis_index("lon")
    even = lat % 2 == 0
    own_s, own_n = pick(even, near[...], far[...])
    halo_s, halo_n = pick(even, near_in[...], far_in[...])
    w_s, f_s, g_s = edge_rows(own_s, halo_s, one_cos(lat * rows, lat_total), True)
    w_n, f_n, g_n = edge_rows(own_n, halo_n, one_cos((lat + 1) * rows, lat_total), False)
    h_s, h_n = f_s - g_s, f_n - g_n
    width = w_s.shape[-1]
    lane = lax.broadcasted_iota(jnp.int32, (4, width), 1)

    def side(at):
        source = 0 if at == 0 else width - 1
        base = at * COL_FIELDS * 4
        p, we, clon, total, number = [cols[pl.ds(base + i * 4, 4), :] for i in range(COL_FIELDS)]

        def put(x, value, target):
            return jnp.where(lane == target, pltpu.roll(value, (target - source) % width, 1), x)

        no = jnp.zeros_like(p)
        total = total + put(put(no, w_s, 0), w_n, rows - 1)
        number = number + put(put(no, -h_s, 0), h_n, rows - 1)
        p = put(put(p, halo_s[0:4], rows), halo_n[0:4], rows + 1)
        clon = put(put(clon, halo_s[20:24], rows), halo_n[20:24], rows + 1)
        we = put(put(we, halo_s[24:28], rows), halo_n[24:28], rows + 1)
        return jnp.concatenate((p, we, clon, total, number), 0)

    west, east = side(0), side(1)
    lon_even = lon % 2 == 0
    near_ref[...] = jnp.where(lon_even, east, west)
    far_ref[...] = jnp.where(lon_even, west, east)


def columns_call(lat_total, rows, cols, near, far, near_in, far_in):
    shape = jax.ShapeDtypeStruct((cols.shape[0] // 2, cols.shape[1]), F32)
    vmem = pl.BlockSpec(memory_space=pltpu.VMEM)
    return pl.pallas_call(
        lambda *refs: columns_kernel(lat_total, rows, *refs),
        in_specs=[vmem] * 5,
        out_specs=[vmem, vmem],
        out_shape=[shape, shape],
        compiler_params=pltpu.CompilerParams(vmem_limit_bytes=4 * 2**20),
        name="column_messages",
    )(cols, near, far, near_in, far_in)


def final_kernel(lat_total, rows, *refs):
    hbm, (rn, rf, rn_in, rf_in, cn, cf, cn_in, cf_in) = refs[:5], refs[5:13]
    new_hbm, res_hbm = refs[13:15]
    bufs, new_buf, res_buf, colv, cosines, sems, out_sems = refs[15:20], *refs[20:]
    pb, lonb, latb, vertb, delta = bufs
    lat, lon = lax.axis_index("lat"), lax.axis_index("lon")
    per = rows // CHUNKS

    def load(field, tile):
        if field == 4:
            return pltpu.make_async_copy(
                hbm[field].at[tile], delta.at[tile, :, pl.ds(PAD, rows), :], sems.at[field, tile]
            )
        return tile_copy(hbm[field], bufs[field], sems.at[field, tile], 0, rows, tile, PAD)

    def send(chunk, which, tile):
        buf, out = ((new_buf, new_hbm), (res_buf, res_hbm))[which]
        return pltpu.make_async_copy(
            buf.at[tile, :, pl.ds(chunk * per, per), :],
            out.at[:, pl.ds(chunk * per, per), pl.ds(tile * LANES, LANES)],
            out_sems.at[chunk, which, tile],
        )

    order = (4, 0, 1, 2, 3)
    for field in order:
        for tile in range(2):
            load(field, tile).start()

    width = 2 * LANES
    wide = lax.broadcasted_iota(jnp.int32, (4, width), 1)
    even = lat % 2 == 0
    cosines[...] = face_cos(lat * rows, cosines.shape, 0, lat_total)

    def two(x):
        return jnp.concatenate((x, x), 1)

    own_s, own_n = pick(even, rn[...], rf[...])
    halo_s, halo_n = pick(even, rn_in[...], rf_in[...])
    w_s, f_s, g_s = edge_rows(own_s, halo_s, two(cosines[0:1, :]), True)
    w_n, f_n, g_n = edge_rows(own_n, halo_n, two(cosines[rows : rows + 1, :]), False)
    lon_even = lon % 2 == 0
    own_w, own_e = pick(lon_even, cn[...], cf[...])
    halo_w, halo_e = pick(lon_even, cn_in[...], cf_in[...])

    def edge_cols(own, halo, sign):
        w = 0.5 * (own[8:12] + halo[8:12])
        h = sign * w * (own[0:4] - halo[0:4]) - 0.5 * (own[4:8] + halo[4:8])
        d_own = (own[16:20] - sign * h) / (own[12:16] + w)
        d_halo = (halo[16:20] + sign * h) / (halo[12:16] + w)
        inside = wide < rows
        return w, h, jnp.where(inside, d_own, 0.0), jnp.where(inside, w * d_halo, 0.0)

    w_w, h_w, d_w, r_w = edge_cols(own_w, halo_w, 1.0)
    w_e, h_e, d_e, r_e = edge_cols(own_e, halo_e, -1.0)

    def put(x, value, source, target):
        return jnp.where(wide == target, pltpu.roll(value, (target - source) % width, 1), x)

    no = jnp.zeros((4, width), F32)

    def halo_delta(halo, w, f, g, source, low, pole):
        add_w = put(put(no, w_w, source, 0), w_e, source, width - 1)
        add_h = put(put(no, -h_w, source, 0), h_e, source, width - 1)
        turned = jnp.where(pole, -g, g)
        flux = f - turned if low else turned - f
        return (halo[16:20] + add_h + flux) / (halo[12:16] + add_w + w)

    lat_last = lax.axis_size("lat") - 1
    d_s = halo_delta(halo_s, w_s, f_s, g_s, rows, True, lat == 0)
    d_n = halo_delta(halo_n, w_n, f_n, g_n, rows + 1, False, lat == lat_last)
    row_s = (own_s[16:20] - (f_s - g_s)) / (own_s[12:16] + w_s)
    row_n = (own_n[16:20] + (f_n - g_n)) / (own_n[12:16] + w_n)
    stack = jnp.concatenate((d_w, d_e, r_w, r_e, jnp.zeros((LANES - 16, width), F32)), 0)
    colv[...] = stack.T

    def put_rows(buf, at, value):
        for t in range(2):
            for k in range(4):
                buf[t, k, at : at + 1, :] = value[k : k + 1, t * LANES : (t + 1) * LANES]

    for tile in range(2):
        load(4, tile).wait()
    for at, value in ((PAD - 1, d_s), (PAD, row_s), (PAD + rows - 1, row_n), (PAD + rows, d_n)):
        put_rows(delta, at, value)

    shape = (BLOCK, LANES)
    lane = lax.broadcasted_iota(jnp.int32, shape, 1)
    edge = (0, LANES - 1)

    def fix(r, carry):
        row = pl.multiple_of(r * BLOCK, BLOCK)
        packed = colv[pl.ds(row, BLOCK), :]
        for k in range(4):
            for t in range(2):
                column = pltpu.roll(packed, (edge[t] - (t * 4 + k)) % LANES, 1)
                at = pl.ds(row + PAD, BLOCK)
                delta[t, k, at, :] = jnp.where(lane == edge[t], column, delta[t, k, at, :])
        return carry

    lax.fori_loop(0, rows // BLOCK, fix, 0)
    for field in order[1:]:
        for tile in range(2):
            load(field, tile).wait()
    put_rows(latb, PAD - 1, halo_s[8:12])
    put_rows(latb, PAD + rows, halo_n[8:12])

    def step(r, carry):
        row = pl.multiple_of(r * BLOCK, BLOCK)
        packed = colv[pl.ds(row, BLOCK), :]
        m_s, m_n = metric(cosines[pl.ds(row, BLOCK), :]), metric(cosines[pl.ds(row + 1, BLOCK), :])
        for k in range(4):

            def get(f, shift=0, level=k):
                at = pl.ds(row + PAD + shift, BLOCK)
                return [bufs[f][t, level, at, :] for t in range(2)]

            d, d_s, d_n = get(4), get(4, -1), get(4, 1)
            clat, clat_s, clat_n = get(2), get(2, -1), get(2, 1)
            clon, p = get(1), get(0)
            d_w, d_e = west_of(d, lane, d[0]), east_of(d, lane, d[1])
            clon_w, clon_e = west_of(clon, lane, clon[0]), east_of(clon, lane, clon[1])
            for t in range(2):
                column = pltpu.roll(packed, (edge[t] - (8 + t * 4 + k)) % LANES, 1)
                x_w = (clon[t] + clon_w[t]) * d_w[t]
                x_e = (clon[t] + clon_e[t]) * d_e[t]
                if t == 0:
                    x_w = jnp.where(lane == 0, 2.0 * column, x_w)
                else:
                    x_e = jnp.where(lane == LANES - 1, 2.0 * column, x_e)
                y = m_n * (clat[t] + clat_n[t]) * d_n[t] + m_s * (clat[t] + clat_s[t]) * d_s[t]
                out = 0.5 * ((x_w + x_e) + y)
                if k > 0:
                    out += get(3)[t] * get(4, 0, k - 1)[t]
                if k < 3:
                    out += get(3, 0, k + 1)[t] * get(4, 0, k + 1)[t]
                res_buf[t, k, pl.ds(row, BLOCK), :] = out
                new_buf[t, k, pl.ds(row, BLOCK), :] = p[t] + d[t]
        return carry

    for chunk in range(CHUNKS):
        lax.fori_loop(chunk * per // BLOCK, (chunk + 1) * per // BLOCK, step, 0)
        for which in range(2):
            for tile in range(2):
                send(chunk, which, tile).start()
    for chunk in range(CHUNKS):
        for which in range(2):
            for tile in range(2):
                send(chunk, which, tile).wait()


def final_call(lat_total, fields, planes, messages):
    lev, rows, width = fields[0].shape
    tiles = width // LANES
    hbm, vmem = pl.BlockSpec(memory_space=pl.ANY), pl.BlockSpec(memory_space=pltpu.VMEM)
    shape = jax.ShapeDtypeStruct(fields[0].shape, F32)
    return pl.pallas_call(
        lambda *refs: final_kernel(lat_total, rows, *refs),
        in_specs=[hbm] * 5 + [vmem] * 8,
        out_specs=[hbm, hbm],
        out_shape=[shape, shape],
        scratch_shapes=[pltpu.VMEM((tiles, lev, rows + 2 * PAD, LANES), F32)] * 5
        + [pltpu.VMEM((tiles, lev, rows, LANES), F32)] * 2
        + [
            pltpu.VMEM((256, LANES), F32),
            pltpu.VMEM((rows + 8, LANES), F32),
            pltpu.SemaphoreType.DMA((5, tiles)),
            pltpu.SemaphoreType.DMA((CHUNKS, 2, tiles)),
        ],
        compiler_params=pltpu.CompilerParams(vmem_limit_bytes=VMEM_LIMIT),
        name="corrected",
    )(*fields, *planes, *messages)


def per_device(pressure, wind_east, wind_north, forcing, coef_lon, coef_lat, coef_vert, diag_coef):
    fields = (pressure, wind_east, wind_north, forcing, coef_lon, coef_lat, coef_vert, diag_coef)
    rows = pressure.shape[1]
    lat_total = rows * lax.axis_size("lat")
    rows_near, rows_far, cols_near, cols_far = swap_pairs(
        lax.axis_size("lon"), lax.axis_size("lat")
    )
    near, far = rows_call(lat_total, fields)
    far_in = lax.ppermute(far, AXES, rows_far)
    near_in = lax.ppermute(near, AXES, rows_near)
    delta, cols = partial_call(lat_total, fields)
    col_near, col_far = columns_call(lat_total, rows, cols, near, far, near_in, far_in)
    col_far_in = lax.ppermute(col_far, AXES, cols_far)
    col_near_in = lax.ppermute(col_near, AXES, cols_near)
    return final_call(
        lat_total,
        (pressure, coef_lon, coef_lat, coef_vert),
        (delta,),
        (near, far, near_in, far_in, col_near, col_far, col_near_in, col_far_in),
    )


def solution(mesh):
    spec = P(None, "lat", "lon")
    return jax.shard_map(
        per_device, mesh=mesh, in_specs=(spec,) * 8, out_specs=(spec, spec), check_vma=False
    )
```

```python
import math

import jax
import jax.numpy as jnp
from jax import lax
from jax.experimental import pallas as pl
from jax.experimental.pallas import tpu as pltpu
from jax.sharding import PartitionSpec as P

F32 = jnp.float32
AXES = ("lon", "lat")
LANES = 128
ROW_FIELDS = 7
COL_FIELDS = 5


def swap_pairs(lon_count, lat_count):
    def flat(lon, lat):
        return (lon % lon_count) * lat_count + lat

    rows_near, rows_far, cols_near, cols_far = [], [], [], []
    for lon in range(lon_count):
        for lat in range(lat_count):
            me = flat(lon, lat)
            rows_near.append((me, flat(lon, lat ^ 1)))
            if lat in (0, lat_count - 1):
                rows_far.append((me, flat(lon + lon_count // 2, lat)))
            else:
                rows_far.append((me, flat(lon, lat + 1 if lat % 2 else lat - 1)))
            cols_near.append((me, flat(lon ^ 1, lat)))
            cols_far.append((me, flat(lon + 1 if lon % 2 else lon - 1, lat)))
    return rows_near, rows_far, cols_near, cols_far


def face_cos(first, shape, axis, lat_total):
    position = (first + lax.broadcasted_iota(jnp.int32, shape, axis)).astype(F32)
    angle = position * (math.pi / lat_total) - math.pi / 2
    square = angle * angle
    cosine = jnp.full(shape, 1.0 / math.factorial(16), F32)
    for power in range(14, -1, -2):
        cosine = (-1.0) ** (power // 2) / math.factorial(power) + square * cosine
    return cosine


def metric(cosine):
    return 0.5 * (1.0 + jnp.abs(cosine))


def up_level(x):
    return jnp.concatenate((x[1:], jnp.zeros_like(x[:1])), 0)


def down_level(x):
    return jnp.concatenate((jnp.zeros_like(x[:1]), x[:-1]), 0)


def one_cos(row, lat_total):
    return face_cos(row, (1, 2 * LANES), 0, lat_total)


def rows_kernel(lat_total, rows, *refs):
    low, high, (near_ref, far_ref) = refs[:8], refs[8:16], refs[16:]
    lat = lax.axis_index("lat")
    width = near_ref.shape[-1]
    lane = lax.broadcasted_iota(jnp.int32, (4, width), 1)

    def message(fields, edge, inner, face, sign):
        p, we, wn, forcing, clon, clat, cvert, diag = [f[:, edge, :] for f in fields]
        p_in, wn_in, clat_in = [fields[i][:, inner, :] for i in (0, 2, 5)]
        cosine = one_cos(face, lat_total)
        east = lane < width - 1
        w_east = jnp.where(east, 0.5 * (clon + pltpu.roll(clon, width - 1, 1)), 0.0)
        h_east = jnp.where(
            east,
            w_east * (pltpu.roll(p, width - 1, 1) - p) - 0.5 * (we + pltpu.roll(we, width - 1, 1)),
            0.0,
        )
        w_in = metric(cosine) * (0.5 * (clat + clat_in))
        h_in = w_in * (p_in - p) - sign * (0.5 * cosine * (wn + wn_in))
        w_up = up_level(cvert)
        h_up = w_up * (up_level(p) - p)
        below = cvert * (p - down_level(p))
        total = diag + w_east + pltpu.roll(w_east, 1, 1) + w_in + cvert + w_up
        number = forcing - diag * p + h_east - pltpu.roll(h_east, 1, 1) + h_in + h_up - below
        return jnp.concatenate((p, wn, clat, total, number, clon, we), 0)

    start = lat * rows
    south = message(low, 0, 1, start + 1, 1.0)
    north = message(high, 7, 6, start + rows - 1, -1.0)
    even = lat % 2 == 0
    near_ref[...] = jnp.where(even, north, south)
    far_ref[...] = jnp.where(even, south, north)


def rows_call(lat_total, fields):
    lev, rows, width = fields[0].shape
    low = pl.BlockSpec((lev, 8, width), lambda i: (0, 0, 0))
    high = pl.BlockSpec((lev, 8, width), lambda i: (0, rows // 8 - 1, 0))
    shape = jax.ShapeDtypeStruct((ROW_FIELDS * lev, width), F32)
    pinned = [pltpu.with_memory_space_constraint(f, pltpu.HBM) for f in fields]
    out = pl.BlockSpec((ROW_FIELDS * lev, width), lambda i: (0, 0))
    return pl.pallas_call(
        lambda *refs: rows_kernel(lat_total, rows, *refs),
        grid=(1,),
        in_specs=[low] * 8 + [high] * 8,
        out_specs=[out, out],
        out_shape=[shape, shape],
        compiler_params=pltpu.CompilerParams(vmem_limit_bytes=SMALL_VMEM),
        name="row_messages",
    )(*pinned, *pinned)


CHUNKS = 5
PAD = 8
BLOCK = 48
SMALL_VMEM = 4 * 2**20
VMEM_LIMIT = 24 * 2**20


def window_mask(lane, index):
    return lane // 4 == index


def window_row(index, offset):
    return 4 * index + offset


def merged(ref, level, row, count, lane):
    at = pl.ds(row, count)
    return jnp.where(lane < LANES // 2, ref[level, at, 0:LANES], ref[level, at, LANES : 2 * LANES])


def window_move(x, index):
    return pltpu.roll(x, (4 * index + 2) % LANES, 1)


def edge_kernel(lat_total, rows, *refs):
    p_ref, we_ref, wn_ref, f_ref, clon_ref, clat_ref, cv_ref, diag_ref = refs[:8]
    cols_ref, pm, wnm, clatm, pack, packed, cosines = refs[8:]
    start = lax.axis_index("lat") * rows
    cosines[...] = face_cos(start, cosines.shape, 0, lat_total)
    shape = (BLOCK, LANES)
    lane = lax.broadcasted_iota(jnp.int32, shape, 1)

    def gather(r, carry):
        row = pl.multiple_of(r * BLOCK, BLOCK)
        for ref, buf in ((p_ref, pm), (wn_ref, wnm), (clat_ref, clatm)):
            for k in range(4):
                buf[k, pl.ds(row + PAD, BLOCK), :] = merged(ref, k, row, BLOCK, lane)
        return carry

    lax.fori_loop(0, rows // BLOCK, gather, 0)
    for buf, sign in ((pm, 1.0), (wnm, -1.0), (clatm, -1.0)):
        for k in range(4):
            for inside, outside in ((PAD, PAD - 1), (PAD + rows - 1, PAD + rows)):
                buf[k, outside : outside + 1, :] = sign * buf[k, inside : inside + 1, :]
    pack[pl.ds(rows, 256 - rows), :] = jnp.zeros((256 - rows, LANES), F32)

    def step(r, carry):
        row = pl.multiple_of(r * BLOCK, BLOCK)
        c_s, c_n = cosines[pl.ds(row, BLOCK), :], cosines[pl.ds(row + 1, BLOCK), :]
        m_s, m_n = metric(c_s), metric(c_n)
        acc = [jnp.zeros(shape, F32) for _ in range(4)]
        for k in range(4):

            def get(buf, shift=0, level=k):
                return buf[level, pl.ds(row + PAD + shift, BLOCK), :]

            def raw(ref, level=k):
                return merged(ref, level, row, BLOCK, lane)

            p, clat, wn = get(pm), get(clatm), get(wnm)
            below, diag = raw(cv_ref), raw(diag_ref)
            w_n, w_s = m_n * (clat + get(clatm, 1)), m_s * (clat + get(clatm, -1))
            flux = w_n * (get(pm, 1) - p) + w_s * (get(pm, -1) - p)
            flux += c_s * (wn + get(wnm, -1)) - c_n * (wn + get(wnm, 1))
            total = diag + below
            number = raw(f_ref) - diag * p
            number += below * (get(pm, 0, k - 1) - p) if k > 0 else -below * p
            if k < 3:
                above = raw(cv_ref, k + 1)
                total += above
                number += above * (get(pm, 0, k + 1) - p)
            total += 0.5 * (w_n + w_s)
            number += 0.5 * flux
            for i, x in enumerate((p, raw(we_ref), raw(clon_ref), total, number)):
                index = i * 4 + k
                acc[k] = jnp.where(window_mask(lane, index), window_move(x, index), acc[k])
        pack[pl.ds(row, BLOCK), :] = (acc[0] + acc[1]) + (acc[2] + acc[3])
        return carry

    lax.fori_loop(0, rows // BLOCK, step, 0)
    packed[...] = pack[...].T

    def column(field, offset):
        return jnp.concatenate(
            [packed[pl.ds(window_row(field * 4 + k, offset), 1), :] for k in range(4)], 0
        )

    for side, (edge, inner, sign) in enumerate(((2, 3, 1.0), (1, 0, -1.0))):
        p, we, clon, total, number = [column(i, edge) for i in range(COL_FIELDS)]
        p_in, we_in, clon_in = [column(i, inner) for i in range(3)]
        w = 0.5 * (clon + clon_in)
        number = number + w * (p_in - p) - sign * (0.5 * (we + we_in))
        for i, x in enumerate((p, we, clon, total + w, number)):
            cols_ref[pl.ds((side * COL_FIELDS + i) * 4, 4), :] = x


def edge_call(lat_total, fields):
    lev, rows, width = fields[0].shape
    cols = jax.ShapeDtypeStruct((2 * COL_FIELDS * lev, 256), F32)
    vmem = pl.BlockSpec(memory_space=pltpu.VMEM)
    return pl.pallas_call(
        lambda *refs: edge_kernel(lat_total, rows, *refs),
        in_specs=[vmem] * 8,
        out_specs=vmem,
        out_shape=cols,
        scratch_shapes=[pltpu.VMEM((lev, rows + 2 * PAD, LANES), F32)] * 3
        + [
            pltpu.VMEM((256, LANES), F32),
            pltpu.VMEM((LANES, 256), F32),
            pltpu.VMEM((rows + 8, LANES), F32),
        ],
        compiler_params=pltpu.CompilerParams(vmem_limit_bytes=VMEM_LIMIT),
        cost_estimate=pl.CostEstimate(flops=10_000_000, bytes_accessed=8_000_000, transcendentals=0),
        name="edge_columns",
    )(*fields)


def edge_rows(own, halo, cosine, low):
    w = metric(cosine) * (0.5 * (own[8:12] + halo[8:12]))
    g = 0.5 * cosine * (own[4:8] + halo[4:8])
    f = w * (own[0:4] - halo[0:4]) if low else w * (halo[0:4] - own[0:4])
    return w, f, g


def pick(even, near, far):
    return jnp.where(even, far, near), jnp.where(even, near, far)


def columns_kernel(lat_total, rows, cols, far, near, far_in, near_in, _, near_ref, far_ref):
    lat, lon = lax.axis_index("lat"), lax.axis_index("lon")
    even = lat % 2 == 0
    own_s, own_n = pick(even, near[...], far[...])
    halo_s, halo_n = pick(even, near_in[...], far_in[...])
    w_s, f_s, g_s = edge_rows(own_s, halo_s, one_cos(lat * rows, lat_total), True)
    w_n, f_n, g_n = edge_rows(own_n, halo_n, one_cos((lat + 1) * rows, lat_total), False)
    h_s, h_n = f_s - g_s, f_n - g_n
    width = w_s.shape[-1]
    lane = lax.broadcasted_iota(jnp.int32, (4, width), 1)

    def side(at):
        source = 0 if at == 0 else width - 1
        base = at * COL_FIELDS * 4
        p, we, clon, total, number = [cols[pl.ds(base + i * 4, 4), :] for i in range(COL_FIELDS)]

        def put(x, value, target):
            return jnp.where(lane == target, pltpu.roll(value, (target - source) % width, 1), x)

        no = jnp.zeros_like(p)
        total = total + put(put(no, w_s, 0), w_n, rows - 1)
        number = number + put(put(no, -h_s, 0), h_n, rows - 1)
        p = put(put(p, halo_s[0:4], rows), halo_n[0:4], rows + 1)
        clon = put(put(clon, halo_s[20:24], rows), halo_n[20:24], rows + 1)
        we = put(put(we, halo_s[24:28], rows), halo_n[24:28], rows + 1)
        return jnp.concatenate((p, we, clon, total, number), 0)

    west, east = side(0), side(1)
    lon_even = lon % 2 == 0
    near_ref[...] = jnp.where(lon_even, east, west)
    far_ref[...] = jnp.where(lon_even, west, east)


def columns_call(lat_total, rows, cols, far, near, far_in, near_in, after):
    shape = jax.ShapeDtypeStruct((cols.shape[0] // 2, cols.shape[1]), F32)
    vmem = pl.BlockSpec(memory_space=pltpu.VMEM)
    return pl.pallas_call(
        lambda *refs: columns_kernel(lat_total, rows, *refs),
        in_specs=[vmem] * 6,
        out_specs=[vmem, vmem],
        out_shape=[shape, shape],
        compiler_params=pltpu.CompilerParams(vmem_limit_bytes=SMALL_VMEM),
        name="column_messages",
    )(cols, far, near, far_in, near_in, after)


def roll_west(tiles, lane):
    a, b = [pltpu.roll(x, 1, 1) for x in tiles]
    return a, jnp.where(lane == 0, a, b)


def roll_east(tiles, lane):
    a, b = [pltpu.roll(x, LANES - 1, 1) for x in tiles]
    return jnp.where(lane == LANES - 1, b, a), b


def halo_rows(lat_total, rows, messages):
    far, near, far_in, near_in = messages
    lat = lax.axis_index("lat")
    even = lat % 2 == 0
    own_s, own_n = pick(even, near, far)
    halo_s, halo_n = pick(even, near_in, far_in)
    w_s, f_s, g_s = edge_rows(own_s, halo_s, one_cos(lat * rows, lat_total), True)
    w_n, f_n, g_n = edge_rows(own_n, halo_n, one_cos((lat + 1) * rows, lat_total), False)
    into_s = f_s - jnp.where(lat == 0, -g_s, g_s)
    into_n = jnp.where(lat == lax.axis_size("lat") - 1, -g_n, g_n) - f_n
    return (halo_s, w_s, into_s), (halo_n, w_n, into_n)


EARLY = 2


def interior_kernel(lat_total, rows, before, *refs):
    early = lax.rem(lax.axis_index("lon"), lax.axis_size("lon") // 2) < EARLY
    state = refs[12:18] if before else refs[19:25]
    scratch = refs[18:] if before else refs[26:]

    @pl.when(early if before else jnp.logical_not(early))
    def _():
        correction(lat_total, rows, refs[:12], state, scratch)

    if not before:
        neighbours(lat_total, rows, refs[6], state, refs[25], scratch[3])


def correction(lat_total, rows, refs, state, scratch):
    p_ref, we_ref, wn_ref, f_ref, clon_ref, clat_ref, cv_ref, diag_ref = refs[:8]
    messages = refs[8:12]
    new_ref, delta, clatb, w_west, w_east, cols_ref = state
    pb, wnb, pack, cosines, sems = scratch
    moves = [
        pltpu.make_async_copy(
            ref.at[:, :, pl.ds(t * LANES, LANES)],
            buf.at[t, :, pl.ds(PAD, rows), :],
            sems.at[i, t],
        )
        for i, (ref, buf) in enumerate(((p_ref, pb), (wn_ref, wnb), (clat_ref, clatb)))
        for t in range(2)
    ]
    for move in moves:
        move.start()
    cosines[...] = face_cos(lax.axis_index("lat") * rows, cosines.shape, 0, lat_total)
    south, north = halo_rows(lat_total, rows, [m[...] for m in messages])
    wide = lax.broadcasted_iota(jnp.int32, (4, 2 * LANES), 1)
    inside = (wide > 0) & (wide < 2 * LANES - 1)

    def put_rows(buf, at, value):
        for t in range(2):
            for k in range(4):
                buf[t, k, at : at + 1, :] = value[k : k + 1, t * LANES : (t + 1) * LANES]

    for at, (halo, w, into) in ((PAD - 1, south), (PAD + rows, north)):
        put_rows(pb, at, halo[0:4])
        put_rows(wnb, at, halo[4:8])
        put_rows(clatb, at, halo[8:12])
        put_rows(delta, at, jnp.where(inside, (halo[16:20] + into) / (halo[12:16] + w), 0.0))
    pack[pl.ds(rows, 256 - rows), :] = jnp.zeros((256 - rows, LANES), F32)
    for move in moves:
        move.wait()

    shape = (BLOCK, LANES)
    lane = lax.broadcasted_iota(jnp.int32, shape, 1)
    edge = (lane == 0, lane == LANES - 1)
    tiles = [pl.ds(t * LANES, LANES) for t in range(2)]

    def first(r, carry):
        row = pl.multiple_of(r * BLOCK, BLOCK)
        c_s, c_n = cosines[pl.ds(row, BLOCK), :], cosines[pl.ds(row + 1, BLOCK), :]
        m_s, m_n = metric(c_s), metric(c_n)
        acc = [jnp.zeros(shape, F32) for _ in range(4)]
        for k in range(4):

            def get(buf, shift=0, level=k):
                return [buf[t, level, pl.ds(row + PAD + shift, BLOCK), :] for t in range(2)]

            def raw(ref, level=k):
                return [ref[level, pl.ds(row, BLOCK), tile] for tile in tiles]

            p, we, clon, clat, wn = get(pb), raw(we_ref), raw(clon_ref), get(clatb), get(wnb)
            p_w, p_e = roll_west(p, lane), roll_east(p, lane)
            we_w, we_e = roll_west(we, lane), roll_east(we, lane)
            clon_w, clon_e = roll_west(clon, lane), roll_east(clon, lane)
            wn_s, wn_n, clat_s, clat_n = get(wnb, -1), get(wnb, 1), get(clatb, -1), get(clatb, 1)
            p_s, p_n = get(pb, -1), get(pb, 1)
            forcing, below, diag = raw(f_ref), raw(cv_ref), raw(diag_ref)
            if k < 3:
                above, p_a = raw(cv_ref, k + 1), get(pb, 0, k + 1)
            if k > 0:
                p_b = get(pb, 0, k - 1)
            for t in range(2):
                w_e, w_w = clon[t] + clon_e[t], clon[t] + clon_w[t]
                w_n, w_s = m_n * (clat[t] + clat_n[t]), m_s * (clat[t] + clat_s[t])
                flux = w_e * (p_e[t] - p[t]) + w_w * (p_w[t] - p[t]) - (we_e[t] - we_w[t])
                flux += w_n * (p_n[t] - p[t]) + w_s * (p_s[t] - p[t])
                flux += c_s * (wn[t] + wn_s[t]) - c_n * (wn[t] + wn_n[t])
                weight = (w_e + w_w) + (w_n + w_s)
                total = diag[t] + below[t]
                number = forcing[t] - diag[t] * p[t]
                number += below[t] * (p_b[t] - p[t]) if k > 0 else -below[t] * p[t]
                if k < 3:
                    total += above[t]
                    number += above[t] * (p_a[t] - p[t])
                d = (number + 0.5 * flux) / (total + 0.5 * weight)
                d = jnp.where(edge[t], 0.0, d)
                at = pl.ds(row, BLOCK)
                delta[t, k, pl.ds(row + PAD, BLOCK), :] = d
                new_ref[t, k, at, :] = p[t] + d
                w_west[t, k, at, :] = jnp.where(edge[0], 0.0, w_w) if t == 0 else w_w
                w_east[t, k, at, :] = jnp.where(edge[1], 0.0, w_e) if t == 1 else w_e
            for i, x in enumerate((clon, clat, below)):
                index = i * 4 + k
                both = jnp.where(lane < LANES // 2, x[0], x[1])
                acc[k] = jnp.where(window_mask(lane, index), window_move(both, index), acc[k])
        pack[pl.ds(row, BLOCK), :] = (acc[0] + acc[1]) + (acc[2] + acc[3])
        return carry

    lax.fori_loop(0, rows // BLOCK, first, 0)
    cols_ref[...] = pack[...].T[:48]


def neighbours(lat_total, rows, cv_ref, state, res_ref, cosines):
    _, delta, clatb, w_west, w_east, _ = state
    cosines[...] = face_cos(lax.axis_index("lat") * rows, cosines.shape, 0, lat_total)
    lane = lax.broadcasted_iota(jnp.int32, (BLOCK, LANES), 1)
    tiles = [pl.ds(t * LANES, LANES) for t in range(2)]

    def second(r, carry):
        row = pl.multiple_of(r * BLOCK, BLOCK)
        at = pl.ds(row, BLOCK)
        m_s, m_n = metric(cosines[at, :]), metric(cosines[pl.ds(row + 1, BLOCK), :])
        for k in range(4):

            def get(buf, shift=0, level=k):
                return [buf[t, level, pl.ds(row + PAD + shift, BLOCK), :] for t in range(2)]

            d, d_s, d_n = get(delta), get(delta, -1), get(delta, 1)
            clat, clat_s, clat_n = get(clatb), get(clatb, -1), get(clatb, 1)
            d_w, d_e = roll_west(d, lane), roll_east(d, lane)
            for t in range(2):
                x_w, x_e = w_west[t, k, at, :] * d_w[t], w_east[t, k, at, :] * d_e[t]
                y = m_n * (clat[t] + clat_n[t]) * d_n[t] + m_s * (clat[t] + clat_s[t]) * d_s[t]
                out = 0.5 * ((x_w + x_e) + y)
                if k > 0:
                    out += cv_ref[k, at, tiles[t]] * get(delta, 0, k - 1)[t]
                if k < 3:
                    out += cv_ref[k + 1, at, tiles[t]] * get(delta, 0, k + 1)[t]
                res_ref[t, k, at, :] = out
        return carry

    lax.fori_loop(0, rows // BLOCK, second, 0)


def interior_call(lat_total, fields, messages, state=(), after=()):
    lev, rows, width = fields[0].shape
    tiles = width // LANES
    vmem = pl.BlockSpec(memory_space=pltpu.VMEM)
    plane = jax.ShapeDtypeStruct((tiles, lev, rows, LANES), F32)
    padded = jax.ShapeDtypeStruct((tiles, lev, rows + 2 * PAD, LANES), F32)
    cols = jax.ShapeDtypeStruct((12 * lev, 256), F32)
    out_shape = [plane, padded, padded, plane, plane, cols]
    before = not state
    if not before:
        out_shape.append(plane)
    operands = (*fields, *messages, *state, *after)
    return pl.pallas_call(
        lambda *refs: interior_kernel(lat_total, rows, before, *refs),
        in_specs=[vmem] * len(operands),
        out_specs=[vmem] * len(out_shape),
        out_shape=out_shape,
        scratch_shapes=[pltpu.VMEM(padded.shape, F32)] * 2
        + [
            pltpu.VMEM((256, LANES), F32),
            pltpu.VMEM((rows + 8, LANES), F32),
            pltpu.SemaphoreType.DMA((3, tiles)),
        ],
        input_output_aliases={12 + i: i for i in range(len(state))},
        compiler_params=pltpu.CompilerParams(vmem_limit_bytes=VMEM_LIMIT),
        cost_estimate=pl.CostEstimate(flops=20_000_000, bytes_accessed=16_000_000, transcendentals=0),
        name="interior_before" if before else "interior_beside",
    )(*operands)


def final_kernel(lat_total, rows, *refs):
    new_in, res_in, cols = refs[:3]
    rf, rn, rf_in, rn_in, cf, cn, cf_in, cn_in = refs[3:11]
    new_hbm, res_hbm = refs[11:13]
    new_buf, res_buf, stack, colv, sems = refs[13:]
    lat, lon = lax.axis_index("lat"), lax.axis_index("lon")
    width = 2 * LANES
    wide = lax.broadcasted_iota(jnp.int32, (4, width), 1)
    south, north = halo_rows(lat_total, rows, (rf[...], rn[...], rf_in[...], rn_in[...]))
    lon_even = lon % 2 == 0
    own_w, own_e = pick(lon_even, cn[...], cf[...])
    halo_w, halo_e = pick(lon_even, cn_in[...], cf_in[...])

    def put(x, value, source, target):
        return jnp.where(wide == target, pltpu.roll(value, (target - source) % width, 1), x)

    def edge_cols(own, halo, sign):
        w = 0.5 * (own[8:12] + halo[8:12])
        h = sign * w * (own[0:4] - halo[0:4]) - 0.5 * (own[4:8] + halo[4:8])
        d_own = (own[16:20] - sign * h) / (own[12:16] + w)
        d_halo = (halo[16:20] + sign * h) / (halo[12:16] + w)
        inside = wide < rows
        return w, h, jnp.where(inside, d_own, 0.0), jnp.where(inside, w * d_halo, 0.0)

    w_w, h_w, d_w, r_w = edge_cols(own_w, halo_w, 1.0)
    w_e, h_e, d_e, r_e = edge_cols(own_e, halo_e, -1.0)
    no = jnp.zeros((4, width), F32)

    def corner(source, halo, w, into):
        add_w = put(put(no, w_w, source, 0), w_e, source, width - 1)
        add_h = put(put(no, -h_w, source, 0), h_e, source, width - 1)
        return w * ((halo[16:20] + add_h + into) / (halo[12:16] + add_w + w))

    corner_s, corner_n = corner(rows, *south), corner(rows + 1, *north)
    m_s = metric(face_cos(lat * rows, (4, width), 1, lat_total))
    m_n = metric(face_cos(lat * rows + 1, (4, width), 1, lat_total))

    def column(field, offset):
        return jnp.concatenate(
            [cols[pl.ds(window_row(field * 4 + k, offset), 1), :] for k in range(4)], 0
        )

    stack[...] = jnp.zeros(stack.shape, F32)
    for edge, inner, source, d, beyond in ((2, 3, 0, d_w, r_w), (1, 0, width - 1, d_e, r_e)):
        clon, clat, below = [column(i, edge) for i in range(3)]
        clat_n, clat_s = pltpu.roll(clat, width - 1, 1), pltpu.roll(clat, 1, 1)
        d_n, d_s = pltpu.roll(d, width - 1, 1), pltpu.roll(d, 1, 1)
        at_edge = 0.5 * (m_n * (clat + clat_n) * d_n + m_s * (clat + clat_s) * d_s)
        at_edge += up_level(below) * up_level(d) + below * down_level(d) + beyond
        at_edge += put(put(no, corner_s, source, 0), corner_n, source, rows - 1)
        at_inner = 0.5 * (clon + column(0, inner)) * d
        for k in range(4):
            stack[pl.ds(window_row(k, edge), 1), :] = at_edge[k : k + 1]
            stack[pl.ds(window_row(k, inner), 1), :] = at_inner[k : k + 1]
            stack[pl.ds(window_row(4 + k, edge), 1), :] = d[k : k + 1]
    colv[...] = stack[...].T

    per = rows // CHUNKS
    lane = lax.broadcasted_iota(jnp.int32, (per, LANES), 1)
    edges = (lane < 2, lane >= LANES - 2)

    def sends(chunk):
        return [
            pltpu.make_async_copy(
                buf.at[t, :, pl.ds(chunk * per, per), :],
                out.at[:, pl.ds(chunk * per, per), pl.ds(t * LANES, LANES)],
                sems.at[chunk, i, t],
            )
            for i, (buf, out) in enumerate(((new_buf, new_hbm), (res_buf, res_hbm)))
            for t in range(2)
        ]

    for chunk in range(CHUNKS):
        at = pl.ds(chunk * per, per)
        packed = colv[at, :]
        for k in range(4):
            to_res = pltpu.roll(packed, (-4 * k - 2) % LANES, 1)
            to_new = pltpu.roll(packed, (-4 * (4 + k) - 2) % LANES, 1)
            for t in range(2):
                res_buf[t, k, at, :] = res_in[t, k, at, :] + jnp.where(edges[t], to_res, 0.0)
                new_buf[t, k, at, :] = new_in[t, k, at, :] + jnp.where(edges[t], to_new, 0.0)
        for copy in sends(chunk):
            copy.start()
    for chunk in range(CHUNKS):
        for copy in sends(chunk):
            copy.wait()


def final_call(lat_total, shape, planes, messages):
    lev, rows, width = shape
    tiles = width // LANES
    hbm, vmem = pl.BlockSpec(memory_space=pl.ANY), pl.BlockSpec(memory_space=pltpu.VMEM)
    out = jax.ShapeDtypeStruct(shape, F32)
    return pl.pallas_call(
        lambda *refs: final_kernel(lat_total, rows, *refs),
        in_specs=[vmem] * 11,
        out_specs=[hbm, hbm],
        out_shape=[out, out],
        scratch_shapes=[pltpu.VMEM((tiles, lev, rows, LANES), F32)] * 2
        + [
            pltpu.VMEM((LANES, 256), F32),
            pltpu.VMEM((256, LANES), F32),
            pltpu.SemaphoreType.DMA((CHUNKS, 2, tiles)),
        ],
        compiler_params=pltpu.CompilerParams(vmem_limit_bytes=VMEM_LIMIT),
        name="edges_and_store",
    )(*planes, *messages)


def per_device(pressure, wind_east, wind_north, forcing, coef_lon, coef_lat, coef_vert, diag_coef):
    fields = (pressure, wind_east, wind_north, forcing, coef_lon, coef_lat, coef_vert, diag_coef)
    rows = pressure.shape[1]
    lat_total = rows * lax.axis_size("lat")
    rows_near, rows_far, cols_near, cols_far = swap_pairs(
        lax.axis_size("lon"), lax.axis_size("lat")
    )
    near, far = rows_call(lat_total, fields)
    far_in = lax.ppermute(far, AXES, rows_far)
    near_in = lax.ppermute(near, AXES, rows_near)
    cols = edge_call(lat_total, fields)
    row_messages = (far, near, far_in, near_in)
    state = interior_call(lat_total, fields, row_messages)
    col_near, col_far = columns_call(lat_total, rows, cols, *row_messages, state[5])
    col_far_in = lax.ppermute(col_far, AXES, cols_far)
    col_near_in = lax.ppermute(col_near, AXES, cols_near)
    state = interior_call(lat_total, fields, row_messages, state, (col_near,))
    planes = (state[0], state[6], state[5])
    col_messages = (col_far, col_near, col_far_in, col_near_in)
    return final_call(lat_total, pressure.shape, planes, row_messages + col_messages)


def solution(mesh):
    spec = P(None, "lat", "lon")
    return jax.shard_map(
        per_device, mesh=mesh, in_specs=(spec,) * 8, out_specs=(spec, spec), check_vma=False
    )
```

```python
import math

import jax
import jax.numpy as jnp
from jax import lax
from jax.experimental import pallas as pl
from jax.experimental.pallas import tpu as pltpu
from jax.sharding import PartitionSpec as P

F32 = jnp.float32
AXES = ("lon", "lat")
LANES = 128
ROW_FIELDS = 7
COL_FIELDS = 5


def exchange_pairs(lon_count, lat_count):
    def flat(lon, lat):
        return (lon % lon_count) * lat_count + lat

    rows_near, rows_far, eastward, westward = [], [], [], []
    for lon in range(lon_count):
        for lat in range(lat_count):
            me = flat(lon, lat)
            rows_near.append((me, flat(lon, lat ^ 1)))
            if lat in (0, lat_count - 1):
                rows_far.append((me, flat(lon + lon_count // 2, lat)))
            else:
                rows_far.append((me, flat(lon, lat + 1 if lat % 2 else lat - 1)))
            eastward.append((me, flat(lon + 1, lat)))
            westward.append((me, flat(lon - 1, lat)))
    return rows_near, rows_far, eastward, westward


def face_cos(first, shape, axis, lat_total):
    position = (first + lax.broadcasted_iota(jnp.int32, shape, axis)).astype(F32)
    angle = position * (math.pi / lat_total) - math.pi / 2
    square = angle * angle
    cosine = jnp.full(shape, 1.0 / math.factorial(16), F32)
    for power in range(14, -1, -2):
        cosine = (-1.0) ** (power // 2) / math.factorial(power) + square * cosine
    return cosine


def metric(cosine):
    return 0.5 * (1.0 + jnp.abs(cosine))


def up_level(x):
    return jnp.concatenate((x[1:], jnp.zeros_like(x[:1])), 0)


def down_level(x):
    return jnp.concatenate((jnp.zeros_like(x[:1]), x[:-1]), 0)


def one_cos(row, lat_total):
    return face_cos(row, (1, 2 * LANES), 0, lat_total)


SMALL_VMEM = 4 * 2**20


def rows_kernel(lat_total, rows, *refs):
    low, high, (near_ref, far_ref) = refs[:8], refs[8:16], refs[16:]
    lat = lax.axis_index("lat")
    width = near_ref.shape[-1]
    lane = lax.broadcasted_iota(jnp.int32, (4, width), 1)

    def message(fields, edge, inner, face, sign):
        p, we, wn, forcing, clon, clat, cvert, diag = [f[:, edge, :] for f in fields]
        p_in, wn_in, clat_in = [fields[i][:, inner, :] for i in (0, 2, 5)]
        cosine = one_cos(face, lat_total)
        east = lane < width - 1
        w_east = jnp.where(east, 0.5 * (clon + pltpu.roll(clon, width - 1, 1)), 0.0)
        h_east = jnp.where(
            east,
            w_east * (pltpu.roll(p, width - 1, 1) - p) - 0.5 * (we + pltpu.roll(we, width - 1, 1)),
            0.0,
        )
        w_in = metric(cosine) * (0.5 * (clat + clat_in))
        h_in = w_in * (p_in - p) - sign * (0.5 * cosine * (wn + wn_in))
        w_up = up_level(cvert)
        h_up = w_up * (up_level(p) - p)
        below = cvert * (p - down_level(p))
        total = diag + w_east + pltpu.roll(w_east, 1, 1) + w_in + cvert + w_up
        number = forcing - diag * p + h_east - pltpu.roll(h_east, 1, 1) + h_in + h_up - below
        return jnp.concatenate((p, wn, clat, total, number, clon, we), 0)

    start = lat * rows
    south = message(low, 0, 1, start + 1, 1.0)
    north = message(high, 7, 6, start + rows - 1, -1.0)
    even = lat % 2 == 0
    near_ref[...] = jnp.where(even, north, south)
    far_ref[...] = jnp.where(even, south, north)


def rows_call(lat_total, fields):
    lev, rows, width = fields[0].shape
    low = pl.BlockSpec((lev, 8, width), lambda i: (0, 0, 0))
    high = pl.BlockSpec((lev, 8, width), lambda i: (0, rows // 8 - 1, 0))
    shape = jax.ShapeDtypeStruct((ROW_FIELDS * lev, width), F32)
    pinned = [pltpu.with_memory_space_constraint(f, pltpu.HBM) for f in fields]
    out = pl.BlockSpec((ROW_FIELDS * lev, width), lambda i: (0, 0))
    return pl.pallas_call(
        lambda *refs: rows_kernel(lat_total, rows, *refs),
        grid=(1,),
        in_specs=[low] * 8 + [high] * 8,
        out_specs=[out, out],
        out_shape=[shape, shape],
        compiler_params=pltpu.CompilerParams(vmem_limit_bytes=SMALL_VMEM),
        name="row_messages",
    )(*pinned, *pinned)


CHUNKS = 5
PAD = 8
BLOCK = 48
VMEM_LIMIT = 24 * 2**20


def window_mask(lane, index):
    return lane // 4 == index


def window_row(index, offset):
    return 4 * index + offset


def merged(ref, level, row, count, lane):
    at = pl.ds(row, count)
    return jnp.where(lane < LANES // 2, ref[level, at, 0:LANES], ref[level, at, LANES : 2 * LANES])


def window_move(x, index):
    return pltpu.roll(x, (4 * index + 2) % LANES, 1)


def edge_kernel(lat_total, rows, *refs):
    p_ref, we_ref, wn_ref, f_ref, clon_ref, clat_ref, cv_ref, diag_ref = refs[:8]
    cols_ref, *planes = refs[8:12]
    pm, wnm, clatm, pack, packed, cosines, sems = refs[12:]
    moves = [
        pltpu.make_async_copy(
            ref.at[:, :, pl.ds(t * LANES, LANES)],
            plane.at[t, :, pl.ds(PAD, rows), :],
            sems.at[i, t],
        )
        for i, (ref, plane) in enumerate(zip((p_ref, wn_ref, clat_ref), planes))
        for t in range(2)
    ]
    for move in moves:
        move.start()
    start = lax.axis_index("lat") * rows
    cosines[...] = face_cos(start, cosines.shape, 0, lat_total)
    shape = (BLOCK, LANES)
    lane = lax.broadcasted_iota(jnp.int32, shape, 1)

    def gather(r, carry):
        row = pl.multiple_of(r * BLOCK, BLOCK)
        for ref, buf in ((p_ref, pm), (wn_ref, wnm), (clat_ref, clatm)):
            for k in range(4):
                buf[k, pl.ds(row + PAD, BLOCK), :] = merged(ref, k, row, BLOCK, lane)
        return carry

    lax.fori_loop(0, rows // BLOCK, gather, 0)
    for buf, sign in ((pm, 1.0), (wnm, -1.0), (clatm, -1.0)):
        for k in range(4):
            for inside, outside in ((PAD, PAD - 1), (PAD + rows - 1, PAD + rows)):
                buf[k, outside : outside + 1, :] = sign * buf[k, inside : inside + 1, :]
    pack[pl.ds(rows, 256 - rows), :] = jnp.zeros((256 - rows, LANES), F32)

    def step(r, carry):
        row = pl.multiple_of(r * BLOCK, BLOCK)
        c_s, c_n = cosines[pl.ds(row, BLOCK), :], cosines[pl.ds(row + 1, BLOCK), :]
        m_s, m_n = metric(c_s), metric(c_n)
        acc = [jnp.zeros(shape, F32) for _ in range(4)]
        for k in range(4):

            def get(buf, shift=0, level=k):
                return buf[level, pl.ds(row + PAD + shift, BLOCK), :]

            def raw(ref, level=k):
                return merged(ref, level, row, BLOCK, lane)

            p, clat, wn = get(pm), get(clatm), get(wnm)
            below, diag = raw(cv_ref) if k == 0 else above, raw(diag_ref)
            w_n, w_s = m_n * (clat + get(clatm, 1)), m_s * (clat + get(clatm, -1))
            flux = w_n * (get(pm, 1) - p) + w_s * (get(pm, -1) - p)
            flux += c_s * (wn + get(wnm, -1)) - c_n * (wn + get(wnm, 1))
            total = diag + below
            number = raw(f_ref) - diag * p - (below * p if k == 0 else lifted)
            if k < 3:
                above = raw(cv_ref, k + 1)
                lifted = above * (get(pm, 0, k + 1) - p)
                total += above
                number += lifted
            total += 0.5 * (w_n + w_s)
            number += 0.5 * flux
            for i, x in enumerate((p, raw(we_ref), raw(clon_ref), total, number)):
                index = i * 4 + k
                acc[k] = jnp.where(window_mask(lane, index), window_move(x, index), acc[k])
        pack[pl.ds(row, BLOCK), :] = (acc[0] + acc[1]) + (acc[2] + acc[3])
        return carry

    lax.fori_loop(0, rows // BLOCK, step, 0)
    packed[...] = pack[...].T

    def column(field, offset):
        return jnp.concatenate(
            [packed[pl.ds(window_row(field * 4 + k, offset), 1), :] for k in range(4)], 0
        )

    for side, (edge, inner, sign) in enumerate(((2, 3, 1.0), (1, 0, -1.0))):
        p, we, clon, total, number = [column(i, edge) for i in range(COL_FIELDS)]
        p_in, we_in, clon_in = [column(i, inner) for i in range(3)]
        w = 0.5 * (clon + clon_in)
        number = number + w * (p_in - p) - sign * (0.5 * (we + we_in))
        for i, x in enumerate((p, we, clon, total + w, number)):
            cols_ref[pl.ds((side * COL_FIELDS + i) * 4, 4), :] = x
    for move in moves:
        move.wait()


def edge_call(lat_total, fields):
    lev, rows, width = fields[0].shape
    cols = jax.ShapeDtypeStruct((2 * COL_FIELDS * lev, 256), F32)
    vmem = pl.BlockSpec(memory_space=pltpu.VMEM)
    return pl.pallas_call(
        lambda *refs: edge_kernel(lat_total, rows, *refs),
        in_specs=[vmem] * 8,
        out_specs=[vmem] * 4,
        out_shape=[cols] + [jax.ShapeDtypeStruct((2, lev, rows + 2 * PAD, LANES), F32)] * 3,
        scratch_shapes=[pltpu.VMEM((lev, rows + 2 * PAD, LANES), F32)] * 3
        + [
            pltpu.VMEM((256, LANES), F32),
            pltpu.VMEM((LANES, 256), F32),
            pltpu.VMEM((rows + 8, LANES), F32),
            pltpu.SemaphoreType.DMA((3, 2)),
        ],
        compiler_params=pltpu.CompilerParams(vmem_limit_bytes=VMEM_LIMIT),
        cost_estimate=pl.CostEstimate(flops=10_000_000, bytes_accessed=8_000_000, transcendentals=0),
        name="edge_columns",
    )(*fields)


def edge_rows(own, halo, cosine, low):
    w = metric(cosine) * (0.5 * (own[8:12] + halo[8:12]))
    g = 0.5 * cosine * (own[4:8] + halo[4:8])
    f = w * (own[0:4] - halo[0:4]) if low else w * (halo[0:4] - own[0:4])
    return w, f, g


def pick(even, near, far):
    return jnp.where(even, far, near), jnp.where(even, near, far)


def columns_kernel(lat_total, rows, cols, near, far, near_in, far_in, _, west_ref, east_ref, sent_ref):
    lat = lax.axis_index("lat")
    even = lat % 2 == 0
    own_s, own_n = pick(even, near[...], far[...])
    halo_s, halo_n = pick(even, near_in[...], far_in[...])
    w_s, f_s, g_s = edge_rows(own_s, halo_s, one_cos(lat * rows, lat_total), True)
    w_n, f_n, g_n = edge_rows(own_n, halo_n, one_cos((lat + 1) * rows, lat_total), False)
    h_s, h_n = f_s - g_s, f_n - g_n
    width = w_s.shape[-1]
    lane = lax.broadcasted_iota(jnp.int32, (4, width), 1)

    def side(at):
        source = 0 if at == 0 else width - 1
        base = at * COL_FIELDS * 4
        p, we, clon, total, number = [cols[pl.ds(base + i * 4, 4), :] for i in range(COL_FIELDS)]

        def put(x, value, target):
            return jnp.where(lane == target, pltpu.roll(value, (target - source) % width, 1), x)

        no = jnp.zeros_like(p)
        total = total + put(put(no, w_s, 0), w_n, rows - 1)
        number = number + put(put(no, -h_s, 0), h_n, rows - 1)
        p = put(put(p, halo_s[0:4], rows), halo_n[0:4], rows + 1)
        clon = put(put(clon, halo_s[20:24], rows), halo_n[20:24], rows + 1)
        we = put(put(we, halo_s[24:28], rows), halo_n[24:28], rows + 1)
        return jnp.concatenate((p, we, clon, total, number), 0)

    west_ref[...] = side(0)
    east = side(1)
    east_ref[...] = east
    sent_ref[...] = east


def columns_call(lat_total, rows, cols, near, far, near_in, far_in, after):
    shape = jax.ShapeDtypeStruct((cols.shape[0] // 2, cols.shape[1]), F32)
    vmem = pl.BlockSpec(memory_space=pltpu.VMEM)
    return pl.pallas_call(
        lambda *refs: columns_kernel(lat_total, rows, *refs),
        in_specs=[vmem] * 6,
        out_specs=[vmem] * 3,
        out_shape=[shape] * 3,
        compiler_params=pltpu.CompilerParams(vmem_limit_bytes=SMALL_VMEM),
        name="column_messages",
    )(cols, near, far, near_in, far_in, after)


def roll_west(tiles, lane):
    a, b = [pltpu.roll(x, 1, 1) for x in tiles]
    return a, jnp.where(lane == 0, a, b)


def roll_east(tiles, lane):
    a, b = [pltpu.roll(x, LANES - 1, 1) for x in tiles]
    return jnp.where(lane == LANES - 1, b, a), b


EDGE_TERMS = 8
STATE = 5
AHEAD = 3
BETWEEN = 3


def place():
    return lax.rem(lax.axis_index("lon"), lax.axis_size("lon") // 2)


def interior_ahead(lat_total, rows, *refs):
    @pl.when(place() == 0)
    def _():
        correction(lat_total, rows, refs[:8], refs[8:11], refs[11:15], refs[15:], 0, AHEAD)


def interior_between(lat_total, rows, *refs):
    fields, messages, planes, refs = refs[:8], refs[8:12], refs[12:14], refs[14 + STATE + 1 :]
    state, (_, terms_ref, res_ref), scratch = refs[:STATE], refs[STATE : STATE + 3], refs[STATE + 3 :]
    first = place() == 0

    @pl.when(place() < 2)
    def _():
        begin, end = jnp.where(first, AHEAD, 0), jnp.where(first, rows // BLOCK, BETWEEN)
        planes_here = (*planes, state[4])
        correction(lat_total, rows, fields, planes_here, state[:4], scratch, begin, end)

    @pl.when(first)
    def _():
        edges(lat_total, rows, fields[4:7], messages, state, terms_ref, scratch)
        residual(lat_total, rows, fields[6], state, res_ref, scratch)


def interior(lat_total, rows, *refs):
    fields, messages, planes, refs = refs[:8], refs[8:12], refs[12:14], refs[14 + STATE + 2 + 1 :]
    state, terms_ref, res_ref, scratch = refs[:STATE], refs[STATE], refs[STATE + 1], refs[STATE + 2 :]

    @pl.when(place() > 0)
    def _():
        begin, planes_here = jnp.where(place() == 1, BETWEEN, 0), (*planes, state[4])
        correction(lat_total, rows, fields, planes_here, state[:4], scratch, begin, rows // BLOCK)
        edges(lat_total, rows, fields[4:7], messages, state, terms_ref, scratch)
        residual(lat_total, rows, fields[6], state, res_ref, scratch)


def quotient(x, y):
    guess = pl.reciprocal(y, approx=True)
    guess = guess * (2.0 - y * guess)
    return x * guess


def correction(lat_total, rows, fields, planes, outs, scratch, begin, end):
    _, we_ref, _, f_ref, clon_ref, _, cv_ref, diag_ref = fields
    pb, wnb, clatb = planes
    new_ref, delta, w_west, w_east = outs
    cosines = scratch[-1]
    cosines[...] = face_cos(lax.axis_index("lat") * rows, cosines.shape, 0, lat_total)
    shape = (BLOCK, LANES)
    lane = lax.broadcasted_iota(jnp.int32, shape, 1)
    edge = (lane == 0, lane == LANES - 1)
    tiles = [pl.ds(t * LANES, LANES) for t in range(2)]

    def first(r, carry):
        row = pl.multiple_of(r * BLOCK, BLOCK)
        c_s, c_n = cosines[pl.ds(row, BLOCK), :], cosines[pl.ds(row + 1, BLOCK), :]
        m_s, m_n = metric(c_s), metric(c_n)
        lifted = None
        for k in range(4):

            def get(buf, shift=0, level=k):
                return [buf[t, level, pl.ds(row + PAD + shift, BLOCK), :] for t in range(2)]

            def raw(ref, level=k):
                return [ref[level, pl.ds(row, BLOCK), tile] for tile in tiles]

            p, we, clon, clat, wn = get(pb), raw(we_ref), raw(clon_ref), get(clatb), get(wnb)
            p_e, we_e, clon_e = [roll_east(x, lane) for x in (p, we, clon)]
            p_w, we_w, clon_w = [roll_west(x, lane) for x in (p, we, clon)]
            wn_s, wn_n, clat_s, clat_n = get(wnb, -1), get(wnb, 1), get(clatb, -1), get(clatb, 1)
            p_s, p_n = get(pb, -1), get(pb, 1)
            forcing, diag = raw(f_ref), raw(diag_ref)
            below = raw(cv_ref) if k == 0 else above
            if k < 3:
                above, p_a = raw(cv_ref, k + 1), get(pb, 0, k + 1)
            fallen, lifted = lifted, []
            for t in range(2):
                w_e, w_w = clon[t] + clon_e[t], clon[t] + clon_w[t]
                w_n, w_s = m_n * (clat[t] + clat_n[t]), m_s * (clat[t] + clat_s[t])
                flux = w_e * (p_e[t] - p[t]) + w_w * (p_w[t] - p[t]) - (we_e[t] - we_w[t])
                flux += w_n * (p_n[t] - p[t]) + w_s * (p_s[t] - p[t])
                flux += c_s * (wn[t] + wn_s[t]) - c_n * (wn[t] + wn_n[t])
                weight = (w_e + w_w) + (w_n + w_s)
                total = diag[t] + below[t]
                number = forcing[t] - diag[t] * p[t] - (below[t] * p[t] if k == 0 else fallen[t])
                if k < 3:
                    lifted.append(above[t] * (p_a[t] - p[t]))
                    total += above[t]
                    number += lifted[t]
                d = quotient(number + 0.5 * flux, total + 0.5 * weight)
                d = jnp.where(edge[t], 0.0, d)
                at = pl.ds(row, BLOCK)
                delta[t, k, pl.ds(row + PAD, BLOCK), :] = d
                new_ref[t, k, at, :] = p[t] + d
                w_west[t, k, at, :] = jnp.where(edge[0], 0.0, w_w) if t == 0 else w_w
                w_east[t, k, at, :] = jnp.where(edge[1], 0.0, w_e) if t == 1 else w_e
        return carry

    lax.fori_loop(begin, end, first, 0)


def edges(lat_total, rows, coefs, messages, state, terms_ref, scratch):
    clon_ref, clat_ref, cv_ref = coefs
    near, far, near_in, far_in = [m[...] for m in messages]
    new_ref, delta, _, _, clatb = state
    pack, packed, _ = scratch
    lat = lax.axis_index("lat")
    width = 2 * LANES
    wide = lax.broadcasted_iota(jnp.int32, (4, width), 1)
    inside = (wide > 0) & (wide < width - 1)
    even = lat % 2 == 0
    own_s, own_n = pick(even, near, far)
    halo_s, halo_n = pick(even, near_in, far_in)
    w_s, f_s, g_s = edge_rows(own_s, halo_s, one_cos(lat * rows, lat_total), True)
    w_n, f_n, g_n = edge_rows(own_n, halo_n, one_cos((lat + 1) * rows, lat_total), False)
    into_s = f_s - jnp.where(lat == 0, -g_s, g_s)
    into_n = jnp.where(lat == lax.axis_size("lat") - 1, -g_n, g_n) - f_n

    def put_rows(buf, at, value):
        for t in range(2):
            for k in range(4):
                buf[t, k, at : at + 1, :] = value[k : k + 1, t * LANES : (t + 1) * LANES]

    corners = []
    for own, halo, w, into, flux, at, beyond in (
        (own_s, halo_s, w_s, into_s, g_s - f_s, 0, -1),
        (own_n, halo_n, w_n, into_n, f_n - g_n, rows - 1, rows),
    ):
        halo_number, halo_total = halo[16:20] + into, halo[12:16] + w
        d_own = jnp.where(inside, (own[16:20] + flux) / (own[12:16] + w), 0.0)
        put_rows(new_ref, at, own[0:4] + d_own)
        put_rows(delta, PAD + at, d_own)
        put_rows(delta, PAD + beyond, jnp.where(inside, halo_number / halo_total, 0.0))
        put_rows(clatb, PAD + beyond, halo[8:12])
        corners.append((w, halo_number, halo_total, at))
    pack[pl.ds(rows, 256 - rows), :] = jnp.zeros((256 - rows, LANES), F32)
    shape = (BLOCK, LANES)
    lane = lax.broadcasted_iota(jnp.int32, shape, 1)
    tiles = [pl.ds(t * LANES, LANES) for t in range(2)]

    def gather(r, carry):
        row = pl.multiple_of(r * BLOCK, BLOCK)
        acc = [jnp.zeros(shape, F32) for _ in range(4)]
        for k in range(4):
            for i, ref in enumerate((clon_ref, clat_ref, cv_ref)):
                index = i * 4 + k
                both = merged(ref, k, row, BLOCK, lane)
                acc[k] = jnp.where(window_mask(lane, index), window_move(both, index), acc[k])
        pack[pl.ds(row, BLOCK), :] = (acc[0] + acc[1]) + (acc[2] + acc[3])
        return carry

    lax.fori_loop(0, rows // BLOCK, gather, 0)
    packed[...] = pack[...].T
    m_s = metric(face_cos(lat * rows, (4, width), 1, lat_total))
    m_n = metric(face_cos(lat * rows + 1, (4, width), 1, lat_total))

    def column(field, offset):
        return jnp.concatenate(
            [packed[pl.ds(window_row(field * 4 + k, offset), 1), :] for k in range(4)], 0
        )

    for side, (edge, inner, source) in enumerate(((2, 3, 0), (1, 0, width - 1))):
        clon, clat, below = [column(i, edge) for i in range(3)]
        ends = [jnp.zeros((4, width), F32), jnp.zeros((4, width), F32), jnp.ones((4, width), F32)]
        for *values, at in corners:
            for i, value in enumerate(values):
                ends[i] = jnp.where(wide == at, pltpu.roll(value, (at - source) % width, 1), ends[i])
        terms = (
            0.5 * m_n * (clat + pltpu.roll(clat, width - 1, 1)),
            0.5 * m_s * (clat + pltpu.roll(clat, 1, 1)),
            0.5 * (clon + column(0, inner)),
            up_level(below),
            below,
            *ends,
        )
        for i, term in enumerate(terms):
            terms_ref[pl.ds((side * EDGE_TERMS + i) * 4, 4), :] = term


def residual(lat_total, rows, cv_ref, state, res_ref, scratch):
    _, delta, w_west, w_east, clatb = state
    cosines = scratch[-1]
    cosines[...] = face_cos(lax.axis_index("lat") * rows, cosines.shape, 0, lat_total)
    lane = lax.broadcasted_iota(jnp.int32, (BLOCK, LANES), 1)
    tiles = [pl.ds(t * LANES, LANES) for t in range(2)]

    def second(r, carry):
        row = pl.multiple_of(r * BLOCK, BLOCK)
        at = pl.ds(row, BLOCK)
        m_s, m_n = metric(cosines[at, :]), metric(cosines[pl.ds(row + 1, BLOCK), :])
        for k in range(4):

            def get(buf, shift=0, level=k):
                return [buf[t, level, pl.ds(row + PAD + shift, BLOCK), :] for t in range(2)]

            d, d_s, d_n = get(delta), get(delta, -1), get(delta, 1)
            clat, clat_s, clat_n = get(clatb), get(clatb, -1), get(clatb, 1)
            d_w, d_e = roll_west(d, lane), roll_east(d, lane)
            for t in range(2):
                x_w, x_e = w_west[t, k, at, :] * d_w[t], w_east[t, k, at, :] * d_e[t]
                y = m_n * (clat[t] + clat_n[t]) * d_n[t] + m_s * (clat[t] + clat_s[t]) * d_s[t]
                out = 0.5 * ((x_w + x_e) + y)
                if k > 0:
                    out += cv_ref[k, at, tiles[t]] * get(delta, 0, k - 1)[t]
                if k < 3:
                    out += cv_ref[k + 1, at, tiles[t]] * get(delta, 0, k + 1)[t]
                res_ref[t, k, at, :] = out
        return carry

    lax.fori_loop(0, rows // BLOCK, second, 0)


def interior_call(lat_total, shape, kernel, inputs, kept, after, results):
    lev, rows, width = shape
    tiles = width // LANES
    vmem = pl.BlockSpec(memory_space=pltpu.VMEM)
    shapes = {
        "plane": (tiles, lev, rows, LANES),
        "padded": (tiles, lev, rows + 2 * PAD, LANES),
        "message": (COL_FIELDS * lev, 256),
        "terms": (2 * EDGE_TERMS * lev, 256),
    }
    operands = (*inputs, *kept, *after)
    return pl.pallas_call(
        lambda *refs: kernel(lat_total, rows, *refs),
        in_specs=[vmem] * len(operands),
        out_specs=[vmem] * len(results),
        out_shape=[jax.ShapeDtypeStruct(shapes[name], F32) for name in results],
        scratch_shapes=[
            pltpu.VMEM((256, LANES), F32),
            pltpu.VMEM((LANES, 256), F32),
            pltpu.VMEM((rows + 8, LANES), F32),
        ],
        input_output_aliases={len(inputs) + i: i for i in range(len(kept))},
        compiler_params=pltpu.CompilerParams(vmem_limit_bytes=VMEM_LIMIT),
        cost_estimate=pl.CostEstimate(flops=20_000_000, bytes_accessed=16_000_000, transcendentals=0),
        name=kernel.__name__,
    )(*operands)


def final_kernel(rows, *refs):
    new_in, res_in, terms, own_w, own_e, halo_w, halo_e = refs[:7]
    new_hbm, res_hbm, new_buf, res_buf, stack, colv, sems = refs[7:]
    width = 2 * LANES
    wide = lax.broadcasted_iota(jnp.int32, (4, width), 1)
    low, high, inside = wide == 0, wide == rows - 1, wide < rows
    own, halo = (own_w, own_e), (halo_w, halo_e)

    def ends(x):
        south, north = pltpu.roll(x, width - rows, 1), pltpu.roll(x, width - 2, 1)
        return jnp.where(low, south, jnp.where(high, north, 0.0))

    for side, (edge, inner, sign) in enumerate(((2, 3, 1.0), (1, 0, -1.0))):
        o_p, o_we, o_clon, o_total, o_number = [own[side][pl.ds(4 * i, 4), :] for i in range(5)]
        h_p, h_we, h_clon, h_total, h_number = [halo[side][pl.ds(4 * i, 4), :] for i in range(5)]
        a_n, a_s, w_in, above, below, c_w, c_number, c_total = [
            terms[pl.ds((side * EDGE_TERMS + i) * 4, 4), :] for i in range(EDGE_TERMS)
        ]
        w = 0.5 * (o_clon + h_clon)
        h = w * (o_p - h_p) - sign * (0.5 * (o_we + h_we))
        d = jnp.where(inside, (o_number - h) / (o_total + w), 0.0)
        beyond = jnp.where(inside, w * ((h_number + h) / (h_total + w)), 0.0)
        corner = c_w * ((c_number - ends(h)) / (c_total + ends(w)))
        at_edge = a_n * pltpu.roll(d, width - 1, 1) + a_s * pltpu.roll(d, 1, 1)
        at_edge += above * up_level(d) + below * down_level(d) + (beyond + corner)
        for first, x in ((edge, at_edge), (inner, w_in * d), (16 + edge, d)):
            for t in range(2):
                stack[t, pl.ds(first, 4, stride=4), :] = x[:, t * LANES : (t + 1) * LANES]
    for t in range(2):
        colv[pl.ds(t * LANES, LANES), :] = stack[t].T

    per = rows // CHUNKS
    lane = lax.broadcasted_iota(jnp.int32, (per, LANES), 1)
    edges = (lane < 2, lane >= LANES - 2)
    edge = (lane == 0, lane == LANES - 1)

    def sends(chunk):
        return [
            pltpu.make_async_copy(
                buf.at[t, :, pl.ds(chunk * per, per), :],
                out.at[:, pl.ds(chunk * per, per), pl.ds(t * LANES, LANES)],
                sems.at[chunk, i, t],
            )
            for i, (buf, out) in enumerate(((new_buf, new_hbm), (res_buf, res_hbm)))
            for t in range(2)
        ]

    for chunk in range(CHUNKS):
        at = pl.ds(chunk * per, per)
        packed = colv[at, :]
        for k in range(4):
            to_res = pltpu.roll(packed, (-4 * k - 2) % LANES, 1)
            to_new = pltpu.roll(packed, (-4 * (4 + k) - 2) % LANES, 1)
            for t in range(2):
                res_buf[t, k, at, :] = res_in[t, k, at, :] + jnp.where(edges[t], to_res, 0.0)
                new_buf[t, k, at, :] = new_in[t, k, at, :] + jnp.where(edge[t], to_new, 0.0)
        for copy in sends(chunk):
            copy.start()
    for chunk in range(CHUNKS):
        for copy in sends(chunk):
            copy.wait()


def final_call(shape, planes, messages):
    lev, rows, width = shape
    tiles = width // LANES
    hbm, vmem = pl.BlockSpec(memory_space=pl.ANY), pl.BlockSpec(memory_space=pltpu.VMEM)
    out = jax.ShapeDtypeStruct(shape, F32)
    return pl.pallas_call(
        lambda *refs: final_kernel(rows, *refs),
        in_specs=[vmem] * 7,
        out_specs=[hbm, hbm],
        out_shape=[out, out],
        scratch_shapes=[pltpu.VMEM((tiles, lev, rows, LANES), F32)] * 2
        + [
            pltpu.VMEM((2, LANES, LANES), F32),
            pltpu.VMEM((256, LANES), F32),
            pltpu.SemaphoreType.DMA((CHUNKS, 2, tiles)),
        ],
        compiler_params=pltpu.CompilerParams(vmem_limit_bytes=VMEM_LIMIT),
        name="edges_and_store",
    )(*planes, *messages)


def per_device(pressure, wind_east, wind_north, forcing, coef_lon, coef_lat, coef_vert, diag_coef):
    fields = (pressure, wind_east, wind_north, forcing, coef_lon, coef_lat, coef_vert, diag_coef)
    rows = pressure.shape[1]
    lat_total = rows * lax.axis_size("lat")
    rows_near, rows_far, eastward, westward = exchange_pairs(
        lax.axis_size("lon"), lax.axis_size("lat")
    )
    near, far = rows_call(lat_total, fields)
    far_in = lax.ppermute(far, AXES, rows_far)
    near_in = lax.ppermute(near, AXES, rows_near)
    cols, p_planes, wn_planes, clat_planes = edge_call(lat_total, fields)
    row_messages = (near, far, near_in, far_in)
    shape = pressure.shape
    planes = (p_planes, wn_planes, clat_planes)
    kinds = ("plane", "padded", "plane", "plane", "padded")
    state = interior_call(
        lat_total, shape, interior_ahead, (*fields, *planes), (), (), kinds[:-1]
    )
    west, east, sent = columns_call(lat_total, rows, cols, *row_messages, state[0])
    from_west = lax.ppermute(sent, AXES, eastward)
    *state, west, terms, residual_part = interior_call(
        lat_total,
        shape,
        interior_between,
        (*fields, *row_messages, *planes[:2]),
        (*state, clat_planes, west),
        (),
        (*kinds, "message", "terms", "plane"),
    )
    from_east = lax.ppermute(west, AXES, westward)
    new_pressure, *_, terms, residual_part = interior_call(
        lat_total,
        shape,
        interior,
        (*fields, *row_messages, *planes[:2]),
        (*state, terms, residual_part),
        (west,),
        (*kinds, "terms", "plane"),
    )
    col_messages = (west, east, from_west, from_east)
    return final_call(shape, (new_pressure, residual_part, terms), col_messages)


def solution(mesh):
    spec = P(None, "lat", "lon")
    return jax.shard_map(
        per_device, mesh=mesh, in_specs=(spec,) * 8, out_specs=(spec, spec), check_vma=False
    )
```

```python
import math

import jax
import jax.numpy as jnp
from jax import lax
from jax.experimental import pallas as pl
from jax.experimental.pallas import tpu as pltpu
from jax.sharding import PartitionSpec as P

F32 = jnp.float32
AXES = ("lon", "lat")
LANES = 128
ROW_FIELDS = 6
COL_FIELDS = 5


def exchange_pairs(lon_count, lat_count):
    def flat(lon, lat):
        return (lon % lon_count) * lat_count + lat

    rows_near, rows_far, eastward, westward = [], [], [], []
    for lon in range(lon_count):
        for lat in range(lat_count):
            me = flat(lon, lat)
            rows_near.append((me, flat(lon, lat ^ 1)))
            if lat in (0, lat_count - 1):
                rows_far.append((me, flat(lon + lon_count // 2, lat)))
            else:
                rows_far.append((me, flat(lon, lat + 1 if lat % 2 else lat - 1)))
            eastward.append((me, flat(lon + 1, lat)))
            westward.append((me, flat(lon - 1, lat)))
    return rows_near, rows_far, eastward, westward


def face_cos(first, shape, axis, lat_total):
    position = (first + lax.broadcasted_iota(jnp.int32, shape, axis)).astype(F32)
    angle = position * (math.pi / lat_total) - math.pi / 2
    square = angle * angle
    cosine = jnp.full(shape, 1.0 / math.factorial(16), F32)
    for power in range(14, -1, -2):
        cosine = (-1.0) ** (power // 2) / math.factorial(power) + square * cosine
    return cosine


def metric(cosine):
    return 0.5 * (1.0 + jnp.abs(cosine))


def up_level(x):
    return jnp.concatenate((x[1:], jnp.zeros_like(x[:1])), 0)


def down_level(x):
    return jnp.concatenate((jnp.zeros_like(x[:1]), x[:-1]), 0)


def one_cos(row, lat_total):
    return face_cos(row, (1, 2 * LANES), 0, lat_total)


SMALL_VMEM = 4 * 2**20


def rows_kernel(lat_total, rows, *refs):
    low, high, (near_ref, far_ref) = refs[:8], refs[8:16], refs[16:]
    lat = lax.axis_index("lat")
    width = near_ref.shape[-1]
    lane = lax.broadcasted_iota(jnp.int32, (4, width), 1)

    def message(fields, edge, inner, face, sign):
        p, we, wn, forcing, clon, clat, cvert, diag = [f[:, edge, :] for f in fields]
        p_in, wn_in, clat_in = [fields[i][:, inner, :] for i in (0, 2, 5)]
        cosine = one_cos(face, lat_total)
        east = lane < width - 1
        w_east = jnp.where(east, 0.5 * (clon + pltpu.roll(clon, width - 1, 1)), 0.0)
        h_east = jnp.where(
            east,
            w_east * (pltpu.roll(p, width - 1, 1) - p) - 0.5 * (we + pltpu.roll(we, width - 1, 1)),
            0.0,
        )
        w_in = metric(cosine) * (0.5 * (clat + clat_in))
        h_in = w_in * (p_in - p) - sign * (0.5 * cosine * (wn + wn_in))
        w_up = up_level(cvert)
        h_up = w_up * (up_level(p) - p)
        below = cvert * (p - down_level(p))
        total = diag + w_east + pltpu.roll(w_east, 1, 1) + w_in + cvert + w_up
        number = forcing - diag * p + h_east - pltpu.roll(h_east, 1, 1) + h_in + h_up - below
        ends = jnp.where(lane == 1, pltpu.roll(we, 1, 1), clon)
        ends = jnp.where(lane == width - 2, pltpu.roll(we, width - 1, 1), ends)
        return jnp.concatenate((p, wn, clat, total, number, ends), 0)

    start = lat * rows
    south = message(low, 0, 1, start + 1, 1.0)
    north = message(high, 7, 6, start + rows - 1, -1.0)
    even = lat % 2 == 0
    near_ref[...] = jnp.where(even, north, south)
    far_ref[...] = jnp.where(even, south, north)


def rows_call(lat_total, fields):
    lev, rows, width = fields[0].shape
    low = pl.BlockSpec((lev, 8, width), lambda i: (0, 0, 0))
    high = pl.BlockSpec((lev, 8, width), lambda i: (0, rows // 8 - 1, 0))
    shape = jax.ShapeDtypeStruct((ROW_FIELDS * lev, width), F32)
    pinned = [pltpu.with_memory_space_constraint(f, pltpu.HBM) for f in fields]
    out = pl.BlockSpec(memory_space=pltpu.VMEM)
    return pl.pallas_call(
        lambda *refs: rows_kernel(lat_total, rows, *refs),
        grid=(1,),
        in_specs=[low] * 8 + [high] * 8,
        out_specs=[out, out],
        out_shape=[shape, shape],
        compiler_params=pltpu.CompilerParams(vmem_limit_bytes=SMALL_VMEM),
        name="row_messages",
    )(*pinned, *pinned)


CHUNKS = 3
PAD = 8
BLOCK = 48
VMEM_LIMIT = 24 * 2**20


def window_mask(lane, index):
    return lane // 4 == index


def window_row(index, offset):
    return 4 * index + offset


def merged(ref, level, row, count, lane):
    at = pl.ds(row, count)
    return jnp.where(lane < LANES // 2, ref[level, at, 0:LANES], ref[level, at, LANES : 2 * LANES])


def window_move(x, index):
    return pltpu.roll(x, (4 * index + 2) % LANES, 1)


def edge_kernel(lat_total, rows, *refs):
    p_ref, we_ref, wn_ref, f_ref, clon_ref, clat_ref, cv_ref, diag_ref = refs[:8]
    cols_ref, *planes = refs[8:12]
    pm, wnm, clatm, pack, packed, cosines, sems = refs[12:]
    moves = [
        pltpu.make_async_copy(
            ref.at[:, :, pl.ds(t * LANES, LANES)],
            plane.at[t, :, pl.ds(PAD, rows), :],
            sems.at[i, t],
        )
        for i, (ref, plane) in enumerate(zip((p_ref, wn_ref, clat_ref), planes))
        for t in range(2)
    ]
    for move in moves:
        move.start()
    start = lax.axis_index("lat") * rows
    cosines[...] = face_cos(start, cosines.shape, 0, lat_total)
    shape = (BLOCK, LANES)
    lane = lax.broadcasted_iota(jnp.int32, shape, 1)

    def gather(r, carry):
        row = pl.multiple_of(r * BLOCK, BLOCK)
        for ref, buf in ((p_ref, pm), (wn_ref, wnm), (clat_ref, clatm)):
            for k in range(4):
                buf[k, pl.ds(row + PAD, BLOCK), :] = merged(ref, k, row, BLOCK, lane)
        return carry

    lax.fori_loop(0, rows // BLOCK, gather, 0)
    for buf, sign in ((pm, 1.0), (wnm, -1.0), (clatm, -1.0)):
        for k in range(4):
            for inside, outside in ((PAD, PAD - 1), (PAD + rows - 1, PAD + rows)):
                buf[k, outside : outside + 1, :] = sign * buf[k, inside : inside + 1, :]
    pack[pl.ds(rows, 256 - rows), :] = jnp.zeros((256 - rows, LANES), F32)

    def step(r, carry):
        row = pl.multiple_of(r * BLOCK, BLOCK)
        c_s, c_n = cosines[pl.ds(row, BLOCK), :], cosines[pl.ds(row + 1, BLOCK), :]
        m_s, m_n = metric(c_s), metric(c_n)
        acc = [jnp.zeros(shape, F32) for _ in range(4)]
        for k in range(4):

            def get(buf, shift=0, level=k):
                return buf[level, pl.ds(row + PAD + shift, BLOCK), :]

            def raw(ref, level=k):
                return merged(ref, level, row, BLOCK, lane)

            p, clat, wn = get(pm), get(clatm), get(wnm)
            below, diag = raw(cv_ref) if k == 0 else above, raw(diag_ref)
            w_n, w_s = m_n * (clat + get(clatm, 1)), m_s * (clat + get(clatm, -1))
            flux = w_n * (get(pm, 1) - p) + w_s * (get(pm, -1) - p)
            flux += c_s * (wn + get(wnm, -1)) - c_n * (wn + get(wnm, 1))
            total = diag + below
            number = raw(f_ref) - diag * p - (below * p if k == 0 else lifted)
            if k < 3:
                above = raw(cv_ref, k + 1)
                lifted = above * (get(pm, 0, k + 1) - p)
                total += above
                number += lifted
            total += 0.5 * (w_n + w_s)
            number += 0.5 * flux
            for i, x in enumerate((p, raw(we_ref), raw(clon_ref), total, number)):
                index = i * 4 + k
                acc[k] = jnp.where(window_mask(lane, index), window_move(x, index), acc[k])
        pack[pl.ds(row, BLOCK), :] = (acc[0] + acc[1]) + (acc[2] + acc[3])
        return carry

    lax.fori_loop(0, rows // BLOCK, step, 0)
    packed[...] = pack[...].T

    def column(field, offset):
        return jnp.concatenate(
            [packed[pl.ds(window_row(field * 4 + k, offset), 1), :] for k in range(4)], 0
        )

    for side, (edge, inner, sign) in enumerate(((2, 3, 1.0), (1, 0, -1.0))):
        p, we, clon, total, number = [column(i, edge) for i in range(COL_FIELDS)]
        p_in, we_in, clon_in = [column(i, inner) for i in range(3)]
        w = 0.5 * (clon + clon_in)
        number = number + w * (p_in - p) - sign * (0.5 * (we + we_in))
        for i, x in enumerate((p, we, clon, total + w, number)):
            cols_ref[pl.ds((side * COL_FIELDS + i) * 4, 4), :] = x
    for move in moves:
        move.wait()


def edge_call(lat_total, fields):
    lev, rows, width = fields[0].shape
    cols = jax.ShapeDtypeStruct((2 * COL_FIELDS * lev, 256), F32)
    vmem = pl.BlockSpec(memory_space=pltpu.VMEM)
    return pl.pallas_call(
        lambda *refs: edge_kernel(lat_total, rows, *refs),
        in_specs=[vmem] * 8,
        out_specs=[vmem] * 4,
        out_shape=[cols] + [jax.ShapeDtypeStruct((2, lev, rows + 2 * PAD, LANES), F32)] * 3,
        scratch_shapes=[pltpu.VMEM((lev, rows + 2 * PAD, LANES), F32)] * 3
        + [
            pltpu.VMEM((256, LANES), F32),
            pltpu.VMEM((LANES, 256), F32),
            pltpu.VMEM((rows + 8, LANES), F32),
            pltpu.SemaphoreType.DMA((3, 2)),
        ],
        compiler_params=pltpu.CompilerParams(vmem_limit_bytes=VMEM_LIMIT),
        cost_estimate=pl.CostEstimate(flops=10_000_000, bytes_accessed=8_000_000, transcendentals=0),
        name="edge_columns",
    )(*fields)


def edge_rows(own, halo, cosine, low):
    w = metric(cosine) * (0.5 * (own[8:12] + halo[8:12]))
    g = 0.5 * cosine * (own[4:8] + halo[4:8])
    f = w * (own[0:4] - halo[0:4]) if low else w * (halo[0:4] - own[0:4])
    return w, f, g


def pick(even, near, far):
    return jnp.where(even, far, near), jnp.where(even, near, far)


def columns_kernel(lat_total, rows, cols, far, near, far_in, near_in, _, west_ref, east_ref, sent_ref):
    lat = lax.axis_index("lat")
    even = lat % 2 == 0
    own_s, own_n = pick(even, near[...], far[...])
    halo_s, halo_n = pick(even, near_in[...], far_in[...])
    w_s, f_s, g_s = edge_rows(own_s, halo_s, one_cos(lat * rows, lat_total), True)
    w_n, f_n, g_n = edge_rows(own_n, halo_n, one_cos((lat + 1) * rows, lat_total), False)
    h_s, h_n = f_s - g_s, f_n - g_n
    width = w_s.shape[-1]
    lane = lax.broadcasted_iota(jnp.int32, (4, width), 1)

    def side(at):
        source, inner = (0, 1) if at == 0 else (width - 1, width - 2)
        base = at * COL_FIELDS * 4
        p, we, clon, total, number = [cols[pl.ds(base + i * 4, 4), :] for i in range(COL_FIELDS)]

        def put(x, value, target, source=source):
            return jnp.where(lane == target, pltpu.roll(value, (target - source) % width, 1), x)

        no = jnp.zeros_like(p)
        total = total + put(put(no, w_s, 0), w_n, rows - 1)
        number = number + put(put(no, -h_s, 0), h_n, rows - 1)
        p = put(put(p, halo_s[0:4], rows), halo_n[0:4], rows + 1)
        clon = put(put(clon, halo_s[20:24], rows), halo_n[20:24], rows + 1)
        we = put(put(we, halo_s[20:24], rows, inner), halo_n[20:24], rows + 1, inner)
        return jnp.concatenate((p, we, clon, total, number), 0)

    west_ref[...] = side(0)
    east = side(1)
    east_ref[...] = east
    sent_ref[...] = east


def columns_call(lat_total, rows, cols, far, near, far_in, near_in, after):
    shape = jax.ShapeDtypeStruct((cols.shape[0] // 2, cols.shape[1]), F32)
    vmem = pl.BlockSpec(memory_space=pltpu.VMEM)
    return pl.pallas_call(
        lambda *refs: columns_kernel(lat_total, rows, *refs),
        in_specs=[vmem] * 6,
        out_specs=[vmem] * 3,
        out_shape=[shape] * 3,
        compiler_params=pltpu.CompilerParams(vmem_limit_bytes=SMALL_VMEM),
        name="column_messages",
    )(cols, far, near, far_in, near_in, after)


def roll_west(tiles, lane):
    a, b = [pltpu.roll(x, 1, 1) for x in tiles]
    return a, jnp.where(lane == 0, a, b)


def roll_east(tiles, lane):
    a, b = [pltpu.roll(x, LANES - 1, 1) for x in tiles]
    return jnp.where(lane == LANES - 1, b, a), b


EDGE_TERMS = 8
STATE = 5
FIRST_AHEAD = 3
OTHERS_AHEAD = 2
BETWEEN = (5, 3, 3, 1)


def place():
    return lax.rem(lax.axis_index("lon"), lax.axis_size("lon") // 2)


def shares(blocks):
    here, lat, last = place(), lax.axis_index("lat"), lax.axis_size("lat") - 1
    slow = (lat == 0) | (lat == last) | (lat == last // 2)
    ahead = jnp.where(slow, OTHERS_AHEAD, 0)
    ahead = jnp.where((here == 0) & (lat != 1), FIRST_AHEAD, jnp.where(here == 0, OTHERS_AHEAD, ahead))
    between = ahead
    for at, count in enumerate(BETWEEN):
        between = jnp.where(here == at, jnp.maximum(count, ahead), between)
    between = jnp.where(here == 1, ahead + BETWEEN[1], between)
    return jnp.minimum(ahead, blocks), jnp.minimum(between, blocks)


def late_residual():
    return (place() > 0) | (lax.axis_index("lat") == 1)


def interior_ahead(lat_total, rows, *refs):
    ahead, _ = shares(rows // BLOCK)

    @pl.when(ahead > 0)
    def _():
        correction(lat_total, rows, refs[:8], refs[8:11], refs[11:15], refs[15:], 0, ahead)


def interior_between(lat_total, rows, *refs):
    fields, messages, planes, refs = refs[:8], refs[8:12], refs[12:14], refs[14 + STATE + 1 :]
    state, (_, terms_ref, res_ref), scratch = refs[:STATE], refs[STATE : STATE + 3], refs[STATE + 3 :]
    ahead, between = shares(rows // BLOCK)

    @pl.when(between > ahead)
    def _():
        here = (*planes, state[4])
        correction(lat_total, rows, fields, here, state[:4], scratch, ahead, between)

    @pl.when(place() == 0)
    def _():
        edges(lat_total, rows, fields[4:7], messages, state, terms_ref, scratch)

    @pl.when(jnp.logical_not(late_residual()))
    def _():
        residual(lat_total, rows, fields[6], state, res_ref, scratch)


def interior(lat_total, rows, *refs):
    fields, messages, planes, refs = refs[:8], refs[8:12], refs[12:14], refs[14 + STATE + 2 + 1 :]
    state, terms_ref, res_ref, scratch = refs[:STATE], refs[STATE], refs[STATE + 1], refs[STATE + 2 :]
    _, between = shares(rows // BLOCK)

    @pl.when(place() > 0)
    def _():
        here = (*planes, state[4])
        correction(lat_total, rows, fields, here, state[:4], scratch, between, rows // BLOCK)
        edges(lat_total, rows, fields[4:7], messages, state, terms_ref, scratch)

    @pl.when(late_residual())
    def _():
        residual(lat_total, rows, fields[6], state, res_ref, scratch)


def quotient(x, y):
    guess = pl.reciprocal(y, approx=True)
    guess = guess * (2.0 - y * guess)
    return x * guess


def correction(lat_total, rows, fields, planes, outs, scratch, begin, end):
    _, we_ref, _, f_ref, clon_ref, _, cv_ref, diag_ref = fields
    pb, wnb, clatb = planes
    new_ref, delta, w_west, w_east = outs
    cosines = scratch[-1]
    cosines[...] = face_cos(lax.axis_index("lat") * rows, cosines.shape, 0, lat_total)
    shape = (BLOCK, LANES)
    lane = lax.broadcasted_iota(jnp.int32, shape, 1)
    edge = (lane == 0, lane == LANES - 1)
    tiles = [pl.ds(t * LANES, LANES) for t in range(2)]

    def first(r, carry):
        row = pl.multiple_of(r * BLOCK, BLOCK)
        c_s, c_n = cosines[pl.ds(row, BLOCK), :], cosines[pl.ds(row + 1, BLOCK), :]
        m_s, m_n = metric(c_s), metric(c_n)
        lifted = None
        for k in range(4):

            def get(buf, shift=0, level=k):
                return [buf[t, level, pl.ds(row + PAD + shift, BLOCK), :] for t in range(2)]

            def raw(ref, level=k):
                return [ref[level, pl.ds(row, BLOCK), tile] for tile in tiles]

            p, we, clon, clat, wn = get(pb), raw(we_ref), raw(clon_ref), get(clatb), get(wnb)
            p_e, we_e, clon_e = [roll_east(x, lane) for x in (p, we, clon)]
            p_w, we_w, clon_w = [roll_west(x, lane) for x in (p, we, clon)]
            wn_s, wn_n, clat_s, clat_n = get(wnb, -1), get(wnb, 1), get(clatb, -1), get(clatb, 1)
            p_s, p_n = get(pb, -1), get(pb, 1)
            forcing, diag = raw(f_ref), raw(diag_ref)
            below = raw(cv_ref) if k == 0 else above
            if k < 3:
                above, p_a = raw(cv_ref, k + 1), get(pb, 0, k + 1)
            fallen, lifted = lifted, []
            for t in range(2):
                w_e, w_w = clon[t] + clon_e[t], clon[t] + clon_w[t]
                w_n, w_s = m_n * (clat[t] + clat_n[t]), m_s * (clat[t] + clat_s[t])
                flux = w_e * (p_e[t] - p[t]) + w_w * (p_w[t] - p[t]) - (we_e[t] - we_w[t])
                flux += w_n * (p_n[t] - p[t]) + w_s * (p_s[t] - p[t])
                flux += c_s * (wn[t] + wn_s[t]) - c_n * (wn[t] + wn_n[t])
                weight = (w_e + w_w) + (w_n + w_s)
                total = diag[t] + below[t]
                number = forcing[t] - diag[t] * p[t] - (below[t] * p[t] if k == 0 else fallen[t])
                if k < 3:
                    lifted.append(above[t] * (p_a[t] - p[t]))
                    total += above[t]
                    number += lifted[t]
                d = quotient(number + 0.5 * flux, total + 0.5 * weight)
                d = jnp.where(edge[t], 0.0, d)
                at = pl.ds(row, BLOCK)
                delta[t, k, pl.ds(row + PAD, BLOCK), :] = d
                new_ref[t, k, at, :] = p[t] + d
                w_west[t, k, at, :] = jnp.where(edge[0], 0.0, w_w) if t == 0 else w_w
                w_east[t, k, at, :] = jnp.where(edge[1], 0.0, w_e) if t == 1 else w_e
        return carry

    lax.fori_loop(begin, end, first, 0)


def edges(lat_total, rows, coefs, messages, state, terms_ref, scratch):
    clon_ref, clat_ref, cv_ref = coefs
    far, near, far_in, near_in = [m[...] for m in messages]
    new_ref, delta, _, _, clatb = state
    pack, packed, _ = scratch
    lat = lax.axis_index("lat")
    width = 2 * LANES
    wide = lax.broadcasted_iota(jnp.int32, (4, width), 1)
    inside = (wide > 0) & (wide < width - 1)
    even = lat % 2 == 0
    own_s, own_n = pick(even, near, far)
    halo_s, halo_n = pick(even, near_in, far_in)
    w_s, f_s, g_s = edge_rows(own_s, halo_s, one_cos(lat * rows, lat_total), True)
    w_n, f_n, g_n = edge_rows(own_n, halo_n, one_cos((lat + 1) * rows, lat_total), False)
    into_s = f_s - jnp.where(lat == 0, -g_s, g_s)
    into_n = jnp.where(lat == lax.axis_size("lat") - 1, -g_n, g_n) - f_n

    def put_rows(buf, at, value):
        for t in range(2):
            for k in range(4):
                buf[t, k, at : at + 1, :] = value[k : k + 1, t * LANES : (t + 1) * LANES]

    corners = []
    for own, halo, w, into, flux, at, beyond in (
        (own_s, halo_s, w_s, into_s, g_s - f_s, 0, -1),
        (own_n, halo_n, w_n, into_n, f_n - g_n, rows - 1, rows),
    ):
        halo_number, halo_total = halo[16:20] + into, halo[12:16] + w
        d_own = jnp.where(inside, (own[16:20] + flux) / (own[12:16] + w), 0.0)
        put_rows(new_ref, at, own[0:4] + d_own)
        put_rows(delta, PAD + at, d_own)
        put_rows(delta, PAD + beyond, jnp.where(inside, halo_number / halo_total, 0.0))
        put_rows(clatb, PAD + beyond, halo[8:12])
        corners.append((w, halo_number, halo_total, at))
    pack[pl.ds(rows, 256 - rows), :] = jnp.zeros((256 - rows, LANES), F32)
    shape = (BLOCK, LANES)
    lane = lax.broadcasted_iota(jnp.int32, shape, 1)
    tiles = [pl.ds(t * LANES, LANES) for t in range(2)]

    def gather(r, carry):
        row = pl.multiple_of(r * BLOCK, BLOCK)
        acc = [jnp.zeros(shape, F32) for _ in range(4)]
        for k in range(4):
            for i, ref in enumerate((clon_ref, clat_ref, cv_ref)):
                index = i * 4 + k
                both = merged(ref, k, row, BLOCK, lane)
                acc[k] = jnp.where(window_mask(lane, index), window_move(both, index), acc[k])
        pack[pl.ds(row, BLOCK), :] = (acc[0] + acc[1]) + (acc[2] + acc[3])
        return carry

    lax.fori_loop(0, rows // BLOCK, gather, 0)
    packed[...] = pack[...].T
    m_s = metric(face_cos(lat * rows, (4, width), 1, lat_total))
    m_n = metric(face_cos(lat * rows + 1, (4, width), 1, lat_total))

    def column(field, offset):
        return jnp.concatenate(
            [packed[pl.ds(window_row(field * 4 + k, offset), 1), :] for k in range(4)], 0
        )

    for side, (edge, inner, source) in enumerate(((2, 3, 0), (1, 0, width - 1))):
        clon, clat, below = [column(i, edge) for i in range(3)]
        ends = [jnp.zeros((4, width), F32), jnp.zeros((4, width), F32), jnp.ones((4, width), F32)]
        for *values, at in corners:
            for i, value in enumerate(values):
                ends[i] = jnp.where(wide == at, pltpu.roll(value, (at - source) % width, 1), ends[i])
        terms = (
            0.5 * m_n * (clat + pltpu.roll(clat, width - 1, 1)),
            0.5 * m_s * (clat + pltpu.roll(clat, 1, 1)),
            0.5 * (clon + column(0, inner)),
            up_level(below),
            below,
            *ends,
        )
        for i, term in enumerate(terms):
            terms_ref[pl.ds((side * EDGE_TERMS + i) * 4, 4), :] = term


def residual(lat_total, rows, cv_ref, state, res_ref, scratch):
    _, delta, w_west, w_east, clatb = state
    cosines = scratch[-1]
    cosines[...] = face_cos(lax.axis_index("lat") * rows, cosines.shape, 0, lat_total)
    lane = lax.broadcasted_iota(jnp.int32, (BLOCK, LANES), 1)
    tiles = [pl.ds(t * LANES, LANES) for t in range(2)]

    def second(r, carry):
        row = pl.multiple_of(r * BLOCK, BLOCK)
        at = pl.ds(row, BLOCK)
        m_s, m_n = metric(cosines[at, :]), metric(cosines[pl.ds(row + 1, BLOCK), :])
        for k in range(4):

            def get(buf, shift=0, level=k):
                return [buf[t, level, pl.ds(row + PAD + shift, BLOCK), :] for t in range(2)]

            d, d_s, d_n = get(delta), get(delta, -1), get(delta, 1)
            clat, clat_s, clat_n = get(clatb), get(clatb, -1), get(clatb, 1)
            d_w, d_e = roll_west(d, lane), roll_east(d, lane)
            for t in range(2):
                x_w, x_e = w_west[t, k, at, :] * d_w[t], w_east[t, k, at, :] * d_e[t]
                y = m_n * (clat[t] + clat_n[t]) * d_n[t] + m_s * (clat[t] + clat_s[t]) * d_s[t]
                out = 0.5 * ((x_w + x_e) + y)
                if k > 0:
                    out += cv_ref[k, at, tiles[t]] * get(delta, 0, k - 1)[t]
                if k < 3:
                    out += cv_ref[k + 1, at, tiles[t]] * get(delta, 0, k + 1)[t]
                res_ref[t, k, at, :] = out
        return carry

    lax.fori_loop(0, rows // BLOCK, second, 0)


def interior_call(lat_total, shape, kernel, inputs, kept, after, results):
    lev, rows, width = shape
    tiles = width // LANES
    vmem = pl.BlockSpec(memory_space=pltpu.VMEM)
    shapes = {
        "plane": (tiles, lev, rows, LANES),
        "padded": (tiles, lev, rows + 2 * PAD, LANES),
        "message": (COL_FIELDS * lev, 256),
        "terms": (2 * EDGE_TERMS * lev, 256),
    }
    operands = (*inputs, *kept, *after)
    return pl.pallas_call(
        lambda *refs: kernel(lat_total, rows, *refs),
        in_specs=[vmem] * len(operands),
        out_specs=[vmem] * len(results),
        out_shape=[jax.ShapeDtypeStruct(shapes[name], F32) for name in results],
        scratch_shapes=[
            pltpu.VMEM((256, LANES), F32),
            pltpu.VMEM((LANES, 256), F32),
            pltpu.VMEM((rows + 8, LANES), F32),
        ],
        input_output_aliases={len(inputs) + i: i for i in range(len(kept))},
        compiler_params=pltpu.CompilerParams(vmem_limit_bytes=VMEM_LIMIT),
        cost_estimate=pl.CostEstimate(flops=20_000_000, bytes_accessed=16_000_000, transcendentals=0),
        name=kernel.__name__,
    )(*operands)


def final_kernel(rows, *refs):
    new_in, res_in, terms, own_w, own_e, halo_w, halo_e = refs[:7]
    new_hbm, res_hbm, new_buf, res_buf, stack, colv, sems = refs[7:]
    width = 2 * LANES
    wide = lax.broadcasted_iota(jnp.int32, (4, width), 1)
    low, high, inside = wide == 0, wide == rows - 1, wide < rows
    own, halo = (own_w, own_e), (halo_w, halo_e)

    def ends(x):
        south, north = pltpu.roll(x, width - rows, 1), pltpu.roll(x, width - 2, 1)
        return jnp.where(low, south, jnp.where(high, north, 0.0))

    for side, (edge, inner, sign) in enumerate(((2, 3, 1.0), (1, 0, -1.0))):
        o_p, o_we, o_clon, o_total, o_number = [own[side][pl.ds(4 * i, 4), :] for i in range(5)]
        h_p, h_we, h_clon, h_total, h_number = [halo[side][pl.ds(4 * i, 4), :] for i in range(5)]
        a_n, a_s, w_in, above, below, c_w, c_number, c_total = [
            terms[pl.ds((side * EDGE_TERMS + i) * 4, 4), :] for i in range(EDGE_TERMS)
        ]
        w = 0.5 * (o_clon + h_clon)
        h = w * (o_p - h_p) - sign * (0.5 * (o_we + h_we))
        d = jnp.where(inside, (o_number - h) / (o_total + w), 0.0)
        beyond = jnp.where(inside, w * ((h_number + h) / (h_total + w)), 0.0)
        corner = c_w * ((c_number - ends(h)) / (c_total + ends(w)))
        at_edge = a_n * pltpu.roll(d, width - 1, 1) + a_s * pltpu.roll(d, 1, 1)
        at_edge += above * up_level(d) + below * down_level(d) + (beyond + corner)
        for first, x in ((edge, at_edge), (inner, w_in * d), (16 + edge, d)):
            for t in range(2):
                stack[t, pl.ds(first, 4, stride=4), :] = x[:, t * LANES : (t + 1) * LANES]
    for t in range(2):
        colv[pl.ds(t * LANES, LANES), :] = stack[t].T

    per = rows // CHUNKS
    lane = lax.broadcasted_iota(jnp.int32, (per, LANES), 1)
    edges = (lane < 2, lane >= LANES - 2)
    edge = (lane == 0, lane == LANES - 1)

    def sends(chunk):
        return [
            pltpu.make_async_copy(
                buf.at[:, pl.ds(chunk * per, per), :],
                out.at[:, pl.ds(chunk * per, per), :],
                sems.at[chunk, i],
            )
            for i, (buf, out) in enumerate(((new_buf, new_hbm), (res_buf, res_hbm)))
        ]

    for chunk in range(CHUNKS):
        at = pl.ds(chunk * per, per)
        packed = colv[at, :]
        for k in range(4):
            to_res = pltpu.roll(packed, (-4 * k - 2) % LANES, 1)
            to_new = pltpu.roll(packed, (-4 * (4 + k) - 2) % LANES, 1)
            for t in range(2):
                tile = pl.ds(t * LANES, LANES)
                res_buf[k, at, tile] = res_in[t, k, at, :] + jnp.where(edges[t], to_res, 0.0)
                new_buf[k, at, tile] = new_in[t, k, at, :] + jnp.where(edge[t], to_new, 0.0)
        for copy in sends(chunk):
            copy.start()
    for chunk in range(CHUNKS):
        for copy in sends(chunk):
            copy.wait()


def final_call(shape, planes, messages):
    lev, rows, width = shape
    hbm, vmem = pl.BlockSpec(memory_space=pl.ANY), pl.BlockSpec(memory_space=pltpu.VMEM)
    out = jax.ShapeDtypeStruct(shape, F32)
    return pl.pallas_call(
        lambda *refs: final_kernel(rows, *refs),
        in_specs=[vmem] * 7,
        out_specs=[hbm, hbm],
        out_shape=[out, out],
        scratch_shapes=[pltpu.VMEM(shape, F32)] * 2
        + [
            pltpu.VMEM((2, LANES, LANES), F32),
            pltpu.VMEM((256, LANES), F32),
            pltpu.SemaphoreType.DMA((CHUNKS, 2)),
        ],
        compiler_params=pltpu.CompilerParams(vmem_limit_bytes=VMEM_LIMIT),
        name="edges_and_store",
    )(*planes, *messages)


def per_device(pressure, wind_east, wind_north, forcing, coef_lon, coef_lat, coef_vert, diag_coef):
    fields = (pressure, wind_east, wind_north, forcing, coef_lon, coef_lat, coef_vert, diag_coef)
    rows = pressure.shape[1]
    lat_total = rows * lax.axis_size("lat")
    rows_near, rows_far, eastward, westward = exchange_pairs(
        lax.axis_size("lon"), lax.axis_size("lat")
    )
    near, far = rows_call(lat_total, fields)
    far_in = lax.ppermute(far, AXES, rows_far)
    near_in = lax.ppermute(near, AXES, rows_near)
    cols, p_planes, wn_planes, clat_planes = edge_call(lat_total, fields)
    row_messages = (far, near, far_in, near_in)
    shape = pressure.shape
    planes = (p_planes, wn_planes, clat_planes)
    kinds = ("plane", "padded", "plane", "plane", "padded")
    state = interior_call(
        lat_total, shape, interior_ahead, (*fields, *planes), (), (), kinds[:-1]
    )
    west, east, sent = columns_call(lat_total, rows, cols, *row_messages, state[0])
    from_west = lax.ppermute(sent, AXES, eastward)
    *state, west, terms, residual_part = interior_call(
        lat_total,
        shape,
        interior_between,
        (*fields, *row_messages, *planes[:2]),
        (*state, clat_planes, west),
        (),
        (*kinds, "message", "terms", "plane"),
    )
    from_east = lax.ppermute(west, AXES, westward)
    new_pressure, *_, terms, residual_part = interior_call(
        lat_total,
        shape,
        interior,
        (*fields, *row_messages, *planes[:2]),
        (*state, terms, residual_part),
        (west,),
        (*kinds, "terms", "plane"),
    )
    col_messages = (west, east, from_west, from_east)
    return final_call(shape, (new_pressure, residual_part, terms), col_messages)


def solution(mesh):
    spec = P(None, "lat", "lon")
    return jax.shard_map(
        per_device, mesh=mesh, in_specs=(spec,) * 8, out_specs=(spec, spec), check_vma=False
    )
```

```python
import math

import jax
import jax.numpy as jnp
from jax import lax
from jax.experimental import pallas as pl
from jax.experimental.pallas import tpu as pltpu
from jax.sharding import PartitionSpec as P

F32 = jnp.float32
AXES = ("lon", "lat")
LANES = 128
ROW_FIELDS = 6
COL_FIELDS = 5


def exchange_pairs(lon_count, lat_count):
    def flat(lon, lat):
        return (lon % lon_count) * lat_count + lat

    rows_near, rows_far, eastward, westward = [], [], [], []
    for lon in range(lon_count):
        for lat in range(lat_count):
            me = flat(lon, lat)
            rows_near.append((me, flat(lon, lat ^ 1)))
            if lat in (0, lat_count - 1):
                rows_far.append((me, flat(lon + lon_count // 2, lat)))
            else:
                rows_far.append((me, flat(lon, lat + 1 if lat % 2 else lat - 1)))
            eastward.append((me, flat(lon + 1, lat)))
            westward.append((me, flat(lon - 1, lat)))
    return rows_near, rows_far, eastward, westward


def face_cos(first, shape, axis, lat_total):
    position = (first + lax.broadcasted_iota(jnp.int32, shape, axis)).astype(F32)
    angle = position * (math.pi / lat_total) - math.pi / 2
    square = angle * angle
    cosine = jnp.full(shape, 1.0 / math.factorial(16), F32)
    for power in range(14, -1, -2):
        cosine = (-1.0) ** (power // 2) / math.factorial(power) + square * cosine
    return cosine


def metric(cosine):
    return 0.5 * (1.0 + jnp.abs(cosine))


def up_level(x):
    return jnp.concatenate((x[1:], jnp.zeros_like(x[:1])), 0)


def down_level(x):
    return jnp.concatenate((jnp.zeros_like(x[:1]), x[:-1]), 0)


def one_cos(row, lat_total):
    return face_cos(row, (1, 2 * LANES), 0, lat_total)


SMALL_VMEM = 4 * 2**20


def rows_kernel(lat_total, rows, *refs):
    low, high, (near_ref, far_ref) = refs[:8], refs[8:16], refs[16:]
    lat = lax.axis_index("lat")
    width = near_ref.shape[-1]
    lane = lax.broadcasted_iota(jnp.int32, (4, width), 1)

    def message(fields, edge, inner, face, sign):
        p, we, wn, forcing, clon, clat, cvert, diag = [f[:, edge, :] for f in fields]
        p_in, wn_in, clat_in = [fields[i][:, inner, :] for i in (0, 2, 5)]
        cosine = one_cos(face, lat_total)
        east = lane < width - 1
        w_east = jnp.where(east, 0.5 * (clon + pltpu.roll(clon, width - 1, 1)), 0.0)
        h_east = jnp.where(
            east,
            w_east * (pltpu.roll(p, width - 1, 1) - p) - 0.5 * (we + pltpu.roll(we, width - 1, 1)),
            0.0,
        )
        w_in = metric(cosine) * (0.5 * (clat + clat_in))
        h_in = w_in * (p_in - p) - sign * (0.5 * cosine * (wn + wn_in))
        w_up = up_level(cvert)
        h_up = w_up * (up_level(p) - p)
        below = cvert * (p - down_level(p))
        west = lane > 0
        clon_w, p_w, we_w = [pltpu.roll(x, 1, 1) for x in (clon, p, we)]
        w_west = jnp.where(west, 0.5 * (clon + clon_w), 0.0)
        h_west = jnp.where(west, w_west * (p - p_w) - 0.5 * (we_w + we), 0.0)
        total = diag + w_east + w_west + w_in + cvert + w_up
        number = forcing - diag * p + h_east - h_west + h_in + h_up - below
        ends = jnp.where(lane == 1, pltpu.roll(we, 1, 1), clon)
        ends = jnp.where(lane == width - 2, pltpu.roll(we, width - 1, 1), ends)
        return jnp.concatenate((p, wn, clat, total, number, ends), 0)

    start = lat * rows
    south = message(low, 0, 1, start + 1, 1.0)
    north = message(high, 7, 6, start + rows - 1, -1.0)
    even = lat % 2 == 0
    near_ref[...] = jnp.where(even, north, south)
    far_ref[...] = jnp.where(even, south, north)


def rows_call(lat_total, fields):
    lev, rows, width = fields[0].shape
    low = pl.BlockSpec((lev, 8, width), lambda i: (0, 0, 0))
    high = pl.BlockSpec((lev, 8, width), lambda i: (0, rows // 8 - 1, 0))
    shape = jax.ShapeDtypeStruct((ROW_FIELDS * lev, width), F32)
    pinned = [pltpu.with_memory_space_constraint(f, pltpu.HBM) for f in fields]
    out = pl.BlockSpec(memory_space=pltpu.VMEM)
    return pl.pallas_call(
        lambda *refs: rows_kernel(lat_total, rows, *refs),
        grid=(1,),
        in_specs=[low] * 8 + [high] * 8,
        out_specs=[out, out],
        out_shape=[shape, shape],
        compiler_params=pltpu.CompilerParams(vmem_limit_bytes=SMALL_VMEM),
        name="row_messages",
    )(*pinned, *pinned)


CHUNKS = 3
PAD = 8
BLOCK = 48
VMEM_LIMIT = 24 * 2**20


def window_mask(lane, index):
    return lane // 4 == index


def window_row(index, offset):
    return 4 * index + offset


def merged(ref, level, row, count, lane):
    at = pl.ds(row, count)
    return jnp.where(lane < LANES // 2, ref[level, at, 0:LANES], ref[level, at, LANES : 2 * LANES])


def window_move(x, index):
    return pltpu.roll(x, (4 * index + 2) % LANES, 1)


def edge_kernel(lat_total, rows, *refs):
    p_ref, we_ref, wn_ref, f_ref, clon_ref, clat_ref, cv_ref, diag_ref = refs[:8]
    cols_ref, *planes = refs[8:12]
    pm, wnm, clatm, pack, packed, cosines, sems = refs[12:]
    moves = [
        pltpu.make_async_copy(
            ref.at[:, :, pl.ds(t * LANES, LANES)],
            plane.at[t, :, pl.ds(PAD, rows), :],
            sems.at[i, t],
        )
        for i, (ref, plane) in enumerate(zip((p_ref, wn_ref, clat_ref), planes))
        for t in range(2)
    ]
    for move in moves:
        move.start()
    start = lax.axis_index("lat") * rows
    cosines[...] = face_cos(start, cosines.shape, 0, lat_total)
    shape = (BLOCK, LANES)
    lane = lax.broadcasted_iota(jnp.int32, shape, 1)

    def gather(r, carry):
        row = pl.multiple_of(r * BLOCK, BLOCK)
        for ref, buf in ((p_ref, pm), (wn_ref, wnm), (clat_ref, clatm)):
            for k in range(4):
                buf[k, pl.ds(row + PAD, BLOCK), :] = merged(ref, k, row, BLOCK, lane)
        return carry

    lax.fori_loop(0, rows // BLOCK, gather, 0)
    for buf, sign in ((pm, 1.0), (wnm, -1.0), (clatm, -1.0)):
        for k in range(4):
            for inside, outside in ((PAD, PAD - 1), (PAD + rows - 1, PAD + rows)):
                buf[k, outside : outside + 1, :] = sign * buf[k, inside : inside + 1, :]
    pack[pl.ds(rows, 256 - rows), :] = jnp.zeros((256 - rows, LANES), F32)

    def step(r, carry):
        row = pl.multiple_of(r * BLOCK, BLOCK)
        c_s, c_n = cosines[pl.ds(row, BLOCK), :], cosines[pl.ds(row + 1, BLOCK), :]
        m_s, m_n = metric(c_s), metric(c_n)
        acc = [jnp.zeros(shape, F32) for _ in range(4)]
        for k in range(4):

            def get(buf, shift=0, level=k):
                return buf[level, pl.ds(row + PAD + shift, BLOCK), :]

            def raw(ref, level=k):
                return merged(ref, level, row, BLOCK, lane)

            p, clat, wn = get(pm), get(clatm), get(wnm)
            below, diag = raw(cv_ref) if k == 0 else above, raw(diag_ref)
            w_n, w_s = m_n * (clat + get(clatm, 1)), m_s * (clat + get(clatm, -1))
            flux = w_n * (get(pm, 1) - p) + w_s * (get(pm, -1) - p)
            flux += c_s * (wn + get(wnm, -1)) - c_n * (wn + get(wnm, 1))
            total = diag + below
            number = raw(f_ref) - diag * p - (below * p if k == 0 else lifted)
            if k < 3:
                above = raw(cv_ref, k + 1)
                lifted = above * (get(pm, 0, k + 1) - p)
                total += above
                number += lifted
            total += 0.5 * (w_n + w_s)
            number += 0.5 * flux
            for i, x in enumerate((p, raw(we_ref), raw(clon_ref), total, number)):
                index = i * 4 + k
                acc[k] = jnp.where(window_mask(lane, index), window_move(x, index), acc[k])
        pack[pl.ds(row, BLOCK), :] = (acc[0] + acc[1]) + (acc[2] + acc[3])
        return carry

    lax.fori_loop(0, rows // BLOCK, step, 0)
    packed[...] = pack[...].T

    def column(field, offset):
        return jnp.concatenate(
            [packed[pl.ds(window_row(field * 4 + k, offset), 1), :] for k in range(4)], 0
        )

    for side, (edge, inner, sign) in enumerate(((2, 3, 1.0), (1, 0, -1.0))):
        p, we, clon, total, number = [column(i, edge) for i in range(COL_FIELDS)]
        p_in, we_in, clon_in = [column(i, inner) for i in range(3)]
        w = 0.5 * (clon + clon_in)
        number = number + w * (p_in - p) - sign * (0.5 * (we + we_in))
        for i, x in enumerate((p, we, clon, total + w, number)):
            cols_ref[pl.ds((side * COL_FIELDS + i) * 4, 4), :] = x
    for move in moves:
        move.wait()


def edge_call(lat_total, fields):
    lev, rows, width = fields[0].shape
    cols = jax.ShapeDtypeStruct((2 * COL_FIELDS * lev, 256), F32)
    vmem = pl.BlockSpec(memory_space=pltpu.VMEM)
    return pl.pallas_call(
        lambda *refs: edge_kernel(lat_total, rows, *refs),
        in_specs=[vmem] * 8,
        out_specs=[vmem] * 4,
        out_shape=[cols] + [jax.ShapeDtypeStruct((2, lev, rows + 2 * PAD, LANES), F32)] * 3,
        scratch_shapes=[pltpu.VMEM((lev, rows + 2 * PAD, LANES), F32)] * 3
        + [
            pltpu.VMEM((256, LANES), F32),
            pltpu.VMEM((LANES, 256), F32),
            pltpu.VMEM((rows + 8, LANES), F32),
            pltpu.SemaphoreType.DMA((3, 2)),
        ],
        compiler_params=pltpu.CompilerParams(vmem_limit_bytes=VMEM_LIMIT),
        cost_estimate=pl.CostEstimate(flops=10_000_000, bytes_accessed=8_000_000, transcendentals=0),
        name="edge_columns",
    )(*fields)


def edge_rows(own, halo, cosine, low):
    w = metric(cosine) * (0.5 * (own[8:12] + halo[8:12]))
    g = 0.5 * cosine * (own[4:8] + halo[4:8])
    f = w * (own[0:4] - halo[0:4]) if low else w * (halo[0:4] - own[0:4])
    return w, f, g


def pick(even, near, far):
    return jnp.where(even, far, near), jnp.where(even, near, far)


def columns_kernel(lat_total, rows, cols, far, near, far_in, near_in, _, west_ref, east_ref, sent_ref):
    lat = lax.axis_index("lat")
    even = lat % 2 == 0
    own_s, own_n = pick(even, near[...], far[...])
    halo_s, halo_n = pick(even, near_in[...], far_in[...])
    w_s, f_s, g_s = edge_rows(own_s, halo_s, one_cos(lat * rows, lat_total), True)
    w_n, f_n, g_n = edge_rows(own_n, halo_n, one_cos((lat + 1) * rows, lat_total), False)
    h_s, h_n = f_s - g_s, f_n - g_n
    width = w_s.shape[-1]
    lane = lax.broadcasted_iota(jnp.int32, (4, width), 1)

    def side(at):
        source, inner = (0, 1) if at == 0 else (width - 1, width - 2)
        base = at * COL_FIELDS * 4
        p, we, clon, total, number = [cols[pl.ds(base + i * 4, 4), :] for i in range(COL_FIELDS)]

        def put(x, value, target, source=source):
            return jnp.where(lane == target, pltpu.roll(value, (target - source) % width, 1), x)

        no = jnp.zeros_like(p)
        total = total + put(put(no, w_s, 0), w_n, rows - 1)
        number = number + put(put(no, -h_s, 0), h_n, rows - 1)
        p = put(put(p, halo_s[0:4], rows), halo_n[0:4], rows + 1)
        clon = put(put(clon, halo_s[20:24], rows), halo_n[20:24], rows + 1)
        we = put(put(we, halo_s[20:24], rows, inner), halo_n[20:24], rows + 1, inner)
        return jnp.concatenate((p, we, clon, total, number), 0)

    west_ref[...] = side(0)
    east = side(1)
    east_ref[...] = east
    sent_ref[...] = east


def columns_call(lat_total, rows, cols, far, near, far_in, near_in, after):
    shape = jax.ShapeDtypeStruct((cols.shape[0] // 2, cols.shape[1]), F32)
    vmem = pl.BlockSpec(memory_space=pltpu.VMEM)
    return pl.pallas_call(
        lambda *refs: columns_kernel(lat_total, rows, *refs),
        in_specs=[vmem] * 6,
        out_specs=[vmem] * 3,
        out_shape=[shape] * 3,
        compiler_params=pltpu.CompilerParams(vmem_limit_bytes=SMALL_VMEM),
        name="column_messages",
    )(cols, far, near, far_in, near_in, after)


def roll_west(tiles, lane):
    a, b = [pltpu.roll(x, 1, 1) for x in tiles]
    return a, jnp.where(lane == 0, a, b)


def roll_east(tiles, lane):
    a, b = [pltpu.roll(x, LANES - 1, 1) for x in tiles]
    return jnp.where(lane == LANES - 1, b, a), b


EDGE_TERMS = 8
STATE = 5
FIRST_AHEAD = 3
OTHERS_AHEAD = 2
BETWEEN = (5, 3, 3, 1, 2, 1)


def place():
    return lax.rem(lax.axis_index("lon"), lax.axis_size("lon") // 2)


def shares(blocks):
    here, lat, last = place(), lax.axis_index("lat"), lax.axis_size("lat") - 1
    slow = (lat == 0) | (lat == last) | (lat == last // 2)
    ahead = jnp.where(slow, OTHERS_AHEAD, 0)
    ahead = jnp.where((here == 0) & (lat != 1), FIRST_AHEAD, jnp.where(here == 0, OTHERS_AHEAD, ahead))
    between = ahead
    for at, count in enumerate(BETWEEN):
        between = jnp.where(here == at, jnp.maximum(count, ahead), between)
    between = jnp.where(here == 1, ahead + BETWEEN[1], between)
    return jnp.minimum(ahead, blocks), jnp.minimum(between, blocks)


def late_residual():
    return (place() > 0) | (lax.axis_index("lat") == 1)


def interior_ahead(lat_total, rows, *refs):
    ahead, _ = shares(rows // BLOCK)

    @pl.when(ahead > 0)
    def _():
        correction(lat_total, rows, refs[:8], refs[8:11], refs[11:15], refs[15:], 0, ahead)


def interior_between(lat_total, rows, *refs):
    fields, messages, planes, refs = refs[:8], refs[8:12], refs[12:14], refs[14 + STATE + 1 :]
    state, (_, terms_ref, res_ref), scratch = refs[:STATE], refs[STATE : STATE + 3], refs[STATE + 3 :]
    ahead, between = shares(rows // BLOCK)

    @pl.when(between > ahead)
    def _():
        here = (*planes, state[4])
        correction(lat_total, rows, fields, here, state[:4], scratch, ahead, between)

    @pl.when(place() == 0)
    def _():
        edges(lat_total, rows, fields[4:7], messages, state, terms_ref, scratch)

    @pl.when(jnp.logical_not(late_residual()))
    def _():
        residual(lat_total, rows, fields[6], state, res_ref, scratch)


def interior(lat_total, rows, *refs):
    fields, messages, planes, refs = refs[:8], refs[8:12], refs[12:14], refs[14 + STATE + 2 + 1 :]
    state, terms_ref, res_ref, scratch = refs[:STATE], refs[STATE], refs[STATE + 1], refs[STATE + 2 :]
    _, between = shares(rows // BLOCK)

    @pl.when(place() > 0)
    def _():
        here = (*planes, state[4])
        correction(lat_total, rows, fields, here, state[:4], scratch, between, rows // BLOCK)
        edges(lat_total, rows, fields[4:7], messages, state, terms_ref, scratch)

    @pl.when(late_residual())
    def _():
        residual(lat_total, rows, fields[6], state, res_ref, scratch)


def quotient(x, y):
    guess = pl.reciprocal(y, approx=True)
    guess = guess * (2.0 - y * guess)
    return x * guess


def correction(lat_total, rows, fields, planes, outs, scratch, begin, end):
    _, we_ref, _, f_ref, clon_ref, _, cv_ref, diag_ref = fields
    pb, wnb, clatb = planes
    new_ref, delta, w_west, w_east = outs
    cosines = scratch[-1]
    cosines[...] = face_cos(lax.axis_index("lat") * rows, cosines.shape, 0, lat_total)
    shape = (BLOCK, LANES)
    lane = lax.broadcasted_iota(jnp.int32, shape, 1)
    edge = (lane == 0, lane == LANES - 1)
    tiles = [pl.ds(t * LANES, LANES) for t in range(2)]

    def first(r, carry):
        row = pl.multiple_of(r * BLOCK, BLOCK)
        c_s, c_n = cosines[pl.ds(row, BLOCK), :], cosines[pl.ds(row + 1, BLOCK), :]
        m_s, m_n = metric(c_s), metric(c_n)
        lifted = None
        for k in range(4):

            def get(buf, shift=0, level=k):
                return [buf[t, level, pl.ds(row + PAD + shift, BLOCK), :] for t in range(2)]

            def raw(ref, level=k):
                return [ref[level, pl.ds(row, BLOCK), tile] for tile in tiles]

            p, we, clon, clat, wn = get(pb), raw(we_ref), raw(clon_ref), get(clatb), get(wnb)
            p_e, we_e, clon_e = [roll_east(x, lane) for x in (p, we, clon)]
            p_w, we_w, clon_w = [roll_west(x, lane) for x in (p, we, clon)]
            wn_s, wn_n, clat_s, clat_n = get(wnb, -1), get(wnb, 1), get(clatb, -1), get(clatb, 1)
            p_s, p_n = get(pb, -1), get(pb, 1)
            forcing, diag = raw(f_ref), raw(diag_ref)
            below = raw(cv_ref) if k == 0 else above
            if k < 3:
                above, p_a = raw(cv_ref, k + 1), get(pb, 0, k + 1)
            fallen, lifted = lifted, []
            for t in range(2):
                w_e, w_w = clon[t] + clon_e[t], clon[t] + clon_w[t]
                w_n, w_s = m_n * (clat[t] + clat_n[t]), m_s * (clat[t] + clat_s[t])
                flux = w_e * (p_e[t] - p[t]) + w_w * (p_w[t] - p[t]) - (we_e[t] - we_w[t])
                flux += w_n * (p_n[t] - p[t]) + w_s * (p_s[t] - p[t])
                flux += c_s * (wn[t] + wn_s[t]) - c_n * (wn[t] + wn_n[t])
                weight = (w_e + w_w) + (w_n + w_s)
                total = diag[t] + below[t]
                number = forcing[t] - diag[t] * p[t] - (below[t] * p[t] if k == 0 else fallen[t])
                if k < 3:
                    lifted.append(above[t] * (p_a[t] - p[t]))
                    total += above[t]
                    number += lifted[t]
                d = quotient(number + 0.5 * flux, total + 0.5 * weight)
                d = jnp.where(edge[t], 0.0, d)
                at = pl.ds(row, BLOCK)
                delta[t, k, pl.ds(row + PAD, BLOCK), :] = d
                new_ref[t, k, at, :] = p[t] + d
                w_west[t, k, at, :] = jnp.where(edge[0], 0.0, w_w) if t == 0 else w_w
                w_east[t, k, at, :] = jnp.where(edge[1], 0.0, w_e) if t == 1 else w_e
        return carry

    lax.fori_loop(begin, end, first, 0)


def edges(lat_total, rows, coefs, messages, state, terms_ref, scratch):
    clon_ref, clat_ref, cv_ref = coefs
    far, near, far_in, near_in = [m[...] for m in messages]
    new_ref, delta, _, _, clatb = state
    pack, packed, _ = scratch
    lat = lax.axis_index("lat")
    width = 2 * LANES
    wide = lax.broadcasted_iota(jnp.int32, (4, width), 1)
    inside = (wide > 0) & (wide < width - 1)
    even = lat % 2 == 0
    own_s, own_n = pick(even, near, far)
    halo_s, halo_n = pick(even, near_in, far_in)
    w_s, f_s, g_s = edge_rows(own_s, halo_s, one_cos(lat * rows, lat_total), True)
    w_n, f_n, g_n = edge_rows(own_n, halo_n, one_cos((lat + 1) * rows, lat_total), False)
    into_s = f_s - jnp.where(lat == 0, -g_s, g_s)
    into_n = jnp.where(lat == lax.axis_size("lat") - 1, -g_n, g_n) - f_n

    def put_rows(buf, at, value):
        for t in range(2):
            for k in range(4):
                buf[t, k, at : at + 1, :] = value[k : k + 1, t * LANES : (t + 1) * LANES]

    corners = []
    for own, halo, w, into, flux, at, beyond in (
        (own_s, halo_s, w_s, into_s, g_s - f_s, 0, -1),
        (own_n, halo_n, w_n, into_n, f_n - g_n, rows - 1, rows),
    ):
        halo_number, halo_total = halo[16:20] + into, halo[12:16] + w
        d_own = jnp.where(inside, (own[16:20] + flux) / (own[12:16] + w), 0.0)
        put_rows(new_ref, at, own[0:4] + d_own)
        put_rows(delta, PAD + at, d_own)
        put_rows(delta, PAD + beyond, jnp.where(inside, halo_number / halo_total, 0.0))
        put_rows(clatb, PAD + beyond, halo[8:12])
        corners.append((w, halo_number, halo_total, at))
    pack[pl.ds(rows, 256 - rows), :] = jnp.zeros((256 - rows, LANES), F32)
    shape = (BLOCK, LANES)
    lane = lax.broadcasted_iota(jnp.int32, shape, 1)
    tiles = [pl.ds(t * LANES, LANES) for t in range(2)]

    def gather(r, carry):
        row = pl.multiple_of(r * BLOCK, BLOCK)
        acc = [jnp.zeros(shape, F32) for _ in range(4)]
        for k in range(4):
            for i, ref in enumerate((clon_ref, clat_ref, cv_ref)):
                index = i * 4 + k
                both = merged(ref, k, row, BLOCK, lane)
                acc[k] = jnp.where(window_mask(lane, index), window_move(both, index), acc[k])
        pack[pl.ds(row, BLOCK), :] = (acc[0] + acc[1]) + (acc[2] + acc[3])
        return carry

    lax.fori_loop(0, rows // BLOCK, gather, 0)
    packed[...] = pack[...].T
    m_s = metric(face_cos(lat * rows, (4, width), 1, lat_total))
    m_n = metric(face_cos(lat * rows + 1, (4, width), 1, lat_total))

    def column(field, offset):
        return jnp.concatenate(
            [packed[pl.ds(window_row(field * 4 + k, offset), 1), :] for k in range(4)], 0
        )

    for side, (edge, inner, source) in enumerate(((2, 3, 0), (1, 0, width - 1))):
        clon, clat, below = [column(i, edge) for i in range(3)]
        ends = [jnp.zeros((4, width), F32), jnp.zeros((4, width), F32), jnp.ones((4, width), F32)]
        for *values, at in corners:
            for i, value in enumerate(values):
                ends[i] = jnp.where(wide == at, pltpu.roll(value, (at - source) % width, 1), ends[i])
        terms = (
            0.5 * m_n * (clat + pltpu.roll(clat, width - 1, 1)),
            0.5 * m_s * (clat + pltpu.roll(clat, 1, 1)),
            0.5 * (clon + column(0, inner)),
            up_level(below),
            below,
            *ends,
        )
        for i, term in enumerate(terms):
            terms_ref[pl.ds((side * EDGE_TERMS + i) * 4, 4), :] = term


def residual(lat_total, rows, cv_ref, state, res_ref, scratch):
    _, delta, w_west, w_east, clatb = state
    cosines = scratch[-1]
    cosines[...] = face_cos(lax.axis_index("lat") * rows, cosines.shape, 0, lat_total)
    lane = lax.broadcasted_iota(jnp.int32, (BLOCK, LANES), 1)
    tiles = [pl.ds(t * LANES, LANES) for t in range(2)]

    def second(r, carry):
        row = pl.multiple_of(r * BLOCK, BLOCK)
        at = pl.ds(row, BLOCK)
        m_s, m_n = metric(cosines[at, :]), metric(cosines[pl.ds(row + 1, BLOCK), :])
        for k in range(4):

            def get(buf, shift=0, level=k):
                return [buf[t, level, pl.ds(row + PAD + shift, BLOCK), :] for t in range(2)]

            d, d_s, d_n = get(delta), get(delta, -1), get(delta, 1)
            clat, clat_s, clat_n = get(clatb), get(clatb, -1), get(clatb, 1)
            d_w, d_e = roll_west(d, lane), roll_east(d, lane)
            for t in range(2):
                x_w, x_e = w_west[t, k, at, :] * d_w[t], w_east[t, k, at, :] * d_e[t]
                y = m_n * (clat[t] + clat_n[t]) * d_n[t] + m_s * (clat[t] + clat_s[t]) * d_s[t]
                out = 0.5 * ((x_w + x_e) + y)
                if k > 0:
                    out += cv_ref[k, at, tiles[t]] * get(delta, 0, k - 1)[t]
                if k < 3:
                    out += cv_ref[k + 1, at, tiles[t]] * get(delta, 0, k + 1)[t]
                res_ref[t, k, at, :] = out
        return carry

    lax.fori_loop(0, rows // BLOCK, second, 0)


def interior_call(lat_total, shape, kernel, inputs, kept, after, results):
    lev, rows, width = shape
    tiles = width // LANES
    vmem = pl.BlockSpec(memory_space=pltpu.VMEM)
    shapes = {
        "plane": (tiles, lev, rows, LANES),
        "padded": (tiles, lev, rows + 2 * PAD, LANES),
        "message": (COL_FIELDS * lev, 256),
        "terms": (2 * EDGE_TERMS * lev, 256),
    }
    operands = (*inputs, *kept, *after)
    return pl.pallas_call(
        lambda *refs: kernel(lat_total, rows, *refs),
        in_specs=[vmem] * len(operands),
        out_specs=[vmem] * len(results),
        out_shape=[jax.ShapeDtypeStruct(shapes[name], F32) for name in results],
        scratch_shapes=[
            pltpu.VMEM((256, LANES), F32),
            pltpu.VMEM((LANES, 256), F32),
            pltpu.VMEM((rows + 8, LANES), F32),
        ],
        input_output_aliases={len(inputs) + i: i for i in range(len(kept))},
        compiler_params=pltpu.CompilerParams(vmem_limit_bytes=VMEM_LIMIT),
        cost_estimate=pl.CostEstimate(flops=20_000_000, bytes_accessed=16_000_000, transcendentals=0),
        name=kernel.__name__,
    )(*operands)


def final_kernel(rows, *refs):
    new_in, res_in, terms, own_w, own_e, halo_w, halo_e = refs[:7]
    new_hbm, res_hbm, new_buf, res_buf, stack, colv, sems = refs[7:]
    width = 2 * LANES
    wide = lax.broadcasted_iota(jnp.int32, (4, width), 1)
    low, high, inside = wide == 0, wide == rows - 1, wide < rows
    own, halo = (own_w, own_e), (halo_w, halo_e)

    def ends(x):
        south, north = pltpu.roll(x, width - rows, 1), pltpu.roll(x, width - 2, 1)
        return jnp.where(low, south, jnp.where(high, north, 0.0))

    for side, (edge, inner, sign) in enumerate(((2, 3, 1.0), (1, 0, -1.0))):
        o_p, o_we, o_clon, o_total, o_number = [own[side][pl.ds(4 * i, 4), :] for i in range(5)]
        h_p, h_we, h_clon, h_total, h_number = [halo[side][pl.ds(4 * i, 4), :] for i in range(5)]
        a_n, a_s, w_in, above, below, c_w, c_number, c_total = [
            terms[pl.ds((side * EDGE_TERMS + i) * 4, 4), :] for i in range(EDGE_TERMS)
        ]
        w = 0.5 * (o_clon + h_clon)
        h = w * (o_p - h_p) - sign * (0.5 * (o_we + h_we))
        d = jnp.where(inside, (o_number - h) / (o_total + w), 0.0)
        beyond = jnp.where(inside, w * ((h_number + h) / (h_total + w)), 0.0)
        corner = c_w * ((c_number - ends(h)) / (c_total + ends(w)))
        at_edge = a_n * pltpu.roll(d, width - 1, 1) + a_s * pltpu.roll(d, 1, 1)
        at_edge += above * up_level(d) + below * down_level(d) + (beyond + corner)
        for first, x in ((edge, at_edge), (inner, w_in * d), (16 + edge, d)):
            for t in range(2):
                stack[t, pl.ds(first, 4, stride=4), :] = x[:, t * LANES : (t + 1) * LANES]
    for t in range(2):
        colv[pl.ds(t * LANES, LANES), :] = stack[t].T

    per = rows // CHUNKS
    lane = lax.broadcasted_iota(jnp.int32, (per, LANES), 1)
    edges = (lane < 2, lane >= LANES - 2)
    edge = (lane == 0, lane == LANES - 1)

    def sends(chunk):
        return [
            pltpu.make_async_copy(
                buf.at[:, pl.ds(chunk * per, per), :],
                out.at[:, pl.ds(chunk * per, per), :],
                sems.at[chunk, i],
            )
            for i, (buf, out) in enumerate(((new_buf, new_hbm), (res_buf, res_hbm)))
        ]

    for chunk in range(CHUNKS):
        at = pl.ds(chunk * per, per)
        packed = colv[at, :]
        for k in range(4):
            to_res = pltpu.roll(packed, (-4 * k - 2) % LANES, 1)
            to_new = pltpu.roll(packed, (-4 * (4 + k) - 2) % LANES, 1)
            for t in range(2):
                tile = pl.ds(t * LANES, LANES)
                res_buf[k, at, tile] = res_in[t, k, at, :] + jnp.where(edges[t], to_res, 0.0)
                new_buf[k, at, tile] = new_in[t, k, at, :] + jnp.where(edge[t], to_new, 0.0)
        for copy in sends(chunk):
            copy.start()
    for chunk in range(CHUNKS):
        for copy in sends(chunk):
            copy.wait()


def final_call(shape, planes, messages):
    lev, rows, width = shape
    hbm, vmem = pl.BlockSpec(memory_space=pl.ANY), pl.BlockSpec(memory_space=pltpu.VMEM)
    out = jax.ShapeDtypeStruct(shape, F32)
    return pl.pallas_call(
        lambda *refs: final_kernel(rows, *refs),
        in_specs=[vmem] * 7,
        out_specs=[hbm, hbm],
        out_shape=[out, out],
        scratch_shapes=[pltpu.VMEM(shape, F32)] * 2
        + [
            pltpu.VMEM((2, LANES, LANES), F32),
            pltpu.VMEM((256, LANES), F32),
            pltpu.SemaphoreType.DMA((CHUNKS, 2)),
        ],
        compiler_params=pltpu.CompilerParams(vmem_limit_bytes=VMEM_LIMIT),
        name="edges_and_store",
    )(*planes, *messages)


def per_device(pressure, wind_east, wind_north, forcing, coef_lon, coef_lat, coef_vert, diag_coef):
    fields = (pressure, wind_east, wind_north, forcing, coef_lon, coef_lat, coef_vert, diag_coef)
    rows = pressure.shape[1]
    lat_total = rows * lax.axis_size("lat")
    rows_near, rows_far, eastward, westward = exchange_pairs(
        lax.axis_size("lon"), lax.axis_size("lat")
    )
    near, far = rows_call(lat_total, fields)
    far_in = lax.ppermute(far, AXES, rows_far)
    near_in = lax.ppermute(near, AXES, rows_near)
    cols, p_planes, wn_planes, clat_planes = edge_call(lat_total, fields)
    row_messages = (far, near, far_in, near_in)
    shape = pressure.shape
    planes = (p_planes, wn_planes, clat_planes)
    kinds = ("plane", "padded", "plane", "plane", "padded")
    state = interior_call(
        lat_total, shape, interior_ahead, (*fields, *planes), (), (), kinds[:-1]
    )
    west, east, sent = columns_call(lat_total, rows, cols, *row_messages, state[0])
    from_west = lax.ppermute(sent, AXES, eastward)
    *state, west, terms, residual_part = interior_call(
        lat_total,
        shape,
        interior_between,
        (*fields, *row_messages, *planes[:2]),
        (*state, clat_planes, west),
        (),
        (*kinds, "message", "terms", "plane"),
    )
    from_east = lax.ppermute(west, AXES, westward)
    new_pressure, *_, terms, residual_part = interior_call(
        lat_total,
        shape,
        interior,
        (*fields, *row_messages, *planes[:2]),
        (*state, terms, residual_part),
        (west,),
        (*kinds, "terms", "plane"),
    )
    col_messages = (west, east, from_west, from_east)
    return final_call(shape, (new_pressure, residual_part, terms), col_messages)


def solution(mesh):
    spec = P(None, "lat", "lon")
    return jax.shard_map(
        per_device, mesh=mesh, in_specs=(spec,) * 8, out_specs=(spec, spec), check_vma=False
    )
```

```python
import math

import jax
import jax.numpy as jnp
from jax import lax
from jax.experimental import pallas as pl
from jax.experimental.pallas import tpu as pltpu
from jax.sharding import PartitionSpec as P

F32 = jnp.float32
AXES = ("lon", "lat")
LANES = 128
ROW_FIELDS = 6
COL_FIELDS = 5


def exchange_pairs(lon_count, lat_count):
    def flat(lon, lat):
        return (lon % lon_count) * lat_count + lat

    rows_near, rows_far, eastward, westward = [], [], [], []
    for lon in range(lon_count):
        for lat in range(lat_count):
            me = flat(lon, lat)
            rows_near.append((me, flat(lon, lat ^ 1)))
            if lat in (0, lat_count - 1):
                rows_far.append((me, flat(lon + lon_count // 2, lat)))
            else:
                rows_far.append((me, flat(lon, lat + 1 if lat % 2 else lat - 1)))
            eastward.append((me, flat(lon + 1, lat)))
            westward.append((me, flat(lon - 1, lat)))
    return rows_near, rows_far, eastward, westward


def face_cos(first, shape, axis, lat_total):
    position = (first + lax.broadcasted_iota(jnp.int32, shape, axis)).astype(F32)
    angle = position * (math.pi / lat_total) - math.pi / 2
    square = angle * angle
    cosine = jnp.full(shape, 1.0 / math.factorial(16), F32)
    for power in range(14, -1, -2):
        cosine = (-1.0) ** (power // 2) / math.factorial(power) + square * cosine
    return cosine


def metric(cosine):
    return 0.5 * (1.0 + jnp.abs(cosine))


def up_level(x):
    return jnp.concatenate((x[1:], jnp.zeros_like(x[:1])), 0)


def down_level(x):
    return jnp.concatenate((jnp.zeros_like(x[:1]), x[:-1]), 0)


def one_cos(row, lat_total):
    return face_cos(row, (1, 2 * LANES), 0, lat_total)


SMALL_VMEM = 4 * 2**20


def rows_kernel(lat_total, rows, *refs):
    low, high, (near_ref, far_ref) = refs[:8], refs[8:16], refs[16:]
    lat = lax.axis_index("lat")
    width = near_ref.shape[-1]
    lane = lax.broadcasted_iota(jnp.int32, (4, width), 1)

    def message(fields, edge, inner, face, sign):
        p, we, wn, forcing, clon, clat, cvert, diag = [f[:, edge, :] for f in fields]
        p_in, wn_in, clat_in = [fields[i][:, inner, :] for i in (0, 2, 5)]
        cosine = one_cos(face, lat_total)
        east = lane < width - 1
        w_east = jnp.where(east, 0.5 * (clon + pltpu.roll(clon, width - 1, 1)), 0.0)
        h_east = jnp.where(
            east,
            w_east * (pltpu.roll(p, width - 1, 1) - p) - 0.5 * (we + pltpu.roll(we, width - 1, 1)),
            0.0,
        )
        w_in = metric(cosine) * (0.5 * (clat + clat_in))
        h_in = w_in * (p_in - p) - sign * (0.5 * cosine * (wn + wn_in))
        w_up = up_level(cvert)
        h_up = w_up * (up_level(p) - p)
        below = cvert * (p - down_level(p))
        west = lane > 0
        clon_w, p_w, we_w = [pltpu.roll(x, 1, 1) for x in (clon, p, we)]
        w_west = jnp.where(west, 0.5 * (clon + clon_w), 0.0)
        h_west = jnp.where(west, w_west * (p - p_w) - 0.5 * (we_w + we), 0.0)
        total = diag + w_east + w_west + w_in + cvert + w_up
        number = forcing - diag * p + h_east - h_west + h_in + h_up - below
        ends = jnp.where(lane == 1, pltpu.roll(we, 1, 1), clon)
        ends = jnp.where(lane == width - 2, pltpu.roll(we, width - 1, 1), ends)
        return jnp.concatenate((p, wn, clat, total, number, ends), 0)

    start = lat * rows
    south = message(low, 0, 1, start + 1, 1.0)
    north = message(high, 7, 6, start + rows - 1, -1.0)
    even = lat % 2 == 0

    @pl.when(even)
    def _():
        near_ref[...] = north
        far_ref[...] = south

    @pl.when(jnp.logical_not(even))
    def _():
        near_ref[...] = south
        far_ref[...] = north


def rows_call(lat_total, fields):
    lev, rows, width = fields[0].shape
    low = pl.BlockSpec((lev, 8, width), lambda i: (0, 0, 0))
    high = pl.BlockSpec((lev, 8, width), lambda i: (0, rows // 8 - 1, 0))
    shape = jax.ShapeDtypeStruct((ROW_FIELDS * lev, width), F32)
    pinned = [pltpu.with_memory_space_constraint(f, pltpu.HBM) for f in fields]
    out = pl.BlockSpec(memory_space=pltpu.VMEM)
    return pl.pallas_call(
        lambda *refs: rows_kernel(lat_total, rows, *refs),
        grid=(1,),
        in_specs=[low] * 8 + [high] * 8,
        out_specs=[out, out],
        out_shape=[shape, shape],
        compiler_params=pltpu.CompilerParams(vmem_limit_bytes=SMALL_VMEM),
        name="row_messages",
    )(*pinned, *pinned)


CUTS = (0, 24, 96, 240)
PAD = 8
BLOCK = 48
VMEM_LIMIT = 24 * 2**20


def window_mask(lane, index):
    return lane // 4 == index


def window_row(index, offset):
    return 4 * index + offset


def merged(ref, level, row, count, lane):
    at = pl.ds(row, count)
    return jnp.where(lane < LANES // 2, ref[level, at, 0:LANES], ref[level, at, LANES : 2 * LANES])


def window_move(x, index):
    return pltpu.roll(x, (4 * index + 2) % LANES, 1)


def edge_kernel(lat_total, rows, *refs):
    p_ref, we_ref, wn_ref, f_ref, clon_ref, clat_ref, cv_ref, diag_ref = refs[:8]
    cols_ref, *planes = refs[8:12]
    pm, wnm, clatm, pack, packed, cosines, sems = refs[12:]
    moves = [
        pltpu.make_async_copy(
            ref.at[:, :, pl.ds(t * LANES, LANES)],
            plane.at[t, :, pl.ds(PAD, rows), :],
            sems.at[i, t],
        )
        for i, (ref, plane) in enumerate(zip((p_ref, wn_ref, clat_ref), planes))
        for t in range(2)
    ]
    for move in moves:
        move.start()
    start = lax.axis_index("lat") * rows
    cosines[...] = face_cos(start, cosines.shape, 0, lat_total)
    shape = (BLOCK, LANES)
    lane = lax.broadcasted_iota(jnp.int32, shape, 1)

    def gather(r, carry):
        row = pl.multiple_of(r * BLOCK, BLOCK)
        for ref, buf in ((p_ref, pm), (wn_ref, wnm), (clat_ref, clatm)):
            for k in range(4):
                buf[k, pl.ds(row + PAD, BLOCK), :] = merged(ref, k, row, BLOCK, lane)
        return carry

    lax.fori_loop(0, rows // BLOCK, gather, 0)
    for buf, sign in ((pm, 1.0), (wnm, -1.0), (clatm, -1.0)):
        for k in range(4):
            for inside, outside in ((PAD, PAD - 1), (PAD + rows - 1, PAD + rows)):
                buf[k, outside : outside + 1, :] = sign * buf[k, inside : inside + 1, :]
    pack[pl.ds(rows, 256 - rows), :] = jnp.zeros((256 - rows, LANES), F32)

    def step(r, carry):
        row = pl.multiple_of(r * BLOCK, BLOCK)
        c_s, c_n = cosines[pl.ds(row, BLOCK), :], cosines[pl.ds(row + 1, BLOCK), :]
        m_s, m_n = metric(c_s), metric(c_n)
        acc = [jnp.zeros(shape, F32) for _ in range(4)]
        for k in range(4):

            def get(buf, shift=0, level=k):
                return buf[level, pl.ds(row + PAD + shift, BLOCK), :]

            def raw(ref, level=k):
                return merged(ref, level, row, BLOCK, lane)

            p, clat, wn = get(pm), get(clatm), get(wnm)
            below, diag = raw(cv_ref) if k == 0 else above, raw(diag_ref)
            w_n, w_s = m_n * (clat + get(clatm, 1)), m_s * (clat + get(clatm, -1))
            flux = w_n * (get(pm, 1) - p) + w_s * (get(pm, -1) - p)
            flux += c_s * (wn + get(wnm, -1)) - c_n * (wn + get(wnm, 1))
            total = diag + below
            number = raw(f_ref) - diag * p - (below * p if k == 0 else lifted)
            if k < 3:
                above = raw(cv_ref, k + 1)
                lifted = above * (get(pm, 0, k + 1) - p)
                total += above
                number += lifted
            total += 0.5 * (w_n + w_s)
            number += 0.5 * flux
            for i, x in enumerate((p, raw(we_ref), raw(clon_ref), total, number)):
                index = i * 4 + k
                acc[k] = jnp.where(window_mask(lane, index), window_move(x, index), acc[k])
        pack[pl.ds(row, BLOCK), :] = (acc[0] + acc[1]) + (acc[2] + acc[3])
        return carry

    lax.fori_loop(0, rows // BLOCK, step, 0)
    packed[...] = pack[...].T

    def column(field, offset):
        return jnp.concatenate(
            [packed[pl.ds(window_row(field * 4 + k, offset), 1), :] for k in range(4)], 0
        )

    for side, (edge, inner, sign) in enumerate(((2, 3, 1.0), (1, 0, -1.0))):
        p, we, clon, total, number = [column(i, edge) for i in range(COL_FIELDS)]
        p_in, we_in, clon_in = [column(i, inner) for i in range(3)]
        w = 0.5 * (clon + clon_in)
        number = number + w * (p_in - p) - sign * (0.5 * (we + we_in))
        for i, x in enumerate((p, we, clon, total + w, number)):
            cols_ref[pl.ds((side * COL_FIELDS + i) * 4, 4), :] = x
    for move in moves:
        move.wait()


def edge_call(lat_total, fields):
    lev, rows, width = fields[0].shape
    cols = jax.ShapeDtypeStruct((2 * COL_FIELDS * lev, 256), F32)
    vmem = pl.BlockSpec(memory_space=pltpu.VMEM)
    return pl.pallas_call(
        lambda *refs: edge_kernel(lat_total, rows, *refs),
        in_specs=[vmem] * 8,
        out_specs=[vmem] * 4,
        out_shape=[cols] + [jax.ShapeDtypeStruct((2, lev, rows + 2 * PAD, LANES), F32)] * 3,
        scratch_shapes=[pltpu.VMEM((lev, rows + 2 * PAD, LANES), F32)] * 3
        + [
            pltpu.VMEM((256, LANES), F32),
            pltpu.VMEM((LANES, 256), F32),
            pltpu.VMEM((rows + 8, LANES), F32),
            pltpu.SemaphoreType.DMA((3, 2)),
        ],
        compiler_params=pltpu.CompilerParams(vmem_limit_bytes=VMEM_LIMIT),
        cost_estimate=pl.CostEstimate(flops=10_000_000, bytes_accessed=8_000_000, transcendentals=0),
        name="edge_columns",
    )(*fields)


def edge_rows(own, halo, cosine, low):
    w = metric(cosine) * (0.5 * (own[8:12] + halo[8:12]))
    g = 0.5 * cosine * (own[4:8] + halo[4:8])
    f = w * (own[0:4] - halo[0:4]) if low else w * (halo[0:4] - own[0:4])
    return w, f, g


def pick(even, near, far):
    return jnp.where(even, far, near), jnp.where(even, near, far)


def columns_kernel(lat_total, rows, cols, far, near, far_in, near_in, _, west_ref, east_ref, sent_ref):
    lat = lax.axis_index("lat")
    even = lat % 2 == 0
    own_s, own_n = pick(even, near[...], far[...])
    halo_s, halo_n = pick(even, near_in[...], far_in[...])
    w_s, f_s, g_s = edge_rows(own_s, halo_s, one_cos(lat * rows, lat_total), True)
    w_n, f_n, g_n = edge_rows(own_n, halo_n, one_cos((lat + 1) * rows, lat_total), False)
    h_s, h_n = f_s - g_s, f_n - g_n
    width = w_s.shape[-1]
    lane = lax.broadcasted_iota(jnp.int32, (4, width), 1)

    def side(at):
        source, inner = (0, 1) if at == 0 else (width - 1, width - 2)
        base = at * COL_FIELDS * 4
        p, we, clon, total, number = [cols[pl.ds(base + i * 4, 4), :] for i in range(COL_FIELDS)]

        def put(x, value, target, source=source):
            return jnp.where(lane == target, pltpu.roll(value, (target - source) % width, 1), x)

        no = jnp.zeros_like(p)
        total = total + put(put(no, w_s, 0), w_n, rows - 1)
        number = number + put(put(no, -h_s, 0), h_n, rows - 1)
        p = put(put(p, halo_s[0:4], rows), halo_n[0:4], rows + 1)
        clon = put(put(clon, halo_s[20:24], rows), halo_n[20:24], rows + 1)
        we = put(put(we, halo_s[20:24], rows, inner), halo_n[20:24], rows + 1, inner)
        return jnp.concatenate((p, we, clon, total, number), 0)

    west_ref[...] = side(0)
    east = side(1)
    east_ref[...] = east
    for i in range(COL_FIELDS):
        for t in range(2):
            half = east[4 * i : 4 * i + 4, t * LANES : (t + 1) * LANES]
            sent_ref[pl.ds(8 * i + 4 * t, 4), :] = half


def columns_call(lat_total, rows, cols, far, near, far_in, near_in, after):
    shape = jax.ShapeDtypeStruct((cols.shape[0] // 2, cols.shape[1]), F32)
    packed = jax.ShapeDtypeStruct((cols.shape[0], LANES), F32)
    vmem = pl.BlockSpec(memory_space=pltpu.VMEM)
    return pl.pallas_call(
        lambda *refs: columns_kernel(lat_total, rows, *refs),
        in_specs=[vmem] * 6,
        out_specs=[vmem] * 3,
        out_shape=[shape, shape, packed],
        compiler_params=pltpu.CompilerParams(vmem_limit_bytes=SMALL_VMEM),
        name="column_messages",
    )(cols, far, near, far_in, near_in, after)


def roll_west(tiles, lane):
    a, b = [pltpu.roll(x, 1, 1) for x in tiles]
    return a, jnp.where(lane == 0, a, b)


def roll_east(tiles, lane):
    a, b = [pltpu.roll(x, LANES - 1, 1) for x in tiles]
    return jnp.where(lane == LANES - 1, b, a), b


EDGE_TERMS = 8
STATE = 5
FIRST_AHEAD = 3
OTHERS_AHEAD = 2
BETWEEN = (5, 3, 3, 1, 2, 1)


def place():
    return lax.rem(lax.axis_index("lon"), lax.axis_size("lon") // 2)


def shares(blocks):
    here, lat, last = place(), lax.axis_index("lat"), lax.axis_size("lat") - 1
    slow = (lat == 0) | (lat == last) | (lat == last // 2)
    ahead = jnp.where(slow, OTHERS_AHEAD, 0)
    ahead = jnp.where((here == 0) & (lat != 1), FIRST_AHEAD, jnp.where(here == 0, OTHERS_AHEAD, ahead))
    between = ahead
    for at, count in enumerate(BETWEEN):
        between = jnp.where(here == at, jnp.maximum(count, ahead), between)
    between = jnp.where(here == 1, ahead + BETWEEN[1], between)
    return jnp.minimum(ahead, blocks), jnp.minimum(between, blocks)


def late_residual():
    return (place() > 0) | (lax.axis_index("lat") == 1)


def interior_ahead(lat_total, rows, *refs):
    ahead, _ = shares(rows // BLOCK)

    @pl.when(ahead > 0)
    def _():
        correction(lat_total, rows, refs[:8], refs[8:11], refs[11:15], refs[15:], 0, ahead)


def interior_between(lat_total, rows, *refs):
    fields, messages, planes, refs = refs[:8], refs[8:12], refs[12:14], refs[14 + STATE + 1 :]
    state, (_, terms_ref, res_ref), scratch = refs[:STATE], refs[STATE : STATE + 3], refs[STATE + 3 :]
    ahead, between = shares(rows // BLOCK)

    @pl.when(between > ahead)
    def _():
        here = (*planes, state[4])
        correction(lat_total, rows, fields, here, state[:4], scratch, ahead, between)

    @pl.when(place() == 0)
    def _():
        edges(lat_total, rows, fields[4:7], messages, state, terms_ref, scratch)

    @pl.when(jnp.logical_not(late_residual()))
    def _():
        residual(lat_total, rows, fields[6], state, res_ref, scratch)


def interior(lat_total, rows, *refs):
    fields, messages, planes, refs = refs[:8], refs[8:12], refs[12:14], refs[14 + STATE + 2 + 1 :]
    state, terms_ref, res_ref, scratch = refs[:STATE], refs[STATE], refs[STATE + 1], refs[STATE + 2 :]
    _, between = shares(rows // BLOCK)

    @pl.when(place() > 0)
    def _():
        here = (*planes, state[4])
        correction(lat_total, rows, fields, here, state[:4], scratch, between, rows // BLOCK)
        edges(lat_total, rows, fields[4:7], messages, state, terms_ref, scratch)

    @pl.when(late_residual())
    def _():
        residual(lat_total, rows, fields[6], state, res_ref, scratch)


def quotient(x, y):
    guess = pl.reciprocal(y, approx=True)
    guess = guess * (2.0 - y * guess)
    return x * guess


def correction(lat_total, rows, fields, planes, outs, scratch, begin, end):
    _, we_ref, _, f_ref, clon_ref, _, cv_ref, diag_ref = fields
    pb, wnb, clatb = planes
    new_ref, delta, w_west, w_east = outs
    cosines = scratch[-1]
    cosines[...] = face_cos(lax.axis_index("lat") * rows, cosines.shape, 0, lat_total)
    shape = (BLOCK, LANES)
    lane = lax.broadcasted_iota(jnp.int32, shape, 1)
    edge = (lane == 0, lane == LANES - 1)
    tiles = [pl.ds(t * LANES, LANES) for t in range(2)]

    def first(r, carry):
        row = pl.multiple_of(r * BLOCK, BLOCK)
        c_s, c_n = cosines[pl.ds(row, BLOCK), :], cosines[pl.ds(row + 1, BLOCK), :]
        m_s, m_n = metric(c_s), metric(c_n)
        lifted = None
        for k in range(4):

            def get(buf, shift=0, level=k):
                return [buf[t, level, pl.ds(row + PAD + shift, BLOCK), :] for t in range(2)]

            def raw(ref, level=k):
                return [ref[level, pl.ds(row, BLOCK), tile] for tile in tiles]

            p, we, clon, clat, wn = get(pb), raw(we_ref), raw(clon_ref), get(clatb), get(wnb)
            p_e, we_e, clon_e = [roll_east(x, lane) for x in (p, we, clon)]
            p_w, we_w, clon_w = [roll_west(x, lane) for x in (p, we, clon)]
            wn_s, wn_n, clat_s, clat_n = get(wnb, -1), get(wnb, 1), get(clatb, -1), get(clatb, 1)
            p_s, p_n = get(pb, -1), get(pb, 1)
            forcing, diag = raw(f_ref), raw(diag_ref)
            below = raw(cv_ref) if k == 0 else above
            if k < 3:
                above, p_a = raw(cv_ref, k + 1), get(pb, 0, k + 1)
            fallen, lifted = lifted, []
            for t in range(2):
                w_e, w_w = clon[t] + clon_e[t], clon[t] + clon_w[t]
                w_n, w_s = m_n * (clat[t] + clat_n[t]), m_s * (clat[t] + clat_s[t])
                flux = w_e * (p_e[t] - p[t]) + w_w * (p_w[t] - p[t]) - (we_e[t] - we_w[t])
                flux += w_n * (p_n[t] - p[t]) + w_s * (p_s[t] - p[t])
                flux += c_s * (wn[t] + wn_s[t]) - c_n * (wn[t] + wn_n[t])
                weight = (w_e + w_w) + (w_n + w_s)
                total = diag[t] + below[t]
                number = forcing[t] - diag[t] * p[t] - (below[t] * p[t] if k == 0 else fallen[t])
                if k < 3:
                    lifted.append(above[t] * (p_a[t] - p[t]))
                    total += above[t]
                    number += lifted[t]
                d = quotient(number + 0.5 * flux, total + 0.5 * weight)
                d = jnp.where(edge[t], 0.0, d)
                at = pl.ds(row, BLOCK)
                delta[t, k, pl.ds(row + PAD, BLOCK), :] = d
                new_ref[t, k, at, :] = p[t] + d
                w_west[t, k, at, :] = jnp.where(edge[0], 0.0, w_w) if t == 0 else w_w
                w_east[t, k, at, :] = jnp.where(edge[1], 0.0, w_e) if t == 1 else w_e
        return carry

    lax.fori_loop(begin, end, first, 0)


def edges(lat_total, rows, coefs, messages, state, terms_ref, scratch):
    clon_ref, clat_ref, cv_ref = coefs
    far, near, far_in, near_in = [m[...] for m in messages]
    new_ref, delta, _, _, clatb = state
    pack, packed, _ = scratch
    lat = lax.axis_index("lat")
    width = 2 * LANES
    wide = lax.broadcasted_iota(jnp.int32, (4, width), 1)
    inside = (wide > 0) & (wide < width - 1)
    even = lat % 2 == 0
    own_s, own_n = pick(even, near, far)
    halo_s, halo_n = pick(even, near_in, far_in)
    w_s, f_s, g_s = edge_rows(own_s, halo_s, one_cos(lat * rows, lat_total), True)
    w_n, f_n, g_n = edge_rows(own_n, halo_n, one_cos((lat + 1) * rows, lat_total), False)
    into_s = f_s - jnp.where(lat == 0, -g_s, g_s)
    into_n = jnp.where(lat == lax.axis_size("lat") - 1, -g_n, g_n) - f_n

    def put_rows(buf, at, value):
        for t in range(2):
            for k in range(4):
                buf[t, k, at : at + 1, :] = value[k : k + 1, t * LANES : (t + 1) * LANES]

    corners = []
    for own, halo, w, into, flux, at, beyond in (
        (own_s, halo_s, w_s, into_s, g_s - f_s, 0, -1),
        (own_n, halo_n, w_n, into_n, f_n - g_n, rows - 1, rows),
    ):
        halo_number, halo_total = halo[16:20] + into, halo[12:16] + w
        d_own = jnp.where(inside, (own[16:20] + flux) / (own[12:16] + w), 0.0)
        put_rows(new_ref, at, own[0:4] + d_own)
        put_rows(delta, PAD + at, d_own)
        put_rows(delta, PAD + beyond, jnp.where(inside, halo_number / halo_total, 0.0))
        put_rows(clatb, PAD + beyond, halo[8:12])
        corners.append((w, halo_number, halo_total, at))
    pack[pl.ds(rows, 256 - rows), :] = jnp.zeros((256 - rows, LANES), F32)
    shape = (BLOCK, LANES)
    lane = lax.broadcasted_iota(jnp.int32, shape, 1)
    tiles = [pl.ds(t * LANES, LANES) for t in range(2)]

    def gather(r, carry):
        row = pl.multiple_of(r * BLOCK, BLOCK)
        acc = [jnp.zeros(shape, F32) for _ in range(4)]
        for k in range(4):
            for i, ref in enumerate((clon_ref, clat_ref, cv_ref)):
                index = i * 4 + k
                both = merged(ref, k, row, BLOCK, lane)
                acc[k] = jnp.where(window_mask(lane, index), window_move(both, index), acc[k])
        pack[pl.ds(row, BLOCK), :] = (acc[0] + acc[1]) + (acc[2] + acc[3])
        return carry

    lax.fori_loop(0, rows // BLOCK, gather, 0)
    packed[...] = pack[...].T
    m_s = metric(face_cos(lat * rows, (4, width), 1, lat_total))
    m_n = metric(face_cos(lat * rows + 1, (4, width), 1, lat_total))

    def column(field, offset):
        return jnp.concatenate(
            [packed[pl.ds(window_row(field * 4 + k, offset), 1), :] for k in range(4)], 0
        )

    for side, (edge, inner, source) in enumerate(((2, 3, 0), (1, 0, width - 1))):
        clon, clat, below = [column(i, edge) for i in range(3)]
        ends = [jnp.zeros((4, width), F32), jnp.zeros((4, width), F32), jnp.ones((4, width), F32)]
        for *values, at in corners:
            for i, value in enumerate(values):
                ends[i] = jnp.where(wide == at, pltpu.roll(value, (at - source) % width, 1), ends[i])
        terms = (
            0.5 * m_n * (clat + pltpu.roll(clat, width - 1, 1)),
            0.5 * m_s * (clat + pltpu.roll(clat, 1, 1)),
            0.5 * (clon + column(0, inner)),
            up_level(below),
            below,
            *ends,
        )
        for i, term in enumerate(terms):
            terms_ref[pl.ds((side * EDGE_TERMS + i) * 4, 4), :] = term


def residual(lat_total, rows, cv_ref, state, res_ref, scratch):
    _, delta, w_west, w_east, clatb = state
    cosines = scratch[-1]
    cosines[...] = face_cos(lax.axis_index("lat") * rows, cosines.shape, 0, lat_total)
    lane = lax.broadcasted_iota(jnp.int32, (BLOCK, LANES), 1)
    tiles = [pl.ds(t * LANES, LANES) for t in range(2)]

    def second(r, carry):
        row = pl.multiple_of(r * BLOCK, BLOCK)
        at = pl.ds(row, BLOCK)
        m_s, m_n = metric(cosines[at, :]), metric(cosines[pl.ds(row + 1, BLOCK), :])
        for k in range(4):

            def get(buf, shift=0, level=k):
                return [buf[t, level, pl.ds(row + PAD + shift, BLOCK), :] for t in range(2)]

            d, d_s, d_n = get(delta), get(delta, -1), get(delta, 1)
            clat, clat_s, clat_n = get(clatb), get(clatb, -1), get(clatb, 1)
            d_w, d_e = roll_west(d, lane), roll_east(d, lane)
            for t in range(2):
                x_w, x_e = w_west[t, k, at, :] * d_w[t], w_east[t, k, at, :] * d_e[t]
                y = m_n * (clat[t] + clat_n[t]) * d_n[t] + m_s * (clat[t] + clat_s[t]) * d_s[t]
                out = 0.5 * ((x_w + x_e) + y)
                if k > 0:
                    out += cv_ref[k, at, tiles[t]] * get(delta, 0, k - 1)[t]
                if k < 3:
                    out += cv_ref[k + 1, at, tiles[t]] * get(delta, 0, k + 1)[t]
                res_ref[t, k, at, :] = out
        return carry

    lax.fori_loop(0, rows // BLOCK, second, 0)


def interior_call(lat_total, shape, kernel, inputs, kept, after, results):
    lev, rows, width = shape
    tiles = width // LANES
    vmem = pl.BlockSpec(memory_space=pltpu.VMEM)
    shapes = {
        "plane": (tiles, lev, rows, LANES),
        "padded": (tiles, lev, rows + 2 * PAD, LANES),
        "message": (COL_FIELDS * lev, 256),
        "terms": (2 * EDGE_TERMS * lev, 256),
    }
    operands = (*inputs, *kept, *after)
    return pl.pallas_call(
        lambda *refs: kernel(lat_total, rows, *refs),
        in_specs=[vmem] * len(operands),
        out_specs=[vmem] * len(results),
        out_shape=[jax.ShapeDtypeStruct(shapes[name], F32) for name in results],
        scratch_shapes=[
            pltpu.VMEM((256, LANES), F32),
            pltpu.VMEM((LANES, 256), F32),
            pltpu.VMEM((rows + 8, LANES), F32),
        ],
        input_output_aliases={len(inputs) + i: i for i in range(len(kept))},
        compiler_params=pltpu.CompilerParams(vmem_limit_bytes=VMEM_LIMIT),
        cost_estimate=pl.CostEstimate(flops=20_000_000, bytes_accessed=16_000_000, transcendentals=0),
        name=kernel.__name__,
    )(*operands)


def final_kernel(rows, *refs):
    new_in, res_in, terms, own_w, own_e, halo_w, halo_e = refs[:7]
    new_hbm, res_hbm, new_buf, res_buf, stack, colv, sems = refs[7:]
    width = 2 * LANES
    wide = lax.broadcasted_iota(jnp.int32, (4, width), 1)
    low, high, inside = wide == 0, wide == rows - 1, wide < rows
    own = (own_w, own_e)

    def ends(x):
        south, north = pltpu.roll(x, width - rows, 1), pltpu.roll(x, width - 2, 1)
        return jnp.where(low, south, jnp.where(high, north, 0.0))

    for side, (edge, inner, sign) in enumerate(((2, 3, 1.0), (1, 0, -1.0))):
        o_p, o_we, o_clon, o_total, o_number = [own[side][pl.ds(4 * i, 4), :] for i in range(5)]
        if side == 0:
            h = [[halo_w[pl.ds(8 * i + 4 * t, 4), :] for t in range(2)] for i in range(5)]
            h_p, h_we, h_clon, h_total, h_number = [jnp.concatenate(pair, 1) for pair in h]
        else:
            h_p, h_we, h_clon, h_total, h_number = [halo_e[pl.ds(4 * i, 4), :] for i in range(5)]
        a_n, a_s, w_in, above, below, c_w, c_number, c_total = [
            terms[pl.ds((side * EDGE_TERMS + i) * 4, 4), :] for i in range(EDGE_TERMS)
        ]
        w = 0.5 * (o_clon + h_clon)
        h = w * (o_p - h_p) - sign * (0.5 * (o_we + h_we))
        d = jnp.where(inside, (o_number - h) / (o_total + w), 0.0)
        beyond = jnp.where(inside, w * ((h_number + h) / (h_total + w)), 0.0)
        corner = c_w * ((c_number - ends(h)) / (c_total + ends(w)))
        at_edge = a_n * pltpu.roll(d, width - 1, 1) + a_s * pltpu.roll(d, 1, 1)
        at_edge += above * up_level(d) + below * down_level(d) + (beyond + corner)
        for first, x in ((edge, at_edge), (inner, w_in * d), (16 + edge, d)):
            for t in range(2):
                stack[t, pl.ds(first, 4, stride=4), :] = x[:, t * LANES : (t + 1) * LANES]
    for t in range(2):
        colv[pl.ds(t * LANES, LANES), :] = stack[t].T

    cuts = [rows * cut // CUTS[-1] for cut in CUTS]
    chunks = [(begin, end - begin) for begin, end in zip(cuts, cuts[1:])]

    def sends(chunk):
        return [
            pltpu.make_async_copy(
                buf.at[:, pl.ds(*chunks[chunk]), :], out.at[:, pl.ds(*chunks[chunk]), :], sems.at[chunk, i]
            )
            for i, (buf, out) in enumerate(((new_buf, new_hbm), (res_buf, res_hbm)))
        ]

    for chunk, (begin, count) in enumerate(chunks):
        at = pl.ds(begin, count)
        lane = lax.broadcasted_iota(jnp.int32, (count, LANES), 1)
        edges = (lane < 2, lane >= LANES - 2)
        edge = (lane == 0, lane == LANES - 1)
        packed = colv[at, :]
        for k in range(4):
            to_res = pltpu.roll(packed, (-4 * k - 2) % LANES, 1)
            to_new = pltpu.roll(packed, (-4 * (4 + k) - 2) % LANES, 1)
            for t in range(2):
                tile = pl.ds(t * LANES, LANES)
                res_buf[k, at, tile] = res_in[t, k, at, :] + jnp.where(edges[t], to_res, 0.0)
                new_buf[k, at, tile] = new_in[t, k, at, :] + jnp.where(edge[t], to_new, 0.0)
        for copy in sends(chunk):
            copy.start()
    for chunk in range(len(chunks)):
        for copy in sends(chunk):
            copy.wait()


def final_call(shape, planes, messages):
    lev, rows, width = shape
    hbm, vmem = pl.BlockSpec(memory_space=pl.ANY), pl.BlockSpec(memory_space=pltpu.VMEM)
    out = jax.ShapeDtypeStruct(shape, F32)
    return pl.pallas_call(
        lambda *refs: final_kernel(rows, *refs),
        in_specs=[vmem] * 7,
        out_specs=[hbm, hbm],
        out_shape=[out, out],
        scratch_shapes=[pltpu.VMEM(shape, F32)] * 2
        + [
            pltpu.VMEM((2, LANES, LANES), F32),
            pltpu.VMEM((256, LANES), F32),
            pltpu.SemaphoreType.DMA((len(CUTS) - 1, 2)),
        ],
        compiler_params=pltpu.CompilerParams(vmem_limit_bytes=VMEM_LIMIT),
        name="edges_and_store",
    )(*planes, *messages)


def per_device(pressure, wind_east, wind_north, forcing, coef_lon, coef_lat, coef_vert, diag_coef):
    fields = (pressure, wind_east, wind_north, forcing, coef_lon, coef_lat, coef_vert, diag_coef)
    rows = pressure.shape[1]
    lat_total = rows * lax.axis_size("lat")
    rows_near, rows_far, eastward, westward = exchange_pairs(
        lax.axis_size("lon"), lax.axis_size("lat")
    )
    near, far = rows_call(lat_total, fields)
    far_in = lax.ppermute(far, AXES, rows_far)
    near_in = lax.ppermute(near, AXES, rows_near)
    cols, p_planes, wn_planes, clat_planes = edge_call(lat_total, fields)
    row_messages = (far, near, far_in, near_in)
    shape = pressure.shape
    planes = (p_planes, wn_planes, clat_planes)
    kinds = ("plane", "padded", "plane", "plane", "padded")
    state = interior_call(
        lat_total, shape, interior_ahead, (*fields, *planes), (), (), kinds[:-1]
    )
    west, east, sent = columns_call(lat_total, rows, cols, *row_messages, state[0])
    from_west = lax.ppermute(sent, AXES, eastward)
    *state, west, terms, residual_part = interior_call(
        lat_total,
        shape,
        interior_between,
        (*fields, *row_messages, *planes[:2]),
        (*state, clat_planes, west),
        (),
        (*kinds, "message", "terms", "plane"),
    )
    from_east = lax.ppermute(west, AXES, westward)
    new_pressure, *_, terms, residual_part = interior_call(
        lat_total,
        shape,
        interior,
        (*fields, *row_messages, *planes[:2]),
        (*state, terms, residual_part),
        (west,),
        (*kinds, "terms", "plane"),
    )
    col_messages = (west, east, from_west, from_east)
    return final_call(shape, (new_pressure, residual_part, terms), col_messages)


def solution(mesh):
    spec = P(None, "lat", "lon")
    return jax.shard_map(
        per_device, mesh=mesh, in_specs=(spec,) * 8, out_specs=(spec, spec), check_vma=False
    )
```

```python
import math

import jax
import jax.numpy as jnp
from jax import lax
from jax.experimental import pallas as pl
from jax.experimental.pallas import tpu as pltpu
from jax.sharding import PartitionSpec as P

F32 = jnp.float32
AXES = ("lon", "lat")
LANES = 128
ROW_FIELDS = 6
COL_FIELDS = 5


def exchange_pairs(lon_count, lat_count):
    def flat(lon, lat):
        return (lon % lon_count) * lat_count + lat

    rows_near, rows_far, eastward, westward = [], [], [], []
    for lon in range(lon_count):
        for lat in range(lat_count):
            me = flat(lon, lat)
            rows_near.append((me, flat(lon, lat ^ 1)))
            if lat in (0, lat_count - 1):
                rows_far.append((me, flat(lon + lon_count // 2, lat)))
            else:
                rows_far.append((me, flat(lon, lat + 1 if lat % 2 else lat - 1)))
            eastward.append((me, flat(lon + 1, lat)))
            westward.append((me, flat(lon - 1, lat)))
    return rows_near, rows_far, eastward, westward


def face_cos(first, shape, axis, lat_total):
    position = (first + lax.broadcasted_iota(jnp.int32, shape, axis)).astype(F32)
    angle = position * (math.pi / lat_total) - math.pi / 2
    square = angle * angle
    cosine = jnp.full(shape, 1.0 / math.factorial(16), F32)
    for power in range(14, -1, -2):
        cosine = (-1.0) ** (power // 2) / math.factorial(power) + square * cosine
    return cosine


def metric(cosine):
    return 0.5 * (1.0 + jnp.abs(cosine))


def up_level(x):
    return jnp.concatenate((x[1:], jnp.zeros_like(x[:1])), 0)


def down_level(x):
    return jnp.concatenate((jnp.zeros_like(x[:1]), x[:-1]), 0)


def one_cos(row, lat_total):
    return face_cos(row, (1, 2 * LANES), 0, lat_total)


SMALL_VMEM = 4 * 2**20


def rows_kernel(lat_total, rows, *refs):
    low, high, (near_ref, far_ref) = refs[:8], refs[8:16], refs[16:]
    lat = lax.axis_index("lat")
    width = near_ref.shape[-1]
    lane = lax.broadcasted_iota(jnp.int32, (4, width), 1)

    def message(fields, edge, inner, face, sign):
        p, we, wn, forcing, clon, clat, cvert, diag = [f[:, edge, :] for f in fields]
        p_in, wn_in, clat_in = [fields[i][:, inner, :] for i in (0, 2, 5)]
        cosine = one_cos(face, lat_total)
        east = lane < width - 1
        w_east = jnp.where(east, 0.5 * (clon + pltpu.roll(clon, width - 1, 1)), 0.0)
        h_east = jnp.where(
            east,
            w_east * (pltpu.roll(p, width - 1, 1) - p) - 0.5 * (we + pltpu.roll(we, width - 1, 1)),
            0.0,
        )
        w_in = metric(cosine) * (0.5 * (clat + clat_in))
        h_in = w_in * (p_in - p) - sign * (0.5 * cosine * (wn + wn_in))
        w_up = up_level(cvert)
        h_up = w_up * (up_level(p) - p)
        below = cvert * (p - down_level(p))
        west = lane > 0
        clon_w, p_w, we_w = [pltpu.roll(x, 1, 1) for x in (clon, p, we)]
        w_west = jnp.where(west, 0.5 * (clon + clon_w), 0.0)
        h_west = jnp.where(west, w_west * (p - p_w) - 0.5 * (we_w + we), 0.0)
        total = diag + w_east + w_west + w_in + cvert + w_up
        number = forcing - diag * p + h_east - h_west + h_in + h_up - below
        ends = jnp.where(lane == 1, pltpu.roll(we, 1, 1), clon)
        ends = jnp.where(lane == width - 2, pltpu.roll(we, width - 1, 1), ends)
        return jnp.concatenate((p, wn, clat, total, number, ends), 0)

    start = lat * rows
    south = message(low, 0, 1, start + 1, 1.0)
    north = message(high, 7, 6, start + rows - 1, -1.0)
    even = lat % 2 == 0

    @pl.when(even)
    def _():
        near_ref[...] = north
        far_ref[...] = south

    @pl.when(jnp.logical_not(even))
    def _():
        near_ref[...] = south
        far_ref[...] = north


def rows_call(lat_total, fields):
    lev, rows, width = fields[0].shape
    low = pl.BlockSpec((lev, 8, width), lambda i: (0, 0, 0))
    high = pl.BlockSpec((lev, 8, width), lambda i: (0, rows // 8 - 1, 0))
    shape = jax.ShapeDtypeStruct((ROW_FIELDS * lev, width), F32)
    pinned = [pltpu.with_memory_space_constraint(f, pltpu.HBM) for f in fields]
    out = pl.BlockSpec(memory_space=pltpu.VMEM)
    return pl.pallas_call(
        lambda *refs: rows_kernel(lat_total, rows, *refs),
        grid=(1,),
        in_specs=[low] * 8 + [high] * 8,
        out_specs=[out, out],
        out_shape=[shape, shape],
        compiler_params=pltpu.CompilerParams(vmem_limit_bytes=SMALL_VMEM),
        name="row_messages",
    )(*pinned, *pinned)


CUTS = (0, 24, 96, 240)
PAD = 8
BLOCK = 48
VMEM_LIMIT = 24 * 2**20


def window_mask(lane, index):
    return lane // 4 == index


def window_row(index, offset):
    return 4 * index + offset


def merged(ref, level, row, count, lane):
    at = pl.ds(row, count)
    return jnp.where(lane < LANES // 2, ref[level, at, 0:LANES], ref[level, at, LANES : 2 * LANES])


def window_move(x, index):
    return pltpu.roll(x, (4 * index + 2) % LANES, 1)


def edge_kernel(lat_total, rows, *refs):
    p_ref, we_ref, wn_ref, f_ref, clon_ref, clat_ref, cv_ref, diag_ref = refs[:8]
    cols_ref, *planes = refs[8:12]
    pm, wnm, clatm, pack, packed, cosines, sems = refs[12:]
    moves = [
        pltpu.make_async_copy(
            ref.at[:, :, pl.ds(t * LANES, LANES)],
            plane.at[t, :, pl.ds(PAD, rows), :],
            sems.at[i, t],
        )
        for i, (ref, plane) in enumerate(zip((p_ref, wn_ref, clat_ref), planes))
        for t in range(2)
    ]
    for move in moves:
        move.start()
    start = lax.axis_index("lat") * rows
    cosines[...] = face_cos(start, cosines.shape, 0, lat_total)
    shape = (BLOCK, LANES)
    lane = lax.broadcasted_iota(jnp.int32, shape, 1)

    def gather(r, carry):
        row = pl.multiple_of(r * BLOCK, BLOCK)
        for ref, buf in ((p_ref, pm), (wn_ref, wnm), (clat_ref, clatm)):
            for k in range(4):
                buf[k, pl.ds(row + PAD, BLOCK), :] = merged(ref, k, row, BLOCK, lane)
        return carry

    lax.fori_loop(0, rows // BLOCK, gather, 0)
    for buf, sign in ((pm, 1.0), (wnm, -1.0), (clatm, -1.0)):
        for k in range(4):
            for inside, outside in ((PAD, PAD - 1), (PAD + rows - 1, PAD + rows)):
                buf[k, outside : outside + 1, :] = sign * buf[k, inside : inside + 1, :]
    pack[pl.ds(rows, 256 - rows), :] = jnp.zeros((256 - rows, LANES), F32)

    def step(r, carry):
        row = pl.multiple_of(r * BLOCK, BLOCK)
        c_s, c_n = cosines[pl.ds(row, BLOCK), :], cosines[pl.ds(row + 1, BLOCK), :]
        m_s, m_n = metric(c_s), metric(c_n)
        acc = [jnp.zeros(shape, F32) for _ in range(4)]
        for k in range(4):

            def get(buf, shift=0, level=k):
                return buf[level, pl.ds(row + PAD + shift, BLOCK), :]

            def raw(ref, level=k):
                return merged(ref, level, row, BLOCK, lane)

            p, clat, wn = get(pm), get(clatm), get(wnm)
            below, diag = raw(cv_ref) if k == 0 else above, raw(diag_ref)
            w_n, w_s = m_n * (clat + get(clatm, 1)), m_s * (clat + get(clatm, -1))
            flux = w_n * (get(pm, 1) - p) + w_s * (get(pm, -1) - p)
            flux += c_s * (wn + get(wnm, -1)) - c_n * (wn + get(wnm, 1))
            total = diag + below
            number = raw(f_ref) - diag * p - (below * p if k == 0 else lifted)
            if k < 3:
                above = raw(cv_ref, k + 1)
                lifted = above * (get(pm, 0, k + 1) - p)
                total += above
                number += lifted
            total += 0.5 * (w_n + w_s)
            number += 0.5 * flux
            for i, x in enumerate((p, raw(we_ref), raw(clon_ref), total, number)):
                index = i * 4 + k
                acc[k] = jnp.where(window_mask(lane, index), window_move(x, index), acc[k])
        pack[pl.ds(row, BLOCK), :] = (acc[0] + acc[1]) + (acc[2] + acc[3])
        return carry

    lax.fori_loop(0, rows // BLOCK, step, 0)
    packed[...] = pack[...].T

    def column(field, offset):
        return jnp.concatenate(
            [packed[pl.ds(window_row(field * 4 + k, offset), 1), :] for k in range(4)], 0
        )

    for side, (edge, inner, sign) in enumerate(((2, 3, 1.0), (1, 0, -1.0))):
        p, we, clon, total, number = [column(i, edge) for i in range(COL_FIELDS)]
        p_in, we_in, clon_in = [column(i, inner) for i in range(3)]
        w = 0.5 * (clon + clon_in)
        number = number + w * (p_in - p) - sign * (0.5 * (we + we_in))
        for i, x in enumerate((p, we, clon, total + w, number)):
            cols_ref[pl.ds((side * COL_FIELDS + i) * 4, 4), :] = x
    for move in moves:
        move.wait()


def edge_call(lat_total, fields):
    lev, rows, width = fields[0].shape
    cols = jax.ShapeDtypeStruct((2 * COL_FIELDS * lev, 256), F32)
    vmem = pl.BlockSpec(memory_space=pltpu.VMEM)
    return pl.pallas_call(
        lambda *refs: edge_kernel(lat_total, rows, *refs),
        in_specs=[vmem] * 8,
        out_specs=[vmem] * 4,
        out_shape=[cols] + [jax.ShapeDtypeStruct((2, lev, rows + 2 * PAD, LANES), F32)] * 3,
        scratch_shapes=[pltpu.VMEM((lev, rows + 2 * PAD, LANES), F32)] * 3
        + [
            pltpu.VMEM((256, LANES), F32),
            pltpu.VMEM((LANES, 256), F32),
            pltpu.VMEM((rows + 8, LANES), F32),
            pltpu.SemaphoreType.DMA((3, 2)),
        ],
        compiler_params=pltpu.CompilerParams(vmem_limit_bytes=VMEM_LIMIT),
        cost_estimate=pl.CostEstimate(flops=10_000_000, bytes_accessed=8_000_000, transcendentals=0),
        name="edge_columns",
    )(*fields)


def edge_rows(own, halo, cosine, low):
    w = metric(cosine) * (0.5 * (own[8:12] + halo[8:12]))
    g = 0.5 * cosine * (own[4:8] + halo[4:8])
    f = w * (own[0:4] - halo[0:4]) if low else w * (halo[0:4] - own[0:4])
    return w, f, g


def pick(even, near, far):
    return jnp.where(even, far, near), jnp.where(even, near, far)


def columns_kernel(lat_total, rows, cols, far, near, far_in, near_in, _, west_ref, east_ref, sent_ref):
    lat = lax.axis_index("lat")
    even = lat % 2 == 0
    own_s, own_n = pick(even, near[...], far[...])
    halo_s, halo_n = pick(even, near_in[...], far_in[...])
    w_s, f_s, g_s = edge_rows(own_s, halo_s, one_cos(lat * rows, lat_total), True)
    w_n, f_n, g_n = edge_rows(own_n, halo_n, one_cos((lat + 1) * rows, lat_total), False)
    h_s, h_n = f_s - g_s, f_n - g_n
    width = w_s.shape[-1]
    lane = lax.broadcasted_iota(jnp.int32, (4, width), 1)

    def side(at):
        source, inner = (0, 1) if at == 0 else (width - 1, width - 2)
        base = at * COL_FIELDS * 4
        p, we, clon, total, number = [cols[pl.ds(base + i * 4, 4), :] for i in range(COL_FIELDS)]

        def put(x, value, target, source=source):
            return jnp.where(lane == target, pltpu.roll(value, (target - source) % width, 1), x)

        no = jnp.zeros_like(p)
        total = total + put(put(no, w_s, 0), w_n, rows - 1)
        number = number + put(put(no, -h_s, 0), h_n, rows - 1)
        p = put(put(p, halo_s[0:4], rows), halo_n[0:4], rows + 1)
        clon = put(put(clon, halo_s[20:24], rows), halo_n[20:24], rows + 1)
        we = put(put(we, halo_s[20:24], rows, inner), halo_n[20:24], rows + 1, inner)
        return jnp.concatenate((p, we, clon, total, number), 0)

    west_ref[...] = side(0)
    east = side(1)
    east_ref[...] = east
    for i in range(COL_FIELDS):
        for t in range(2):
            half = east[4 * i : 4 * i + 4, t * LANES : (t + 1) * LANES]
            sent_ref[pl.ds(8 * i + 4 * t, 4), :] = half


def columns_call(lat_total, rows, cols, far, near, far_in, near_in, after):
    shape = jax.ShapeDtypeStruct((cols.shape[0] // 2, cols.shape[1]), F32)
    packed = jax.ShapeDtypeStruct((cols.shape[0], LANES), F32)
    vmem = pl.BlockSpec(memory_space=pltpu.VMEM)
    return pl.pallas_call(
        lambda *refs: columns_kernel(lat_total, rows, *refs),
        in_specs=[vmem] * 6,
        out_specs=[vmem] * 3,
        out_shape=[shape, shape, packed],
        compiler_params=pltpu.CompilerParams(vmem_limit_bytes=SMALL_VMEM),
        name="column_messages",
    )(cols, far, near, far_in, near_in, after)


def roll_west(tiles, lane):
    a, b = [pltpu.roll(x, 1, 1) for x in tiles]
    return a, jnp.where(lane == 0, a, b)


def roll_east(tiles, lane):
    a, b = [pltpu.roll(x, LANES - 1, 1) for x in tiles]
    return jnp.where(lane == LANES - 1, b, a), b


EDGE_TERMS = 8
STATE = 5
FIRST_AHEAD = 3
OTHERS_AHEAD = 2
BETWEEN = (5, 4, 3, 1, 2, 1)


def place():
    return lax.rem(lax.axis_index("lon"), lax.axis_size("lon") // 2)


def shares(blocks):
    here, lat, last = place(), lax.axis_index("lat"), lax.axis_size("lat") - 1
    slow = (lat == 0) | (lat == last) | (lat == last // 2)
    ahead = jnp.where(slow, OTHERS_AHEAD, 0)
    ahead = jnp.where((here == 0) & (lat != 1), FIRST_AHEAD, jnp.where(here == 0, OTHERS_AHEAD, ahead))
    between = ahead
    for at, count in enumerate(BETWEEN):
        between = jnp.where(here == at, jnp.maximum(count, ahead), between)
    between = jnp.where(here == 1, ahead + BETWEEN[1], between)
    return jnp.minimum(ahead, blocks), jnp.minimum(between, blocks)


def late_residual():
    return (place() > 0) | (lax.axis_index("lat") == 1)


def interior_ahead(lat_total, rows, *refs):
    ahead, _ = shares(rows // BLOCK)

    @pl.when(ahead > 0)
    def _():
        correction(lat_total, rows, refs[:8], refs[8:11], refs[11:15], refs[15:], 0, ahead)


def interior_between(lat_total, rows, *refs):
    fields, messages, planes, refs = refs[:8], refs[8:12], refs[12:14], refs[14 + STATE + 1 :]
    state, (_, terms_ref, res_ref), scratch = refs[:STATE], refs[STATE : STATE + 3], refs[STATE + 3 :]
    ahead, between = shares(rows // BLOCK)

    @pl.when(between > ahead)
    def _():
        here = (*planes, state[4])
        correction(lat_total, rows, fields, here, state[:4], scratch, ahead, between)

    @pl.when(place() == 0)
    def _():
        edges(lat_total, rows, fields[4:7], messages, state, terms_ref, scratch)

    @pl.when(jnp.logical_not(late_residual()))
    def _():
        residual(lat_total, rows, fields[6], state, res_ref, scratch)


def interior(lat_total, rows, *refs):
    fields, messages, planes, refs = refs[:8], refs[8:12], refs[12:14], refs[14 + STATE + 2 + 1 :]
    state, terms_ref, res_ref, scratch = refs[:STATE], refs[STATE], refs[STATE + 1], refs[STATE + 2 :]
    _, between = shares(rows // BLOCK)

    @pl.when(place() > 0)
    def _():
        here = (*planes, state[4])
        correction(lat_total, rows, fields, here, state[:4], scratch, between, rows // BLOCK)
        edges(lat_total, rows, fields[4:7], messages, state, terms_ref, scratch)

    @pl.when(late_residual())
    def _():
        residual(lat_total, rows, fields[6], state, res_ref, scratch)


def quotient(x, y):
    guess = pl.reciprocal(y, approx=True)
    guess = guess * (2.0 - y * guess)
    return x * guess


def correction(lat_total, rows, fields, planes, outs, scratch, begin, end):
    _, we_ref, _, f_ref, clon_ref, _, cv_ref, diag_ref = fields
    pb, wnb, clatb = planes
    new_ref, delta, w_west, w_east = outs
    cosines = scratch[-1]
    cosines[...] = face_cos(lax.axis_index("lat") * rows, cosines.shape, 0, lat_total)
    shape = (BLOCK, LANES)
    lane = lax.broadcasted_iota(jnp.int32, shape, 1)
    edge = (lane == 0, lane == LANES - 1)
    tiles = [pl.ds(t * LANES, LANES) for t in range(2)]

    def first(r, carry):
        row = pl.multiple_of(r * BLOCK, BLOCK)
        c_s, c_n = cosines[pl.ds(row, BLOCK), :], cosines[pl.ds(row + 1, BLOCK), :]
        m_s, m_n = metric(c_s), metric(c_n)
        lifted = None
        for k in range(4):

            def get(buf, shift=0, level=k):
                return [buf[t, level, pl.ds(row + PAD + shift, BLOCK), :] for t in range(2)]

            def raw(ref, level=k):
                return [ref[level, pl.ds(row, BLOCK), tile] for tile in tiles]

            p, we, clon, clat, wn = get(pb), raw(we_ref), raw(clon_ref), get(clatb), get(wnb)
            p_e, we_e, clon_e = [roll_east(x, lane) for x in (p, we, clon)]
            p_w, we_w, clon_w = [roll_west(x, lane) for x in (p, we, clon)]
            wn_s, wn_n, clat_s, clat_n = get(wnb, -1), get(wnb, 1), get(clatb, -1), get(clatb, 1)
            p_s, p_n = get(pb, -1), get(pb, 1)
            forcing, diag = raw(f_ref), raw(diag_ref)
            below = raw(cv_ref) if k == 0 else above
            if k < 3:
                above, p_a = raw(cv_ref, k + 1), get(pb, 0, k + 1)
            fallen, lifted = lifted, []
            for t in range(2):
                w_e, w_w = clon[t] + clon_e[t], clon[t] + clon_w[t]
                w_n, w_s = m_n * (clat[t] + clat_n[t]), m_s * (clat[t] + clat_s[t])
                flux = w_e * (p_e[t] - p[t]) + w_w * (p_w[t] - p[t]) - (we_e[t] - we_w[t])
                flux += w_n * (p_n[t] - p[t]) + w_s * (p_s[t] - p[t])
                flux += c_s * (wn[t] + wn_s[t]) - c_n * (wn[t] + wn_n[t])
                weight = (w_e + w_w) + (w_n + w_s)
                total = diag[t] + below[t]
                number = forcing[t] - diag[t] * p[t] - (below[t] * p[t] if k == 0 else fallen[t])
                if k < 3:
                    lifted.append(above[t] * (p_a[t] - p[t]))
                    total += above[t]
                    number += lifted[t]
                d = quotient(number + 0.5 * flux, total + 0.5 * weight)
                d = jnp.where(edge[t], 0.0, d)
                at = pl.ds(row, BLOCK)
                delta[t, k, pl.ds(row + PAD, BLOCK), :] = d
                new_ref[t, k, at, :] = p[t] + d
                w_west[t, k, at, :] = jnp.where(edge[0], 0.0, w_w) if t == 0 else w_w
                w_east[t, k, at, :] = jnp.where(edge[1], 0.0, w_e) if t == 1 else w_e
        return carry

    lax.fori_loop(begin, end, first, 0)


def edges(lat_total, rows, coefs, messages, state, terms_ref, scratch):
    clon_ref, clat_ref, cv_ref = coefs
    far, near, far_in, near_in = [m[...] for m in messages]
    new_ref, delta, _, _, clatb = state
    pack, packed, _ = scratch
    lat = lax.axis_index("lat")
    width = 2 * LANES
    wide = lax.broadcasted_iota(jnp.int32, (4, width), 1)
    inside = (wide > 0) & (wide < width - 1)
    even = lat % 2 == 0
    own_s, own_n = pick(even, near, far)
    halo_s, halo_n = pick(even, near_in, far_in)
    w_s, f_s, g_s = edge_rows(own_s, halo_s, one_cos(lat * rows, lat_total), True)
    w_n, f_n, g_n = edge_rows(own_n, halo_n, one_cos((lat + 1) * rows, lat_total), False)
    into_s = f_s - jnp.where(lat == 0, -g_s, g_s)
    into_n = jnp.where(lat == lax.axis_size("lat") - 1, -g_n, g_n) - f_n

    def put_rows(buf, at, value):
        for t in range(2):
            for k in range(4):
                buf[t, k, at : at + 1, :] = value[k : k + 1, t * LANES : (t + 1) * LANES]

    corners = []
    for own, halo, w, into, flux, at, beyond in (
        (own_s, halo_s, w_s, into_s, g_s - f_s, 0, -1),
        (own_n, halo_n, w_n, into_n, f_n - g_n, rows - 1, rows),
    ):
        halo_number, halo_total = halo[16:20] + into, halo[12:16] + w
        d_own = jnp.where(inside, (own[16:20] + flux) / (own[12:16] + w), 0.0)
        put_rows(new_ref, at, own[0:4] + d_own)
        put_rows(delta, PAD + at, d_own)
        put_rows(delta, PAD + beyond, jnp.where(inside, halo_number / halo_total, 0.0))
        put_rows(clatb, PAD + beyond, halo[8:12])
        corners.append((w, halo_number, halo_total, at))
    pack[pl.ds(rows, 256 - rows), :] = jnp.zeros((256 - rows, LANES), F32)
    shape = (BLOCK, LANES)
    lane = lax.broadcasted_iota(jnp.int32, shape, 1)
    tiles = [pl.ds(t * LANES, LANES) for t in range(2)]

    def gather(r, carry):
        row = pl.multiple_of(r * BLOCK, BLOCK)
        acc = [jnp.zeros(shape, F32) for _ in range(4)]
        for k in range(4):
            for i, ref in enumerate((clon_ref, clat_ref, cv_ref)):
                index = i * 4 + k
                both = merged(ref, k, row, BLOCK, lane)
                acc[k] = jnp.where(window_mask(lane, index), window_move(both, index), acc[k])
        pack[pl.ds(row, BLOCK), :] = (acc[0] + acc[1]) + (acc[2] + acc[3])
        return carry

    lax.fori_loop(0, rows // BLOCK, gather, 0)
    packed[...] = pack[...].T
    m_s = metric(face_cos(lat * rows, (4, width), 1, lat_total))
    m_n = metric(face_cos(lat * rows + 1, (4, width), 1, lat_total))

    def column(field, offset):
        return jnp.concatenate(
            [packed[pl.ds(window_row(field * 4 + k, offset), 1), :] for k in range(4)], 0
        )

    for side, (edge, inner, source) in enumerate(((2, 3, 0), (1, 0, width - 1))):
        clon, clat, below = [column(i, edge) for i in range(3)]
        ends = [jnp.zeros((4, width), F32), jnp.zeros((4, width), F32), jnp.ones((4, width), F32)]
        for *values, at in corners:
            for i, value in enumerate(values):
                ends[i] = jnp.where(wide == at, pltpu.roll(value, (at - source) % width, 1), ends[i])
        terms = (
            0.5 * m_n * (clat + pltpu.roll(clat, width - 1, 1)),
            0.5 * m_s * (clat + pltpu.roll(clat, 1, 1)),
            0.5 * (clon + column(0, inner)),
            up_level(below),
            below,
            *ends,
        )
        for i, term in enumerate(terms):
            terms_ref[pl.ds((side * EDGE_TERMS + i) * 4, 4), :] = term


def residual(lat_total, rows, cv_ref, state, res_ref, scratch):
    _, delta, w_west, w_east, clatb = state
    cosines = scratch[-1]
    cosines[...] = face_cos(lax.axis_index("lat") * rows, cosines.shape, 0, lat_total)
    lane = lax.broadcasted_iota(jnp.int32, (BLOCK, LANES), 1)
    tiles = [pl.ds(t * LANES, LANES) for t in range(2)]

    def second(r, carry):
        row = pl.multiple_of(r * BLOCK, BLOCK)
        at = pl.ds(row, BLOCK)
        m_s, m_n = metric(cosines[at, :]), metric(cosines[pl.ds(row + 1, BLOCK), :])
        for k in range(4):

            def get(buf, shift=0, level=k):
                return [buf[t, level, pl.ds(row + PAD + shift, BLOCK), :] for t in range(2)]

            d, d_s, d_n = get(delta), get(delta, -1), get(delta, 1)
            clat, clat_s, clat_n = get(clatb), get(clatb, -1), get(clatb, 1)
            d_w, d_e = roll_west(d, lane), roll_east(d, lane)
            for t in range(2):
                x_w, x_e = w_west[t, k, at, :] * d_w[t], w_east[t, k, at, :] * d_e[t]
                y = m_n * (clat[t] + clat_n[t]) * d_n[t] + m_s * (clat[t] + clat_s[t]) * d_s[t]
                out = 0.5 * ((x_w + x_e) + y)
                if k > 0:
                    out += cv_ref[k, at, tiles[t]] * get(delta, 0, k - 1)[t]
                if k < 3:
                    out += cv_ref[k + 1, at, tiles[t]] * get(delta, 0, k + 1)[t]
                res_ref[t, k, at, :] = out
        return carry

    lax.fori_loop(0, rows // BLOCK, second, 0)


def interior_call(lat_total, shape, kernel, inputs, kept, after, results):
    lev, rows, width = shape
    tiles = width // LANES
    vmem = pl.BlockSpec(memory_space=pltpu.VMEM)
    shapes = {
        "plane": (tiles, lev, rows, LANES),
        "padded": (tiles, lev, rows + 2 * PAD, LANES),
        "message": (COL_FIELDS * lev, 256),
        "terms": (2 * EDGE_TERMS * lev, 256),
    }
    operands = (*inputs, *kept, *after)
    return pl.pallas_call(
        lambda *refs: kernel(lat_total, rows, *refs),
        in_specs=[vmem] * len(operands),
        out_specs=[vmem] * len(results),
        out_shape=[jax.ShapeDtypeStruct(shapes[name], F32) for name in results],
        scratch_shapes=[
            pltpu.VMEM((256, LANES), F32),
            pltpu.VMEM((LANES, 256), F32),
            pltpu.VMEM((rows + 8, LANES), F32),
        ],
        input_output_aliases={len(inputs) + i: i for i in range(len(kept))},
        compiler_params=pltpu.CompilerParams(vmem_limit_bytes=VMEM_LIMIT),
        cost_estimate=pl.CostEstimate(flops=20_000_000, bytes_accessed=16_000_000, transcendentals=0),
        name=kernel.__name__,
    )(*operands)


def final_kernel(rows, *refs):
    new_in, res_in, terms, own_w, own_e, halo_w, halo_e = refs[:7]
    new_hbm, res_hbm, new_buf, res_buf, stack, colv, sems = refs[7:]
    width = 2 * LANES
    wide = lax.broadcasted_iota(jnp.int32, (4, width), 1)
    low, high, inside = wide == 0, wide == rows - 1, wide < rows
    own = (own_w, own_e)

    def ends(x):
        south, north = pltpu.roll(x, width - rows, 1), pltpu.roll(x, width - 2, 1)
        return jnp.where(low, south, jnp.where(high, north, 0.0))

    for side, (edge, inner, sign) in enumerate(((2, 3, 1.0), (1, 0, -1.0))):
        o_p, o_we, o_clon, o_total, o_number = [own[side][pl.ds(4 * i, 4), :] for i in range(5)]
        if side == 0:
            h = [[halo_w[pl.ds(8 * i + 4 * t, 4), :] for t in range(2)] for i in range(5)]
            h_p, h_we, h_clon, h_total, h_number = [jnp.concatenate(pair, 1) for pair in h]
        else:
            h_p, h_we, h_clon, h_total, h_number = [halo_e[pl.ds(4 * i, 4), :] for i in range(5)]
        a_n, a_s, w_in, above, below, c_w, c_number, c_total = [
            terms[pl.ds((side * EDGE_TERMS + i) * 4, 4), :] for i in range(EDGE_TERMS)
        ]
        w = 0.5 * (o_clon + h_clon)
        h = w * (o_p - h_p) - sign * (0.5 * (o_we + h_we))
        d = jnp.where(inside, (o_number - h) / (o_total + w), 0.0)
        beyond = jnp.where(inside, w * ((h_number + h) / (h_total + w)), 0.0)
        corner = c_w * ((c_number - ends(h)) / (c_total + ends(w)))
        at_edge = a_n * pltpu.roll(d, width - 1, 1) + a_s * pltpu.roll(d, 1, 1)
        at_edge += above * up_level(d) + below * down_level(d) + (beyond + corner)
        for first, x in ((edge, at_edge), (inner, w_in * d), (16 + edge, d)):
            for t in range(2):
                stack[t, pl.ds(first, 4, stride=4), :] = x[:, t * LANES : (t + 1) * LANES]
    for t in range(2):
        colv[pl.ds(t * LANES, LANES), :] = stack[t].T

    cuts = [rows * cut // CUTS[-1] for cut in CUTS]
    chunks = [(begin, end - begin) for begin, end in zip(cuts, cuts[1:])]

    def sends(chunk):
        return [
            pltpu.make_async_copy(
                buf.at[:, pl.ds(*chunks[chunk]), :], out.at[:, pl.ds(*chunks[chunk]), :], sems.at[chunk, i]
            )
            for i, (buf, out) in enumerate(((new_buf, new_hbm), (res_buf, res_hbm)))
        ]

    for chunk, (begin, count) in enumerate(chunks):
        at = pl.ds(begin, count)
        lane = lax.broadcasted_iota(jnp.int32, (count, LANES), 1)
        edges = (lane < 2, lane >= LANES - 2)
        edge = (lane == 0, lane == LANES - 1)
        packed = colv[at, :]
        for k in range(4):
            to_res = pltpu.roll(packed, (-4 * k - 2) % LANES, 1)
            to_new = pltpu.roll(packed, (-4 * (4 + k) - 2) % LANES, 1)
            for t in range(2):
                tile = pl.ds(t * LANES, LANES)
                res_buf[k, at, tile] = res_in[t, k, at, :] + jnp.where(edges[t], to_res, 0.0)
                new_buf[k, at, tile] = new_in[t, k, at, :] + jnp.where(edge[t], to_new, 0.0)
        for copy in sends(chunk):
            copy.start()
    for chunk in range(len(chunks)):
        for copy in sends(chunk):
            copy.wait()


def final_call(shape, planes, messages):
    lev, rows, width = shape
    hbm, vmem = pl.BlockSpec(memory_space=pl.ANY), pl.BlockSpec(memory_space=pltpu.VMEM)
    out = jax.ShapeDtypeStruct(shape, F32)
    return pl.pallas_call(
        lambda *refs: final_kernel(rows, *refs),
        in_specs=[vmem] * 7,
        out_specs=[hbm, hbm],
        out_shape=[out, out],
        scratch_shapes=[pltpu.VMEM(shape, F32)] * 2
        + [
            pltpu.VMEM((2, LANES, LANES), F32),
            pltpu.VMEM((256, LANES), F32),
            pltpu.SemaphoreType.DMA((len(CUTS) - 1, 2)),
        ],
        compiler_params=pltpu.CompilerParams(vmem_limit_bytes=VMEM_LIMIT),
        name="edges_and_store",
    )(*planes, *messages)


def per_device(pressure, wind_east, wind_north, forcing, coef_lon, coef_lat, coef_vert, diag_coef):
    fields = (pressure, wind_east, wind_north, forcing, coef_lon, coef_lat, coef_vert, diag_coef)
    rows = pressure.shape[1]
    lat_total = rows * lax.axis_size("lat")
    rows_near, rows_far, eastward, westward = exchange_pairs(
        lax.axis_size("lon"), lax.axis_size("lat")
    )
    near, far = rows_call(lat_total, fields)
    far_in = lax.ppermute(far, AXES, rows_far)
    near_in = lax.ppermute(near, AXES, rows_near)
    cols, p_planes, wn_planes, clat_planes = edge_call(lat_total, fields)
    row_messages = (far, near, far_in, near_in)
    shape = pressure.shape
    planes = (p_planes, wn_planes, clat_planes)
    kinds = ("plane", "padded", "plane", "plane", "padded")
    state = interior_call(
        lat_total, shape, interior_ahead, (*fields, *planes), (), (), kinds[:-1]
    )
    west, east, sent = columns_call(lat_total, rows, cols, *row_messages, state[0])
    from_west = lax.ppermute(sent, AXES, eastward)
    *state, west, terms, residual_part = interior_call(
        lat_total,
        shape,
        interior_between,
        (*fields, *row_messages, *planes[:2]),
        (*state, clat_planes, west),
        (),
        (*kinds, "message", "terms", "plane"),
    )
    from_east = lax.ppermute(west, AXES, westward)
    new_pressure, *_, terms, residual_part = interior_call(
        lat_total,
        shape,
        interior,
        (*fields, *row_messages, *planes[:2]),
        (*state, terms, residual_part),
        (west,),
        (*kinds, "terms", "plane"),
    )
    col_messages = (west, east, from_west, from_east)
    return final_call(shape, (new_pressure, residual_part, terms), col_messages)


def solution(mesh):
    spec = P(None, "lat", "lon")
    return jax.shard_map(
        per_device, mesh=mesh, in_specs=(spec,) * 8, out_specs=(spec, spec), check_vma=False
    )
```
